32 devices in a mesh: clip: 4 (over x, core), frame: 8 (over z, y).
Axes of the slice: x: 2, y: 2, z: 4, core: 2. Of those that a mesh axis runs over, the one named last changes fastest.
Arguments:
- stream: bfloat16 [64, 256, 768], P(('clip', 'frame')), may hold values from -24 to 24
- out_grad: bfloat16 [64, 256, 768], P(('clip', 'frame')), may hold values from -6 to 6
- token_mask: int32 [64, 256], P(('clip', 'frame')), may hold values from 0 to 1, as said below
- ln1_gain: float32 [768], replicated, may hold values from 0.25 to 1.75
- ln1_bias: float32 [768], replicated, may hold values from -3 to 3
- w_qkv: bfloat16 [768, 2304], replicated, may hold values from -0.3125 to 0.3125
- b_qv: float32 [1536], replicated, may hold values from -4 to 4
- w_out: bfloat16 [768, 768], replicated, may hold values from -0.4375 to 0.4375
- b_out: float32 [768], replicated, may hold values from -3 to 3
- ln2_gain: float32 [768], replicated, may hold values from 0.25 to 1.75
- ln2_bias: float32 [768], replicated, may hold values from -3 to 3
- w_up: bfloat16 [768, 3072], replicated, may hold values from -0.21875 to 0.21875
- b_up: float32 [3072], replicated, may hold values from -4 to 4
- w_down: bfloat16 [3072, 768], replicated, may hold values from -0.109375 to 0.109375
- b_down: float32 [768], replicated, may hold values from -3 to 3
Outputs:
- output: bfloat16 [64, 256, 768], P(('clip', 'frame'))
- input_grad: bfloat16 [64, 256, 768], P(('clip', 'frame'))
- grad_ln1_gain: float32 [768], P('frame')
- grad_ln1_bias: float32 [768], P('frame')
- grad_w_qkv: float32 [768, 2304], P('frame')
- grad_b_qv: float32 [1536], P('frame')
- grad_w_out: float32 [768, 768], P('frame')
- grad_b_out: float32 [768], P('frame')
- grad_ln2_gain: float32 [768], P('frame')
- grad_ln2_bias: float32 [768], P('frame')
- grad_w_up: float32 [768, 3072], P('frame')
- grad_b_up: float32 [3072], P('frame')
- grad_w_down: float32 [3072, 768], P('frame')
- grad_b_down: float32 [768], P('frame')
- statistics: float32 [5], replicated
The draws below stay inside these ranges and needn't reach their ends.
Inputs may be any that keep to these rules, and one draw needn't show every extreme that they name: `token_mask`: each clip draws its own chance of a masked token, from one half to one.
All inputs are finite; a program needn't handle non-finite values.
Results may differ from the reference program's by a relative error of at most 0.015.
Values may be sent and summed in bfloat16 or wider, within the bound.
A program may use at most 192 MiB of HBM per device.

```python
import math
import jax
import jax.numpy as jnp
from jax import lax

D = 768
HEADS = 12
HEAD_DIM = 64
FF = 3072
TUBES = 16
TUBE_POS = 16
FRAME_SPLIT = 8
CLIP_SPLIT = 1
FRAMES_DEV = 2
CLIPS_DEV = 1
ROWS_DEV = 2
GROUP_CLIPS = 1
CLIPS = 4
ROWS = 64
SPATIAL = 256
LENGTH = 256
N_CLIP = 4
N_FRAME = 8
DEVICES = 32


def clip_of_rows():
    rows_all = jnp.arange(ROWS, dtype=jnp.int32)
    device = rows_all // ROWS_DEV
    frame_place = device % N_FRAME
    clip_index = device // N_FRAME * GROUP_CLIPS + frame_place // FRAME_SPLIT * CLIPS_DEV + rows_all % CLIPS_DEV
    return (device, clip_index)


def draw_stream(key, part):
    key = jax.random.fold_in(key, 11)
    first, second = jax.random.split(key)
    device, clip_index = clip_of_rows()
    place = device.astype(jnp.float32) / max(DEVICES - 1, 1)
    share = 0.2 + 0.4 * clip_index.astype(jnp.float32) / max(CLIPS - 1, 1)
    noise = jnp.clip(jax.random.normal(first, (ROWS, SPATIAL, D), jnp.float32), -4.0, 4.0)
    common = jnp.clip(jax.random.normal(second, (CLIPS, D), jnp.float32), -4.0, 4.0)
    factor = 1.0 + 2.0 * place
    keep = jnp.sqrt(1.0 - share * share)
    values = keep[:, None, None] * noise + share[:, None, None] * common[clip_index][:, None, :]
    return (factor[:, None, None] * values).astype(jnp.bfloat16)


def draw_token_mask(key, part):
    key = jax.random.fold_in(key, 23)
    first, second = jax.random.split(key)
    device, clip_index = clip_of_rows()
    offset = jax.random.randint(first, (), 0, 9)
    level = 8 + (clip_index * 5 + offset) % 9
    ticket = jax.random.randint(second, (ROWS, SPATIAL), 0, 16)
    return (ticket < level[:, None]).astype(jnp.int32)


def levels(stream_key, dims, cuts, low, high):
    gain, own = 1.0, jax.random.fold_in(stream_key, 6)
    for position, shards_of in cuts:
        steps = jnp.exp(jax.random.uniform(jax.random.fold_in(own, position), (shards_of,), jnp.float32, low / len(cuts), high / len(cuts)))
        gain = gain * jnp.repeat(steps, dims[position] // shards_of).reshape([-1 if axis == position else 1 for axis in range(len(dims))])
    return gain


def scatter_about(rng, dims, width, reach, cuts=(), kind=jnp.bfloat16):
    values = width * jax.random.normal(rng, dims, jnp.float32)
    if cuts:
        values = values * levels(rng, dims, cuts, -0.22, 0.18)
    return jnp.clip(values, -reach, reach).astype(kind)


def setup_inputs(seed: int = 0) -> dict:
    key_of = jax.random.split(jax.random.key(seed), 16)
    stream = draw_stream(jax.random.fold_in(key_of[15], 71), 0)
    out_grad = scatter_about(key_of[1], (ROWS, SPATIAL, D), 1.0, 6.0, ((0, 32),))
    token_mask = draw_token_mask(jax.random.fold_in(key_of[15], 71), 0)
    ln1_gain = jnp.clip(1.0 + 0.15 * jax.random.normal(key_of[3], (D,), jnp.float32), 0.25, 1.75)
    ln1_bias = scatter_about(key_of[4], (D,), 0.3, 3.0, (), jnp.float32)
    w_qkv = scatter_about(key_of[5], (D, 3 * D), (D // 2) ** -0.5, 0.3125)
    b_qv = scatter_about(key_of[6], (2 * D,), 0.5, 4.0, (), jnp.float32)
    w_out = scatter_about(key_of[7], (D, D), (D // 4) ** -0.5, 0.4375)
    b_out = scatter_about(key_of[8], (D,), 0.3, 3.0, (), jnp.float32)
    ln2_gain = jnp.clip(1.0 + 0.15 * jax.random.normal(key_of[9], (D,), jnp.float32), 0.25, 1.75)
    ln2_bias = scatter_about(key_of[10], (D,), 0.3, 3.0, (), jnp.float32)
    w_up = scatter_about(key_of[11], (D, FF), D ** -0.5, 0.21875)
    b_up = scatter_about(key_of[12], (FF,), 0.5, 4.0, (), jnp.float32)
    w_down = scatter_about(key_of[13], (FF, D), FF ** -0.5, 0.109375)
    b_down = scatter_about(key_of[14], (D,), 0.3, 3.0, (), jnp.float32)
    return dict(stream=stream, out_grad=out_grad, token_mask=token_mask, ln1_gain=ln1_gain, ln1_bias=ln1_bias, w_qkv=w_qkv, b_qv=b_qv, w_out=w_out, b_out=b_out, ln2_gain=ln2_gain, ln2_bias=ln2_bias, w_up=w_up, b_up=b_up, w_down=w_down, b_down=b_down)


EPS = 1e-05
PRECISION_HIGH = lax.Precision.HIGHEST

@jax.custom_vjp
def low(v):
    return lax.optimization_barrier(v.astype(jnp.bfloat16)).astype(jnp.float32)

@jax.custom_vjp
def low_back(v):
    return v

def low_keep(v):
    return (low(v), None)

def low_pass(kept, grad):
    return (grad,)

def back_keep(v):
    return (v, None)

def back_low(kept, grad):
    return (low(grad),)
low.defvjp(low_keep, low_pass)
low_back.defvjp(back_keep, back_low)

def layer_norm(inputs, norm_gain, norm_shift):
    center = lax.optimization_barrier(jnp.mean(inputs, axis=-1, keepdims=True))
    shifted = inputs - center
    spread = lax.optimization_barrier(jnp.mean(shifted * shifted, axis=-1, keepdims=True))
    return shifted * lax.rsqrt(spread + EPS) * norm_gain + norm_shift

def to_seq(tensor):
    tensor = tensor.reshape(N_CLIP, CLIP_SPLIT, FRAME_SPLIT, FRAMES_DEV, CLIPS_DEV, TUBES, TUBE_POS, D)
    tensor = jnp.transpose(tensor, (0, 1, 4, 5, 2, 3, 6, 7))
    return tensor.reshape(CLIPS * TUBES, LENGTH, D)

def from_seq(tensor):
    tensor = tensor.reshape(N_CLIP, CLIP_SPLIT, CLIPS_DEV, TUBES, FRAME_SPLIT, FRAMES_DEV, TUBE_POS, D)
    tensor = jnp.transpose(tensor, (0, 1, 4, 5, 2, 3, 6, 7))
    return tensor.reshape(ROWS, SPATIAL, D)

def reference(stream, out_grad, token_mask, ln1_gain, ln1_bias, w_qkv, b_qv, w_out, b_out, ln2_gain, ln2_bias, w_up, b_up, w_down, b_down):
    params = tuple((item.astype(jnp.float32) for item in (ln1_gain, ln1_bias, w_qkv, b_qv, w_out, b_out, ln2_gain, ln2_bias, w_up, b_up, w_down, b_down)))
    inputs = to_seq(stream.astype(jnp.float32))
    cotangent = to_seq(out_grad.astype(jnp.float32) * token_mask[:, :, None].astype(jnp.float32))
    seq_total = CLIPS * TUBES
    per_block = math.gcd(seq_total, max(1, 4096 // LENGTH))
    blocks = seq_total // per_block
    scale = 1.0 / math.sqrt(HEAD_DIM)

    def forward(tokens, gain_one, bias_one, query_key_value_projection, bias_qv, output_projection, output_proj_bias, gain_two, bias_two, up_projection, up_proj_bias, down_projection, down_proj_bias):
        zeros = jnp.zeros((D,), jnp.float32)
        third_bias_term = jnp.concatenate([bias_qv[:D], zeros, bias_qv[D:]])

        def one_block(piece):
            first_normed_input = low(layer_norm(piece, gain_one, bias_one))
            query_key_value = jnp.einsum('wgf,fz->wgz', first_normed_input, query_key_value_projection, precision=PRECISION_HIGH) + third_bias_term
            query_key_value = low(low_back(query_key_value))
            queries = query_key_value[:, :, :D].reshape(per_block, LENGTH, HEADS, HEAD_DIM)
            key_part = query_key_value[:, :, D:2 * D].reshape(per_block, LENGTH, HEADS, HEAD_DIM)
            values = query_key_value[:, :, 2 * D:].reshape(per_block, LENGTH, HEADS, HEAD_DIM)
            scores = jnp.einsum('slhe,smhe->shlm', queries, key_part, precision=PRECISION_HIGH) * scale
            scores = low_back(scores)
            largest = lax.optimization_barrier(jnp.max(scores, axis=-1, keepdims=True))
            logsum = largest + jnp.log(lax.optimization_barrier(jnp.sum(jnp.exp(scores - largest), axis=-1, keepdims=True)))
            attend = low(jnp.exp(scores - logsum))
            mixed_heads = jnp.einsum('shlm,smhe->slhe', attend, values, precision=PRECISION_HIGH).reshape(per_block, LENGTH, D)
            mixed_heads = low(low_back(mixed_heads))
            attention_branch = low_back(jnp.einsum('wgf,fz->wgz', mixed_heads, output_projection, precision=PRECISION_HIGH) + output_proj_bias)
            middle = piece + attention_branch
            second_normed_input = low(layer_norm(middle, gain_two, bias_two))
            hidden_state = low_back(jnp.einsum('tnq,qa->tna', second_normed_input, up_projection, precision=PRECISION_HIGH) + up_proj_bias)
            activated_hidden = low(jax.nn.gelu(hidden_state, approximate=False))
            feedforward_branch = jnp.einsum('qwi,ik->qwk', activated_hidden, down_projection, precision=PRECISION_HIGH) + down_proj_bias
            result = middle + feedforward_branch
            sums = jnp.stack([jnp.sum(piece * piece), jnp.sum(middle * middle), jnp.sum(result * result), jnp.sum(attention_branch * attention_branch), jnp.sum(feedforward_branch * feedforward_branch)])
            return (result, sums)
        results, sums = lax.map(jax.checkpoint(one_block), tokens.reshape(blocks, per_block, LENGTH, D))
        return (results.reshape(seq_total, LENGTH, D), lax.optimization_barrier(jnp.sum(sums, axis=0)))
    result, pull, sums = jax.vjp(forward, inputs, *params, has_aux=True)
    grads = pull(cotangent)
    output = from_seq(result).astype(jnp.bfloat16)
    input_grad = from_seq(grads[0]).astype(jnp.bfloat16)
    statistics = jnp.sqrt(sums / (ROWS * SPATIAL * D))
    return (output, input_grad, grads[1], grads[2], grads[3], grads[4], grads[5], grads[6], grads[7], grads[8], grads[9], grads[10], grads[11], grads[12], statistics)
```

```python
import functools
import math

import jax
import jax.numpy as jnp
from jax import lax
from jax.experimental import pallas as pl
from jax.experimental.pallas import tpu as pltpu
from jax.sharding import PartitionSpec as P

HEADS = 12
FRAMES = 16
TUBES = 16
EPS = 1e-05

F32 = jnp.float32
BF16 = jnp.bfloat16
MESH = pl.DeviceIdType.MESH
ROW_BLOCK = 64


def dot_nn(lhs, rhs):
    return lax.dot_general(lhs, rhs, (((1,), (0,)), ((), ())), preferred_element_type=F32)


def dot_nt(lhs, rhs):
    return lax.dot_general(lhs, rhs, (((1,), (1,)), ((), ())), preferred_element_type=F32)


def dot_tn(lhs, rhs):
    return lax.dot_general(lhs, rhs, (((0,), (0,)), ((), ())), preferred_element_type=F32)


def unit_norm(rows):
    shifted = rows - jnp.mean(rows, axis=-1, keepdims=True)
    inverse = lax.rsqrt(jnp.mean(shifted * shifted, axis=-1, keepdims=True) + EPS)
    return shifted * inverse, inverse


def norm_pull(scaled, unit, inverse):
    first = jnp.mean(scaled, axis=-1, keepdims=True)
    second = jnp.mean(scaled * unit, axis=-1, keepdims=True)
    return inverse * (scaled - first - unit * second)


def gelu_and_slope(hidden):
    bell = jnp.exp(hidden * hidden * -0.5)
    t = 1.0 / (1.0 + jnp.abs(hidden) * (0.3275911 / math.sqrt(2.0)))
    poly = t * (
        0.5 * 0.254829592
        + t
        * (
            0.5 * -0.284496736
            + t * (0.5 * 1.421413741 + t * (0.5 * -1.453152027 + t * (0.5 * 1.061405429)))
        )
    )
    below = poly * bell
    cumulative = jnp.where(hidden >= 0.0, 1.0 - below, below)
    return hidden * cumulative, cumulative + hidden * bell * (1.0 / math.sqrt(2.0 * math.pi))


def fold8(rows):
    return jnp.sum(rows.reshape(rows.shape[0] // 8, 8, rows.shape[1]), axis=0)


def ds(start, size, unit=None):
    return pl.ds(pl.multiple_of(start, unit or size), size)


class Plan:
    def __init__(self, clips, frames, stream_shape, ff):
        self.C, self.F, self.FF = clips, frames, ff
        self.rows, self.spatial, self.D = stream_shape
        self.frame_split = min(FRAMES, frames)
        self.clip_split = frames // self.frame_split
        self.fd = FRAMES // self.frame_split
        self.td = TUBES // self.frame_split
        self.cd = self.rows // self.fd
        self.pos = self.spatial // TUBES
        self.L = FRAMES * self.pos
        self.S = self.cd * self.td
        self.T = self.S * self.L
        self.R = self.D // frames
        self.Rh = self.R // 2
        self.blocks = clips * frames
        self.half = self.blocks * self.Rh
        self.nj = ff // self.D
        self.X = clips // 2
        self.Y = self.X if frames % self.X == 0 else 1
        powers = all(n & (n - 1) == 0 for n in (clips, frames, self.X, self.Y))
        self.fits = (
            self.clip_split == 1
            and clips >= 2
            and powers
            and frames % 2 == 0
            and self.R % 32 == 0
            and ff == clips * self.D
            and self.FF // 8 == self.D // 2
            and self.pos % 16 == 0
            and 8 % frames == 0
        )

    def steps(self, part):
        bits = lambda n: [1 << i for i in range(n.bit_length() - 1)]
        along_x = [("clip", 2 * b) for b in bits(self.X)]
        along_y = [("frame", b) for b in bits(self.Y)]
        along_z = [("frame", self.Y * b) for b in bits(self.F // self.Y)]
        first = along_x + along_y if part == 0 else along_y + along_x
        return [("clip", 1)] + first + along_z

    def gather_steps(self):
        return [("clip", 2 * (1 << i)) for i in range(self.X.bit_length() - 1)] + [("clip", 1)]

    def place(self, part, chunk, frame):
        clip = (chunk % self.X) * 2 + chunk // self.X
        where = 0
        for axis, bit in self.steps(part):
            where = where * 2 + ((clip if axis == "clip" else frame) // bit) % 2
        return where


class Scatter:
    def __init__(self, plan, me, part, held, slots, result, send_sems, recv_sems):
        self.plan, self.me, self.held, self.slots = plan, me, held, slots
        self.result, self.send_sems, self.recv_sems = result, send_sems, recv_sems
        self.steps = plan.steps(part)
        self.gather = plan.gather_steps()
        self.at = 0
        self.base = 0
        self.size = plan.blocks
        self.copies = []
        self.slot_of_me = (me["clip"] % 2) * plan.X + me["clip"] // 2

    def bit_of(self, axis, bit):
        return (self.me[axis] // bit) % 2

    def partner(self, axis, bit):
        flipped = self.me[axis] + bit * (1 - 2 * self.bit_of(axis, bit))
        return {**self.me, axis: flipped}

    def rows(self, base, size):
        return pl.ds(pl.multiple_of(base * self.plan.Rh, self.plan.Rh), size * self.plan.Rh)

    def send(self, src, dst, axis, bit):
        to = self.partner(axis, bit)
        copy = pltpu.make_async_remote_copy(
            src_ref=src,
            dst_ref=dst,
            send_sem=self.send_sems.at[len(self.copies)],
            recv_sem=self.recv_sems.at[len(self.copies)],
            device_id=(to["clip"], to["frame"]),
            device_id_type=MESH,
        )
        copy.start()
        self.copies.append(copy)

    def start(self):
        if self.at < len(self.steps):
            axis, bit = self.steps[self.at]
            mine = self.bit_of(axis, bit)
            half = self.size // 2
            self.send(
                self.held.at[self.rows(self.base + (1 - mine) * half, half)],
                self.slots[self.at],
                axis,
                bit,
            )
            self.base = self.base + mine * half
            self.size = half
        elif self.at < len(self.steps) + len(self.gather):
            done = self.at - len(self.steps)
            axis, bit = self.gather[done]
            size = 1 << done
            region = self.rows((self.slot_of_me // size) * size, size)
            self.send(self.result.at[region], self.result.at[region], axis, bit)

    def advance(self):
        self.copies[self.at].wait_recv()
        if self.at < len(self.steps):
            slot = self.slots[self.at]
            last = self.at == len(self.steps) - 1
            target = self.result if last else self.held
            target_base = self.slot_of_me if last else self.base
            base, held = self.base, self.held

            def add(i, _):
                total = held[self.rows(base + i, 1)].astype(F32) + slot[self.rows(i, 1)].astype(F32)
                target[self.rows(target_base + i, 1)] = total.astype(BF16)
                return 0

            lax.fori_loop(0, self.size, add, 0)
        self.at += 1
        self.start()

    def finish(self):
        while self.at < len(self.steps) + len(self.gather):
            self.advance()
        for copy in self.copies:
            copy.wait_send()


def layer_kernel(plan, refs):
    D, T, S, L, FF, nj = plan.D, plan.T, plan.S, plan.L, plan.FF, plan.nj
    me = {"clip": lax.axis_index("clip"), "frame": lax.axis_index("frame")}
    frame = me["frame"]
    hidden_tile = D // 3
    xin, gin, n1, qkv, prob, mixed = (refs[k] for k in ("xin", "gin", "n1", "qkv", "prob", "mixed"))
    mid, n2, act, slope, obuf, acc = (refs[k] for k in ("mid", "n2", "act", "slope", "obuf", "acc"))
    dmid, sums, rows_ref = refs["dmid"], refs["sums"], refs["rows"]
    wqkv, wout, wup, wdown = (refs[k] for k in ("wqkv", "wout", "wup", "wdown"))
    dbranch, dmixed, igbuf = n2, mixed, obuf

    def row(i):
        return rows_ref[pl.ds(i, 1), :]

    loads = []
    for i, (src, dst) in enumerate(
        [
            (refs["wqkv_h"], wqkv),
            (refs["wout_h"], wout),
            (refs["wup_h"], wup),
            (refs["wdown_h"].at[pl.ds(0, FF // 2)], wdown.at[0]),
            (refs["wdown_h"].at[pl.ds(FF // 2, FF // 2)], wdown.at[1]),
        ]
    ):
        load = pltpu.make_async_copy(src, dst, refs["load_sems"].at[i])
        load.start()
        loads.append(load)

    barrier = pltpu.get_barrier_semaphore()
    greeted = [(me["clip"], lax.rem(frame + i, plan.F)) for i in range(1, plan.F)]
    for axis, bit in plan.gather_steps():
        flipped = me[axis] + bit * (1 - 2 * ((me[axis] // bit) % 2))
        greeted.append((flipped, frame))
    for peer in greeted:
        pl.semaphore_signal(barrier, inc=1, device_id=peer, device_id_type=MESH)
    pl.semaphore_wait(barrier, len(greeted))

    def tubes(n, device):
        clip_set, tube = n // plan.td, n % plan.td
        return clip_set, ds((device * plan.td + tube) * plan.pos, plan.pos)

    sends = []

    def to_tubes(which, source, target, n):
        arriving = []
        for i in range(plan.F):
            peer = lax.rem(frame + i, plan.F)
            clip_set, positions = tubes(n, peer)
            src = source.at[:, clip_set, positions]
            dst = target.at[n, pl.ds(frame * plan.fd, plan.fd)]
            recv = refs["a2a_recv"].at[which, n, i]
            if i == 0:
                copy = pltpu.make_async_copy(src, dst, recv)
                copy.start()
                arriving.append(copy.wait)
            else:
                copy = pltpu.make_async_remote_copy(
                    src_ref=src,
                    dst_ref=dst,
                    send_sem=refs["a2a_send"].at[which, n, i],
                    recv_sem=recv,
                    device_id=(me["clip"], peer),
                    device_id_type=MESH,
                )
                copy.start()
                sends.append(copy.wait_send)
                arriving.append(copy.wait_recv)
        return arriving

    def to_frames(which, source, target, n):
        arriving = []
        for i in range(plan.F):
            peer = lax.rem(frame + i, plan.F)
            clip_set, positions = tubes(n, frame)
            src = source.at[n, pl.ds(peer * plan.fd, plan.fd)]
            dst = target.at[:, clip_set, positions]
            recv = refs["a2a_recv"].at[which, n, i]
            if i == 0:
                copy = pltpu.make_async_copy(src, dst, recv)
                copy.start()
                arriving.append((lambda: None, copy.wait))
            else:
                copy = pltpu.make_async_remote_copy(
                    src_ref=src,
                    dst_ref=dst,
                    send_sem=refs["a2a_send"].at[which, n, i],
                    recv_sem=recv,
                    device_id=(me["clip"], peer),
                    device_id_type=MESH,
                )
                copy.start()
                arriving.append((copy.wait_recv, copy.wait_send))
        return arriving

    def wait_all(waits):
        for wait in waits:
            wait()

    x_arrives = [to_tubes(0, refs["stream"], xin, n) for n in range(S)]
    g_arrives = [to_tubes(1, refs["grad"], gin, n) for n in range(S)]

    scatters = {}
    for group in range(3):
        for part in range(2):
            at = group * 2 + part
            scatters[group, part] = Scatter(
                plan,
                me,
                part,
                refs["groups"][group].at[part],
                refs["slots"][at],
                refs["res"].at[at],
                refs["rs_send"].at[at],
                refs["rs_recv"].at[at],
            )

    def start(group):
        for part in range(2):
            scatters[group, part].start()

    def advance(group):
        for part in range(2):
            scatters[group, part].advance()

    def seq_rows(ref, s, start, size):
        frames = size // plan.pos
        block = ref[s, pl.ds(start // plan.pos, frames)]
        return block.reshape(size, D)

    sums[...] = jnp.zeros_like(sums)

    def tally(i, value):
        sums[i] += fold8(value)

    lanes = lax.broadcasted_iota(jnp.int32, (1, 128), 1)
    head_masks = [(lanes < 64).astype(BF16), (lanes >= 64).astype(BF16)]
    scale = 1.0 / math.sqrt(D // HEADS)

    for s in range(S):
        wait_all(x_arrives[s])

        def first_norm(i, _):
            x = seq_rows(xin, s, i * ROW_BLOCK, ROW_BLOCK).astype(F32)
            unit, _ = unit_norm(x)
            tally(8, x * x)
            n1[ds(s * L + i * ROW_BLOCK, ROW_BLOCK), :] = (unit * row(0) + row(1)).astype(BF16)
            return 0

        lax.fori_loop(0, L // ROW_BLOCK, first_norm, 0)
        if s == 0:
            loads[0].wait()
        tokens = pl.ds(s * L, L)
        for third in range(3):

            def project(i, _):
                column = third * D + i * hidden_tile
                out = dot_nn(n1[tokens, :], wqkv[:, ds(column, hidden_tile)])
                if third != 1:
                    bias = rows_ref[pl.ds(2 + third // 2, 1), ds(i * hidden_tile, hidden_tile)]
                    out = out + bias
                if third == 0:
                    out = out * scale
                qkv[third, tokens, ds(i * hidden_tile, hidden_tile)] = out.astype(BF16)
                return 0

            lax.fori_loop(0, D // hidden_tile, project, 0)

        def attend(pair, _):
            columns = ds(pair * 128, 128)
            q = qkv[0, tokens, columns]
            k = qkv[1, tokens, columns]
            v = qkv[2, tokens, columns]
            out = jnp.zeros((L, 128), F32)
            for e in range(2):
                scores = dot_nt(q * head_masks[e], k)
                power = jnp.exp(scores - jnp.max(scores, axis=-1, keepdims=True))
                share = 1.0 / jnp.sum(power, axis=-1, keepdims=True)
                weight = (power * share).astype(BF16)
                prob[s * HEADS + pair * 2 + e] = weight
                out = out + dot_nn(weight, v * head_masks[e])
            mixed[tokens, columns] = out.astype(BF16)
            return 0

        lax.fori_loop(0, HEADS // 2, attend, 0)

    loads[1].wait()

    def project_out(i, _):
        columns = ds(i * hidden_tile, hidden_tile)
        mid[:, columns] = dot_nn(mixed[...], wout[:, columns]) + rows_ref[pl.ds(4, 1), columns]
        return 0

    lax.fori_loop(0, D // hidden_tile, project_out, 0)
    for s in range(S):

        def second_norm(i, _):
            rows = ds(s * L + i * ROW_BLOCK, ROW_BLOCK)
            branch = mid[rows, :]
            middle = seq_rows(xin, s, i * ROW_BLOCK, ROW_BLOCK).astype(F32) + branch
            mid[rows, :] = middle
            tally(9, middle * middle)
            tally(11, branch * branch)
            unit, _ = unit_norm(middle)
            n2[rows, :] = (unit * row(5) + row(6)).astype(BF16)
            return 0

        lax.fori_loop(0, L // ROW_BLOCK, second_norm, 0)

    loads[2].wait()

    def up(i, _):
        j, part = i // 3, i % 3
        columns = ds(part * hidden_tile, hidden_tile)
        bias = rows_ref[pl.ds(8 + j, 1), columns]
        hidden = dot_nn(n2[...], wup[:, ds(i * hidden_tile, hidden_tile)]) + bias
        active, steep = gelu_and_slope(hidden)
        act[ds(j * T, T), columns] = active.astype(BF16)
        slope[ds(j * T, T), columns] = steep.astype(BF16)
        return 0

    lax.fori_loop(0, FF // hidden_tile, up, 0)
    loads[3].wait()
    loads[4].wait()
    out_arrives = []
    for s in range(S):

        def down(i, _):
            columns = ds(i * hidden_tile, hidden_tile)
            total = rows_ref[pl.ds(7, 1), columns]
            for j in range(nj):
                per = nj // 2
                total = total + dot_nn(
                    act[pl.ds(j * T + s * L, L), :],
                    wdown[j // per, pl.ds((j % per) * D, D), columns],
                )
            result = total + mid[pl.ds(s * L, L), columns]
            sums[10, :, columns] += fold8(result * result)
            sums[12, :, columns] += fold8(total * total)
            obuf[s, :, :, columns] = result.astype(BF16).reshape(FRAMES, plan.pos, hidden_tile)
            return 0

        lax.fori_loop(0, D // hidden_tile, down, 0)
        out_arrives += to_frames(2, obuf, refs["out_h"], s)

    for s in range(S):
        wait_all(g_arrives[s])
    wide = D // 2

    def put(group, chunk, frame_block, block):
        for part in range(2):
            at = plan.place(part, chunk, frame_block)
            rows = pl.ds(pl.multiple_of(at * plan.Rh, plan.Rh), plan.Rh)
            piece = block[part * plan.Rh : (part + 1) * plan.Rh]
            refs["groups"][group][part, rows, :] = piece.astype(BF16)

    g_rows = gin[...].reshape(T, D)

    def grad_down(i, _):
        a = act[ds((i // 2) * T, T), ds((i % 2) * wide, wide)]
        out = dot_tn(a, gin[...].reshape(T, D))
        per = 8 // plan.F
        for c in range(plan.C):
            put(0, c, i // per, out[c * plan.R : (c + 1) * plan.R])
        return 0

    del g_rows
    lax.fori_loop(0, FF // wide, grad_down, 0)
    start(0)

    def through_gelu(i, _):
        j, part = i // 3, i % 3
        columns = ds(part * hidden_tile, hidden_tile)
        per = nj // 2
        rows = ds((j % per) * D + part * hidden_tile, hidden_tile)
        d_active = dot_nt(gin[...].reshape(T, D), wdown[j // per, rows, :])
        d_hidden = (d_active * slope[ds(j * T, T), columns].astype(F32)).astype(BF16)
        slope[ds(j * T, T), columns] = d_hidden
        sums[13 + j, :, columns] += fold8(d_hidden.astype(F32))
        return 0

    lax.fori_loop(0, FF // hidden_tile, through_gelu, 0)
    advance(0)

    def grad_columns(group, chunk, lhs, rhs):
        def half(m, _):
            out = dot_tn(lhs(ds(m * wide, wide)), rhs())
            for f in range(plan.F // 2):
                put(group, chunk, m * (plan.F // 2) + f, out[f * plan.R : (f + 1) * plan.R])
            return 0

        lax.fori_loop(0, 2, half, 0)

    def grad_up(c, _):
        grad_columns(
            1, c, lambda columns: n2[:, columns], lambda: slope[ds(c * T, T), :]
        )
        return 0

    lax.fori_loop(0, plan.C, grad_up, 0)
    start(1)

    def d_two(i, _):
        rows = ds(i * hidden_tile, hidden_tile)
        total = jnp.zeros((T, hidden_tile), F32)
        for j in range(nj):
            total = total + dot_nt(slope[pl.ds(j * T, T), :], wup[rows, pl.ds(j * D, D)])
        acc[:, rows] = total
        return 0

    lax.fori_loop(0, D // hidden_tile, d_two, 0)
    advance(1)

    for s in range(S):

        def second_norm_back(i, _):
            rows = ds(s * L + i * ROW_BLOCK, ROW_BLOCK)
            up_grad = acc[rows, :]
            unit, inverse = unit_norm(mid[rows, :])
            g = seq_rows(gin, s, i * ROW_BLOCK, ROW_BLOCK).astype(F32)
            d_middle = g + norm_pull(up_grad * row(5), unit, inverse)
            dmid[rows, :] = d_middle
            low = d_middle.astype(BF16)
            dbranch[rows, :] = low
            tally(4, low.astype(F32))
            tally(5, up_grad * unit)
            tally(6, up_grad)
            tally(7, g)
            return 0

        lax.fori_loop(0, L // ROW_BLOCK, second_norm_back, 0)

    advance(0)
    last = plan.C - 1
    grad_columns(2, last, lambda columns: mixed[:, columns], lambda: dbranch[...])

    def through_out(i, _):
        columns = ds(i * hidden_tile, hidden_tile)
        dmixed[:, columns] = dot_nt(dbranch[...], wout[columns, :]).astype(BF16)
        return 0

    lax.fori_loop(0, D // hidden_tile, through_out, 0)

    for s in range(S):
        tokens = pl.ds(s * L, L)

        def attend_back(pair, _):
            columns = ds(pair * 128, 128)
            q = qkv[0, tokens, columns]
            k = qkv[1, tokens, columns]
            v = qkv[2, tokens, columns]
            d_out = dmixed[tokens, columns]
            zero = jnp.zeros((L, 128), F32)
            d_q, d_k, d_v = zero, zero, zero
            for e in range(2):
                weight = prob[s * HEADS + pair * 2 + e]
                own = d_out * head_masks[e]
                d_weight = dot_nt(own, v)
                d_v = d_v + dot_tn(weight, own)
                wide_weight = weight.astype(F32)
                centre = jnp.sum(wide_weight * d_weight, axis=-1, keepdims=True)
                d_score = (wide_weight * (d_weight - centre)).astype(BF16)
                d_q = d_q + dot_nn(d_score, k * head_masks[e])
                d_k = d_k + dot_tn(d_score, q * head_masks[e])
            qkv[0, tokens, columns] = (d_q * scale).astype(BF16)
            qkv[1, tokens, columns] = d_k.astype(BF16)
            qkv[2, tokens, columns] = d_v.astype(BF16)
            return 0

        lax.fori_loop(0, HEADS // 2, attend_back, 0)
        advance(s % 2)

    def grad_qkv(c, _):
        grad_columns(2, c, lambda columns: n1[:, columns], lambda: qkv[c])
        return 0

    lax.fori_loop(0, 3, grad_qkv, 0)
    start(2)

    def d_one(i, _):
        rows = ds(i * hidden_tile, hidden_tile)
        total = jnp.zeros((T, hidden_tile), F32)
        for j in range(3):
            total = total + dot_nt(qkv[j], wqkv[rows, pl.ds(j * D, D)])
        acc[:, rows] = total
        return 0

    lax.fori_loop(0, D // hidden_tile, d_one, 0)
    advance(2)
    for recv, send in out_arrives:
        send()
    in_arrives = []
    for s in range(S):

        def first_norm_back(i, _):
            rows = ds(s * L + i * ROW_BLOCK, ROW_BLOCK)
            up_grad = acc[rows, :]
            x = seq_rows(xin, s, i * ROW_BLOCK, ROW_BLOCK).astype(F32)
            unit, inverse = unit_norm(x)
            total = dmid[rows, :] + norm_pull(up_grad * row(0), unit, inverse)
            frames = ROW_BLOCK // plan.pos
            igbuf[s, pl.ds(i * frames, frames)] = total.astype(BF16).reshape(frames, plan.pos, D)
            tally(0, up_grad * unit)
            tally(1, up_grad)
            tally(2, qkv[0, rows, :].astype(F32))
            tally(3, qkv[2, rows, :].astype(F32))
            return 0

        lax.fori_loop(0, L // ROW_BLOCK, first_norm_back, 0)
        in_arrives += to_frames(3, igbuf, refs["ig_h"], s)

    vbuf, vrecv = refs["vbuf"], refs["vrecv"]
    count = sums.shape[0]
    for i in range(count):
        vbuf[0, pl.ds(i, 1), :] = jnp.sum(sums[i], axis=0, keepdims=True)
    hops = plan.steps(0)
    small = []
    for i, (axis, bit) in enumerate(hops):
        flipped = me[axis] + bit * (1 - 2 * ((me[axis] // bit) % 2))
        to = {**me, axis: flipped}
        copy = pltpu.make_async_remote_copy(
            src_ref=vbuf.at[i],
            dst_ref=vrecv.at[i],
            send_sem=refs["v_send"].at[i],
            recv_sem=refs["v_recv"].at[i],
            device_id=(to["clip"], to["frame"]),
            device_id_type=MESH,
        )
        copy.start()
        small.append(copy)
        if i == 0:
            advance(0)
            advance(1)
        elif i % 2 == 0:
            advance(2)
        copy.wait_recv()
        vbuf[i + 1] = vbuf[i] + vrecv[i]
    refs["vec"][...] = vbuf[len(hops)]
    for copy in small:
        copy.wait_send()
    for group in (0, 1, 2):
        for part in range(2):
            scatters[group, part].finish()
    for recv, send in out_arrives:
        recv()
    for recv, send in in_arrives:
        send()
        recv()
    wait_all(sends)


def fused(plan, stream, masked, weights, rows):
    D, T, S, L, FF = plan.D, plan.T, plan.S, plan.L, plan.FF
    n_steps = len(plan.steps(0))
    n_hops = n_steps + len(plan.gather_steps())
    n_vec = 13 + plan.nj
    vec_rows = -(-n_vec // 8) * 8
    vmem = lambda shape, kind=BF16: pltpu.VMEM(shape, kind)
    scratch = {
        "wqkv": vmem((D, 3 * D)),
        "wout": vmem((D, D)),
        "wup": vmem((D, FF)),
        "wdown": vmem((2, FF // 2, D)),
        "xin": vmem((S, FRAMES, plan.pos, D)),
        "gin": vmem((S, FRAMES, plan.pos, D)),
        "n1": vmem((T, D)),
        "qkv": vmem((3, T, D)),
        "prob": vmem((S * HEADS, L, L)),
        "mixed": vmem((T, D)),
        "mid": vmem((T, D), F32),
        "n2": vmem((T, D)),
        "act": vmem((plan.nj * T, D)),
        "slope": vmem((plan.nj * T, D)),
        "obuf": vmem((S, FRAMES, plan.pos, D)),
        "acc": vmem((T, D), F32),
        "dmid": vmem((T, D), F32),
        "sums": vmem((n_vec, 8, D), F32),
        "g_down": vmem((2, plan.half, D)),
        "g_up": vmem((2, plan.half, D)),
        "vbuf": vmem((n_steps + 1, vec_rows, D), F32),
        "vrecv": vmem((n_steps, vec_rows, D), F32),
        "load_sems": pltpu.SemaphoreType.DMA((5,)),
        "a2a_send": pltpu.SemaphoreType.DMA((4, S, plan.F)),
        "a2a_recv": pltpu.SemaphoreType.DMA((4, S, plan.F)),
        "rs_send": pltpu.SemaphoreType.DMA((6, n_hops)),
        "rs_recv": pltpu.SemaphoreType.DMA((6, n_hops)),
        "v_send": pltpu.SemaphoreType.DMA((n_steps,)),
        "v_recv": pltpu.SemaphoreType.DMA((n_steps,)),
    }
    for i in range(n_steps):
        scratch[f"slot{i}"] = vmem((4 if i == 0 else 6, plan.half >> (i + 1), D))
    names_in = ["stream", "grad", "wqkv_h", "wout_h", "wup_h", "wdown_h", "rows"]
    names_out = ["out_h", "ig_h", "res", "vec"]
    names = names_in + names_out + list(scratch)

    def kernel(*args):
        refs = dict(zip(names, args))
        refs["groups"] = (refs["g_down"], refs["g_up"], refs["wdown"])
        refs["slots"] = []
        for at in range(6):
            first = (
                refs["slot0"].at[at]
                if at < 4
                else refs["act"].at[pl.ds((at - 4) * (plan.half // 2), plan.half // 2)]
            )
            later = [refs[f"slot{i}"].at[at] for i in range(1, n_steps)]
            refs["slots"].append([first] + later)
        layer_kernel(plan, refs)

    hbm = pl.BlockSpec(memory_space=pl.ANY)
    in_vmem = pl.BlockSpec(memory_space=pltpu.VMEM)
    token_shape = (plan.fd, plan.cd, plan.spatial, D)
    out = pl.pallas_call(
        kernel,
        out_shape=(
            jax.ShapeDtypeStruct(token_shape, BF16),
            jax.ShapeDtypeStruct(token_shape, BF16),
            jax.ShapeDtypeStruct((6, plan.C * plan.Rh, D), BF16),
            jax.ShapeDtypeStruct((vec_rows, D), F32),
        ),
        in_specs=[hbm] * 6 + [in_vmem],
        out_specs=(hbm, hbm, in_vmem, in_vmem),
        scratch_shapes=list(scratch.values()),
        compiler_params=pltpu.CompilerParams(
            collective_id=0, has_side_effects=True, vmem_limit_bytes=VMEM_LIMIT
        ),
        name="tube_layer",
    )(stream.reshape(token_shape), masked.reshape(token_shape), *weights, rows)
    return out


VMEM_LIMIT = 64 * 1024 * 1024 - 512 * 1024


def with_kernel(
    plan,
    stream,
    out_grad,
    token_mask,
    ln1_gain,
    ln1_bias,
    w_qkv,
    b_qv,
    w_out,
    b_out,
    ln2_gain,
    ln2_bias,
    w_up,
    b_up,
    w_down,
    b_down,
):
    D, C, R, Rh = plan.D, plan.C, plan.R, plan.Rh
    masked = jnp.where(token_mask[:, :, None] == 1, out_grad, jnp.zeros((), BF16))
    small = [ln1_gain, ln1_bias, b_qv, b_out, ln2_gain, ln2_bias, b_down, b_up]
    rows = jnp.concatenate(small).reshape(8 + plan.nj, D)
    output, input_grad, gathered, totals = fused(
        plan, stream, masked, (w_qkv, w_out, w_up, w_down), rows
    )
    gathered = gathered.reshape(3, 2, C, Rh, D).astype(F32)
    g_down = jnp.transpose(gathered[0], (1, 0, 2, 3)).reshape(C * R, D)
    by_row = lambda group: jnp.transpose(gathered[group], (0, 2, 1, 3))
    g_up = by_row(1).reshape(R, C * D)
    projections = by_row(2)
    g_qkv = projections[:, :, :3].reshape(R, 3 * D)
    g_out = projections[:, :, 3].reshape(R, D)
    frame = lax.axis_index("frame")

    def own(first, count=1):
        flat = totals[first : first + count].reshape(-1)
        share = count * D // plan.F
        return lax.dynamic_slice(flat, (frame * share,), (share,))

    entries = plan.T * D * C * plan.F
    squares = jnp.sum(totals[8:13], axis=-1)
    statistics = jnp.sqrt(squares / entries)
    return (
        output.reshape(stream.shape),
        input_grad.reshape(stream.shape),
        own(0),
        own(1),
        g_qkv,
        own(2, 2),
        g_out,
        own(4),
        own(5),
        own(6),
        g_up,
        own(13, plan.nj),
        g_down,
        own(7),
        statistics,
    )


def layer_norm(inputs, norm_gain, norm_shift):
    center = jnp.mean(inputs, axis=-1, keepdims=True)
    shifted = inputs - center
    spread = jnp.mean(shifted * shifted, axis=-1, keepdims=True)
    inverse = lax.rsqrt(spread + EPS)
    unit = shifted * inverse
    return (unit * norm_gain + norm_shift, unit, inverse)


def norm_backward(upstream, unit, inverse, norm_gain):
    scaled = upstream * norm_gain
    first = jnp.mean(scaled, axis=-1, keepdims=True)
    second = jnp.mean(scaled * unit, axis=-1, keepdims=True)
    return inverse * (scaled - first - unit * second)


def gelu_slope(hidden_state):
    cumulative = 0.5 * (1.0 + lax.erf(hidden_state * (1.0 / math.sqrt(2.0))))
    density = jnp.exp(-0.5 * hidden_state * hidden_state) * (1.0 / math.sqrt(2.0 * math.pi))
    return cumulative + hidden_state * density


def with_collectives(
    stream,
    out_grad,
    token_mask,
    ln1_gain,
    ln1_bias,
    w_qkv,
    b_qv,
    w_out,
    b_out,
    ln2_gain,
    ln2_bias,
    w_up,
    b_up,
    w_down,
    b_down,
):
    frame_count = lax.axis_size("frame")
    clip_count = lax.axis_size("clip")
    device_count = clip_count * frame_count
    frame_split = min(FRAMES, frame_count)
    clip_split = frame_count // frame_split
    frames_dev = FRAMES // frame_split
    tubes_dev = TUBES // frame_split
    row_count, spatial, width = stream.shape
    clips_dev = row_count // frames_dev
    clip_sets = clips_dev // clip_split
    tube_pos = spatial // TUBES
    length = FRAMES * tube_pos
    head_dim = width // HEADS
    scale = 1.0 / math.sqrt(head_dim)

    def leaving(tensor):
        return tensor.reshape(frames_dev, clip_sets, frame_count, tubes_dev * tube_pos, width)

    def arranged(tensor):
        tensor = tensor.reshape(clip_split, FRAMES, clip_sets, tubes_dev, tube_pos, width)
        tensor = jnp.transpose(tensor, (0, 2, 3, 1, 4, 5))
        return tensor.reshape(-1, width)

    def restored(tensor):
        tensor = tensor.reshape(clip_split, clip_sets, tubes_dev, FRAMES, tube_pos, width)
        tensor = jnp.transpose(tensor, (0, 3, 1, 2, 4, 5))
        return tensor.reshape(frame_count * frames_dev, clip_sets, 1, tubes_dev * tube_pos, width)

    masked = jnp.where(token_mask[:, :, None] == 1, out_grad, jnp.zeros((), jnp.bfloat16))
    arrived = (
        lax.all_to_all(leaving(stream), "frame", split_axis=2, concat_axis=0, tiled=True),
        lax.all_to_all(leaving(masked), "frame", split_axis=2, concat_axis=0, tiled=True),
    )
    inputs = arranged(arrived[0]).astype(jnp.float32)
    grad_y = arranged(arrived[1])
    seq_count = inputs.shape[0] // length

    def split_heads(tensor):
        return tensor.reshape(seq_count, length, HEADS, head_dim)

    def attention_scores(queries, key_part):
        return (
            jnp.einsum("slhe,smhe->shlm", queries, key_part, preferred_element_type=jnp.float32)
            * scale
        )

    first_normed_input, unit_one, inverse_one = layer_norm(inputs, ln1_gain, ln1_bias)
    first_normed_input = first_normed_input.astype(jnp.bfloat16)
    third_bias_term = jnp.concatenate(
        [b_qv[:width], jnp.zeros((width,), jnp.float32), b_qv[width:]]
    )
    query_key_value = (
        jnp.dot(first_normed_input, w_qkv, preferred_element_type=jnp.float32) + third_bias_term
    ).astype(jnp.bfloat16)
    queries = split_heads(query_key_value[:, :width])
    key_part = split_heads(query_key_value[:, width : 2 * width])
    values = split_heads(query_key_value[:, 2 * width :])
    scores = attention_scores(queries, key_part)
    largest = jnp.max(scores, axis=-1, keepdims=True)
    logsum = largest + jnp.log(jnp.sum(jnp.exp(scores - largest), axis=-1, keepdims=True))
    attend_low = jnp.exp(scores - logsum).astype(jnp.bfloat16)
    mixed_heads = jnp.einsum(
        "shlm,smhe->slhe", attend_low, values, preferred_element_type=jnp.float32
    )
    mixed_heads = mixed_heads.reshape(-1, width).astype(jnp.bfloat16)
    attention_branch = jnp.dot(mixed_heads, w_out, preferred_element_type=jnp.float32) + b_out
    middle = inputs + attention_branch
    second_normed_input, unit_two, inverse_two = layer_norm(middle, ln2_gain, ln2_bias)
    second_normed_input = second_normed_input.astype(jnp.bfloat16)
    hidden_state = jnp.dot(second_normed_input, w_up, preferred_element_type=jnp.float32) + b_up
    activated_hidden = jax.nn.gelu(hidden_state, approximate=False).astype(jnp.bfloat16)
    feedforward_branch = (
        jnp.dot(activated_hidden, w_down, preferred_element_type=jnp.float32) + b_down
    )
    result = middle + feedforward_branch
    squares = jnp.stack(
        [
            jnp.sum(inputs * inputs),
            jnp.sum(middle * middle),
            jnp.sum(result * result),
            jnp.sum(attention_branch * attention_branch),
            jnp.sum(feedforward_branch * feedforward_branch),
        ]
    )
    totals = lax.psum(squares, ("clip", "frame"))
    statistics = jnp.sqrt(totals / (row_count * spatial * width * device_count))
    grad_w_down = jnp.einsum(
        "tf,td->fd", activated_hidden, grad_y, preferred_element_type=jnp.float32
    )
    grad_b_down = jnp.sum(grad_y.astype(jnp.float32), axis=0)
    d_active = jnp.einsum("td,fd->tf", grad_y, w_down, preferred_element_type=jnp.float32)
    d_hidden = (d_active * gelu_slope(hidden_state)).astype(jnp.bfloat16)
    grad_w_up = jnp.einsum(
        "td,tf->df", second_normed_input, d_hidden, preferred_element_type=jnp.float32
    )
    grad_b_up = jnp.sum(d_hidden.astype(jnp.float32), axis=0)
    d_two = jnp.einsum("tf,df->td", d_hidden, w_up, preferred_element_type=jnp.float32)
    grad_ln2_gain = jnp.sum(d_two * unit_two, axis=0)
    grad_ln2_bias = jnp.sum(d_two, axis=0)
    d_middle = grad_y.astype(jnp.float32) + norm_backward(d_two, unit_two, inverse_two, ln2_gain)
    d_branch = d_middle.astype(jnp.bfloat16)
    grad_w_out = jnp.einsum("td,te->de", mixed_heads, d_branch, preferred_element_type=jnp.float32)
    grad_b_out = jnp.sum(d_branch.astype(jnp.float32), axis=0)
    d_mixed = jnp.einsum("te,de->td", d_branch, w_out, preferred_element_type=jnp.float32)
    d_mixed = split_heads(d_mixed.astype(jnp.bfloat16))
    again = attention_scores(queries, key_part)
    attend = jnp.exp(again - logsum)
    attend_again = attend.astype(jnp.bfloat16)
    d_attend = jnp.einsum("slhe,smhe->shlm", d_mixed, values, preferred_element_type=jnp.float32)
    d_values = jnp.einsum(
        "shlm,slhe->smhe", attend_again, d_mixed, preferred_element_type=jnp.float32
    )
    centre_term = jnp.sum(attend * d_attend, axis=-1, keepdims=True)
    d_scores = (attend * (d_attend - centre_term)).astype(jnp.bfloat16)
    d_queries = (
        jnp.einsum("shlm,smhe->slhe", d_scores, key_part, preferred_element_type=jnp.float32)
        * scale
    )
    d_keys = (
        jnp.einsum("shlm,slhe->smhe", d_scores, queries, preferred_element_type=jnp.float32) * scale
    )
    d_qkv = jnp.concatenate(
        [d_queries.reshape(-1, width), d_keys.reshape(-1, width), d_values.reshape(-1, width)],
        axis=1,
    ).astype(jnp.bfloat16)
    grad_w_qkv = jnp.einsum(
        "td,te->de", first_normed_input, d_qkv, preferred_element_type=jnp.float32
    )
    bias_sums = jnp.sum(d_qkv.astype(jnp.float32), axis=0)
    grad_b_qv = jnp.concatenate([bias_sums[:width], bias_sums[2 * width :]])
    d_one = jnp.einsum("te,de->td", d_qkv, w_qkv, preferred_element_type=jnp.float32)
    grad_ln1_gain = jnp.sum(d_one * unit_one, axis=0)
    grad_ln1_bias = jnp.sum(d_one, axis=0)
    d_inputs = d_middle + norm_backward(d_one, unit_one, inverse_one, ln1_gain)
    departed = (
        lax.all_to_all(
            restored(result.astype(jnp.bfloat16)), "frame", split_axis=0, concat_axis=2, tiled=True
        ),
        lax.all_to_all(
            restored(d_inputs.astype(jnp.bfloat16)),
            "frame",
            split_axis=0,
            concat_axis=2,
            tiled=True,
        ),
    )
    output = departed[0].reshape(row_count, spatial, width)
    input_grad = departed[1].reshape(row_count, spatial, width)
    gradients = [
        grad_ln1_gain,
        grad_ln1_bias,
        grad_w_qkv,
        grad_b_qv,
        grad_w_out,
        grad_b_out,
        grad_ln2_gain,
        grad_ln2_bias,
        grad_w_up,
        grad_b_up,
        grad_w_down,
        grad_b_down,
    ]
    grouped = jnp.concatenate([item.reshape(frame_count, -1) for item in gradients], axis=1)
    extent_all = grouped.shape[1]
    padding = -extent_all % clip_count
    grouped = jnp.concatenate([grouped, jnp.zeros((frame_count, padding), jnp.float32)], axis=1)
    own_rows = lax.psum_scatter(
        grouped.astype(jnp.bfloat16), "frame", scatter_dimension=0, tiled=True
    ).astype(jnp.float32)
    summed = lax.psum(own_rows, "clip").reshape(-1)
    finished = []
    offset = 0
    for item in gradients:
        extent = item.size // frame_count
        local_shape = (item.shape[0] // frame_count,) + item.shape[1:]
        finished.append(summed[offset : offset + extent].reshape(local_shape))
        offset = offset + extent
    return (
        output,
        input_grad,
        finished[0],
        finished[1],
        finished[2],
        finished[3],
        finished[4],
        finished[5],
        finished[6],
        finished[7],
        finished[8],
        finished[9],
        finished[10],
        finished[11],
        statistics,
    )


def solution(mesh):
    clips, frames = mesh.shape["clip"], mesh.shape["frame"]

    def on_device(stream, *rest):
        ff = rest[-4].shape[1]
        plan = Plan(clips, frames, stream.shape, ff)
        if plan.fits:
            return with_kernel(plan, stream, *rest)
        return with_collectives(stream, *rest)

    tokens = P(("clip", "frame"), None, None)
    in_specs = (tokens, tokens, P(("clip", "frame"), None)) + (P(),) * 12
    rows, vector = P("frame", None), P("frame")
    out_specs = (
        tokens,
        tokens,
        vector,
        vector,
        rows,
        vector,
        rows,
        vector,
        vector,
        vector,
        rows,
        vector,
        rows,
        vector,
        P(),
    )
    return jax.shard_map(
        on_device, mesh=mesh, in_specs=in_specs, out_specs=out_specs, check_vma=False
    )
```

```python
import functools
import math
from types import SimpleNamespace

import jax
import jax.numpy as jnp
from jax import lax
from jax.experimental import pallas as pl
from jax.experimental.pallas import tpu as pltpu
from jax.sharding import PartitionSpec as P

HEADS = 12
FRAMES = 16
TUBES = 16
EPS = 1e-05

F32 = jnp.float32
BF16 = jnp.bfloat16
MESH = pl.DeviceIdType.MESH
ROW_BLOCK = 64
CLIP = "clip"
FRAME = "frame"


SIXTHS = 6
SHARES = (
    (("yzx", 2), ("xyz", 2), ("zyx", 2),),
    (("yxz", 2), ("xzy", 2), ("xyz", 2),),
    (("xzy", 2), ("yxz", 2), ("xyz", 2),),
)
DUE = dict(
    GU1=(0,),
    GU2=(1,),
    GU3=(2,),
    DM=(3, 4),
    AB00=(5,),
    AB01=(0, 1),
    AB10=(2,),
    D1=(0, 3, 4),
    L11=(1,),
    V0=(6, 7, 8, 2, 5),
    V1=(0, 4, 3, 6, 1, 7, 2, 8, 5, 0),
    V2=(3, 4, 8, 7, 6, 2, 0, 1, 4),
    V3=(0, 5, 2, 1, 2, 3, 4, 1, 8, 4, 3, 7, 3, 6),
    V4=(5, 6, 8, 7, 5, 6, 5, 8, 6),
    END=(7, 8, 7),
)


def dot_nn(lhs, rhs):
    return lax.dot_general(lhs, rhs, (((1,), (0,)), ((), ())), preferred_element_type=F32)


def dot_nt(lhs, rhs):
    return lax.dot_general(lhs, rhs, (((1,), (1,)), ((), ())), preferred_element_type=F32)


def dot_tn(lhs, rhs):
    return lax.dot_general(lhs, rhs, (((0,), (0,)), ((), ())), preferred_element_type=F32)


def unit_norm(rows):
    shifted = rows - jnp.mean(rows, axis=-1, keepdims=True)
    inverse = lax.rsqrt(jnp.mean(shifted * shifted, axis=-1, keepdims=True) + EPS)
    return shifted * inverse, inverse


def norm_pull(scaled, unit, inverse):
    first = jnp.mean(scaled, axis=-1, keepdims=True)
    second = jnp.mean(scaled * unit, axis=-1, keepdims=True)
    return inverse * (scaled - first - unit * second)


def gelu_and_slope(hidden):
    bell = jnp.exp(hidden * hidden * -0.5)
    t = 1.0 / (1.0 + jnp.abs(hidden) * (0.3275911 / math.sqrt(2.0)))
    poly = t * (
        0.5 * 0.254829592
        + t
        * (
            0.5 * -0.284496736
            + t * (0.5 * 1.421413741 + t * (0.5 * -1.453152027 + t * (0.5 * 1.061405429)))
        )
    )
    below = poly * bell
    cumulative = jnp.where(hidden >= 0.0, 1.0 - below, below)
    return hidden * cumulative, cumulative + hidden * bell * (1.0 / math.sqrt(2.0 * math.pi))


def fold8(rows):
    return jnp.sum(rows.reshape(rows.shape[0] // 8, 8, rows.shape[1]), axis=0)


def ds(start, size, unit=None):
    return pl.ds(pl.multiple_of(start, unit or size), size)


class Plan:
    def __init__(self, clips, frames, stream_shape, ff):
        self.C, self.F, self.FF = clips, frames, ff
        self.rows, self.spatial, self.D = stream_shape
        self.frame_split = min(FRAMES, frames)
        self.clip_split = frames // self.frame_split
        self.fd = FRAMES // self.frame_split
        self.td = TUBES // self.frame_split
        self.cd = self.rows // self.fd
        self.pos = self.spatial // TUBES
        self.L = FRAMES * self.pos
        self.S = self.cd * self.td
        self.T = self.S * self.L
        self.R = self.D // frames
        self.blocks = clips * frames
        self.whole = self.blocks * self.R
        self.parts = []
        for group, shares in enumerate(SHARES):
            first = 0
            for part, (order, share) in enumerate(shares):
                rows = self.R * share // SIXTHS
                self.parts.append((group, order, first, rows))
                first += rows
        self.nj = ff // self.D
        self.X = clips // 2
        self.Y = self.X if frames % self.X == 0 else 1
        powers = all(n & (n - 1) == 0 for n in (clips, frames, self.X, self.Y))
        self.fits = (
            self.clip_split == 1
            and clips >= 2
            and powers
            and frames % 2 == 0
            and self.R % (16 * SIXTHS) == 0
            and ff == clips * self.D
            and self.pos % 16 == 0
            and self.D % (ff // frames) == 0
        )

    def steps(self, order):
        bits = lambda n: [1 << i for i in range(n.bit_length() - 1)]
        along = dict(
            x=[(CLIP, 2 * b) for b in bits(self.X)],
            y=[(FRAME, b) for b in bits(self.Y)],
            z=[(FRAME, self.Y * b) for b in bits(self.F // self.Y)],
        )
        return [(CLIP, 1)] + along[order[0]] + along[order[1]] + along[order[2]]

    def gather_steps(self):
        return [(CLIP, 2 * (1 << i)) for i in range(self.X.bit_length() - 1)] + [(CLIP, 1)]

    def place(self, order, chunk, frame):
        clip = (chunk % self.X) * 2 + chunk // self.X
        where = 0
        for axis, bit in self.steps(order):
            where = where * 2 + ((clip if axis == CLIP else frame) // bit) % 2
        return where


class Scatter:
    def __init__(self, plan, me, part, held, slots, results, send_sems, recv_sems):
        group, order, first, self.height = plan.parts[part]
        self.plan, self.me = plan, me
        self.steps = plan.steps(order)
        self.gather = plan.gather_steps()
        rows = lambda count, per: pl.ds(first * per, count * per)
        self.held = held.at[rows(self.height, plan.blocks)]
        self.slots = [
            slot.at[rows(self.height, plan.blocks >> (i + 1))] for i, slot in enumerate(slots)
        ]
        self.result = results.at[rows(self.height, plan.C)]
        self.send_sems, self.recv_sems = send_sems.at[part], recv_sems.at[part]
        self.at = 0
        self.base = 0
        self.size = plan.blocks
        self.copies = []
        self.slot_of_me = (me[CLIP] % 2) * plan.X + me[CLIP] // 2

    def bit_of(self, axis, bit):
        return (self.me[axis] // bit) % 2

    def partner(self, axis, bit):
        flipped = self.me[axis] + bit * (1 - 2 * self.bit_of(axis, bit))
        return {**self.me, axis: flipped}

    def rows(self, base, size):
        return pl.ds(pl.multiple_of(base * self.height, self.height), size * self.height)

    def send(self, src, dst, axis, bit):
        to = self.partner(axis, bit)
        copy = pltpu.make_async_remote_copy(
            src_ref=src,
            dst_ref=dst,
            send_sem=self.send_sems.at[len(self.copies)],
            recv_sem=self.recv_sems.at[len(self.copies)],
            device_id=(to[CLIP], to[FRAME]),
            device_id_type=MESH,
        )
        copy.start()
        self.copies.append(copy)

    def start(self):
        if self.at < len(self.steps):
            axis, bit = self.steps[self.at]
            mine = self.bit_of(axis, bit)
            half = self.size // 2
            self.send(
                self.held.at[self.rows(self.base + (1 - mine) * half, half)],
                self.slots[self.at],
                axis,
                bit,
            )
            self.base = self.base + mine * half
            self.size = half
        elif self.at < len(self.steps) + len(self.gather):
            done = self.at - len(self.steps)
            axis, bit = self.gather[done]
            size = 1 << done
            region = self.rows((self.slot_of_me // size) * size, size)
            self.send(self.result.at[region], self.result.at[region], axis, bit)

    def advance(self):
        self.copies[self.at].wait_recv()
        if self.at < len(self.steps):
            slot = self.slots[self.at]
            last = self.at == len(self.steps) - 1
            target = self.result if last else self.held
            target_base = self.slot_of_me if last else self.base
            base, held = self.base, self.held

            def add(i, _):
                total = held[self.rows(base + i, 1)].astype(F32) + slot[self.rows(i, 1)].astype(F32)
                target[self.rows(target_base + i, 1)] = total.astype(BF16)
                return 0

            lax.fori_loop(0, self.size, add, 0)
        self.at += 1
        self.start()

    def done(self):
        return self.at == len(self.steps) + len(self.gather)

    def finish(self):
        assert self.done()
        for copy in self.copies:
            copy.wait_send()


def layer_kernel(plan, refs):
    D, T, S, L, FF, nj = plan.D, plan.T, plan.S, plan.L, plan.FF, plan.nj
    me = {CLIP: lax.axis_index(CLIP), FRAME: lax.axis_index(FRAME)}
    frame = me[FRAME]
    xin, gin, n1, qkv, prob, mixed = refs.xin, refs.gin, refs.n1, refs.qkv, refs.prob, refs.mixed
    mid, n2, act, slope, obuf, acc = refs.mid, refs.n2, refs.act, refs.slope, refs.obuf, refs.acc
    dmid, sums = refs.dmid, refs.sums
    for source, target in zip(refs.small, refs.small_rows):
        target[...] = source[...].reshape(1, -1)
    ln1_gain, ln1_bias, b_qv, b_out, ln2_gain, ln2_bias, b_up, b_down = refs.small_rows
    wqkv, wout, wup, wdown = refs.wqkv, refs.wout, refs.wup, refs.wdown
    dbranch, dmixed, igbuf = n2, mixed, obuf

    barrier = pltpu.get_barrier_semaphore()
    greeted = [(me[CLIP], lax.rem(frame + i, plan.F)) for i in range(1, plan.F)]
    for axis, bit in plan.gather_steps():
        flipped = me[axis] + bit * (1 - 2 * ((me[axis] // bit) % 2))
        greeted.append((flipped, frame))
    for peer in greeted:
        pl.semaphore_signal(barrier, inc=1, device_id=peer, device_id_type=MESH)
    pl.semaphore_wait(barrier, len(greeted))

    def tubes(n, device):
        clip_set, tube = n // plan.td, n % plan.td
        return clip_set, ds((device * plan.td + tube) * plan.pos, plan.pos)

    sends = []

    def to_tubes(which, source, target, n):
        arriving = []
        for i in range(plan.F):
            peer = lax.rem(frame + i, plan.F)
            clip_set, positions = tubes(n, peer)
            src = source.at[:, clip_set, positions]
            dst = target.at[n, pl.ds(frame * plan.fd, plan.fd)]
            recv = refs.a2a_recv.at[which, n, i]
            if i == 0:
                copy = pltpu.make_async_copy(src, dst, recv)
                copy.start()
                arriving.append(copy.wait)
            else:
                copy = pltpu.make_async_remote_copy(
                    src_ref=src,
                    dst_ref=dst,
                    send_sem=refs.a2a_send.at[which, n, i],
                    recv_sem=recv,
                    device_id=(me[CLIP], peer),
                    device_id_type=MESH,
                )
                copy.start()
                sends.append(copy.wait_send)
                arriving.append(copy.wait_recv)
        return arriving

    def to_frames(which, source, target, n):
        arriving = []
        for i in range(plan.F):
            peer = lax.rem(frame + i, plan.F)
            clip_set, positions = tubes(n, frame)
            src = source.at[n, pl.ds(peer * plan.fd, plan.fd)]
            dst = target.at[:, clip_set, positions]
            recv = refs.a2a_recv.at[which, n, i]
            if i == 0:
                copy = pltpu.make_async_copy(src, dst, recv)
                copy.start()
                arriving.append((lambda: None, copy.wait))
            else:
                copy = pltpu.make_async_remote_copy(
                    src_ref=src,
                    dst_ref=dst,
                    send_sem=refs.a2a_send.at[which, n, i],
                    recv_sem=recv,
                    device_id=(me[CLIP], peer),
                    device_id_type=MESH,
                )
                copy.start()
                arriving.append((copy.wait_recv, copy.wait_send))
        return arriving

    def wait_all(waits):
        for wait in waits:
            wait()

    x_arrives = [to_tubes(0, refs.stream, xin, 0)]
    g_arrives = []

    loads = []
    for i, (src, dst) in enumerate(zip(refs.from_hbm, (wqkv, wout, wup, wdown))):
        load = pltpu.make_async_copy(src, dst, refs.load_sems.at[i])
        load.start()
        loads.append(load)

    raw = n2
    grad_loads = []
    for r in range(plan.rows):
        grad_load = pltpu.make_async_copy(
            refs.grad.at[r // plan.cd, r % plan.cd],
            raw.at[pl.ds(r * plan.spatial, plan.spatial)],
            refs.grad_sems.at[r],
        )
        grad_load.start()
        grad_loads.append(grad_load.wait)
    wait_all(grad_loads)
    places = (plan.spatial, plan.spatial)
    diagonal = lax.broadcasted_iota(jnp.int32, places, 0) == lax.broadcasted_iota(
        jnp.int32, places, 1
    )
    for r in range(plan.rows):
        kept = refs.mask[pl.ds(r, 1), :] == 1
        keep = jnp.where(diagonal & kept, 1.0, 0.0).astype(BF16)
        rows = dot_nn(keep, raw[pl.ds(r * plan.spatial, plan.spatial), :])
        refs.gsrc[r // plan.cd, r % plan.cd] = rows.astype(BF16)
    for n in range(1, S):
        wait_all(sends)
        sends.clear()
        x_arrives.append(to_tubes(0, refs.stream, xin, n))

    scatters = [
        Scatter(
            plan,
            me,
            part,
            refs.groups[group],
            refs.group_slots[group],
            refs.res.at[group],
            refs.rs_send,
            refs.rs_recv,
        )
        for part, (group, *_) in enumerate(plan.parts)
    ]

    def start(group):
        for part, scatter in enumerate(scatters):
            if plan.parts[part][0] == group:
                scatter.start()

    def tick(name):
        for part in DUE.get(name, ()):
            if part < len(scatters) and scatters[part].copies and not scatters[part].done():
                scatters[part].advance()

    def pieces(name, count, total, body):
        for i in range(count):
            lax.fori_loop(total * i // count, total * (i + 1) // count, body, 0)
            tick(name + str(i))

    def seq_rows(ref, s, start, size):
        frames = size // plan.pos
        block = ref[s, pl.ds(start // plan.pos, frames)]
        return block.reshape(size, D)

    sums[...] = jnp.zeros_like(sums)

    def tally(i, value):
        sums[i] += fold8(value)

    lanes = lax.broadcasted_iota(jnp.int32, (1, 128), 1)
    head_masks = [(lanes < 64).astype(BF16), (lanes >= 64).astype(BF16)]
    scale = 1.0 / math.sqrt(D // HEADS)

    def head_columns(pair):
        at = pair * 128
        return tuple(ds(first + at, 128) for first in (0, 0, D, 2 * D))

    for s in range(S):
        wait_all(x_arrives[s])
        if s == S - 1:
            g_arrives += [to_tubes(1, refs.gsrc, gin, n) for n in range(S)]

        def first_norm(i, _):
            x = seq_rows(xin, s, i * ROW_BLOCK, ROW_BLOCK).astype(F32)
            unit, _ = unit_norm(x)
            tally(8, x * x)
            n1[ds(s * L + i * ROW_BLOCK, ROW_BLOCK), :] = (unit * ln1_gain[...] + ln1_bias[...]).astype(BF16)
            return 0

        lax.fori_loop(0, L // ROW_BLOCK, first_norm, 0)
        if s == 0:
            loads[0].wait()
        tokens = pl.ds(s * L, L)
        for third in range(3):
            columns = pl.ds(third * D, D)
            out = dot_nn(n1[tokens, :], wqkv[:, columns])
            if third != 1:
                out = out + b_qv[:, pl.ds(third // 2 * D, D)]
            if third == 0:
                out = out * scale
            qkv[tokens, columns] = out.astype(BF16)

        def attend(pair, _):
            columns, q_at, k_at, v_at = head_columns(pair)
            q, k, v = qkv[tokens, q_at], qkv[tokens, k_at], qkv[tokens, v_at]
            out = jnp.zeros((L, 128), F32)
            for e in range(2):
                scores = dot_nt(q * head_masks[e], k)
                power = jnp.exp(scores - jnp.max(scores, axis=-1, keepdims=True))
                share = 1.0 / jnp.sum(power, axis=-1, keepdims=True)
                weight = (power * share).astype(BF16)
                prob[s * HEADS + pair * 2 + e] = weight
                out = out + dot_nn(weight, v * head_masks[e])
            mixed[tokens, columns] = out.astype(BF16)
            return 0

        lax.fori_loop(0, HEADS // 2, attend, 0)

    loads[1].wait()

    mid[...] = dot_nn(mixed[...], wout[...]) + b_out[...]
    for s in range(S):

        def second_norm(i, _):
            rows = ds(s * L + i * ROW_BLOCK, ROW_BLOCK)
            branch = mid[rows, :]
            middle = seq_rows(xin, s, i * ROW_BLOCK, ROW_BLOCK).astype(F32) + branch
            mid[rows, :] = middle
            tally(9, middle * middle)
            tally(11, branch * branch)
            unit, _ = unit_norm(middle)
            n2[rows, :] = (unit * ln2_gain[...] + ln2_bias[...]).astype(BF16)
            return 0

        lax.fori_loop(0, L // ROW_BLOCK, second_norm, 0)

    loads[2].wait()

    def up(i, _):
        columns = ds(i * D, D)
        hidden = dot_nn(n2[...], wup[:, columns]) + b_up[:, columns]
        active, steep = gelu_and_slope(hidden)
        act[:, columns] = active.astype(BF16)
        slope[:, columns] = steep.astype(BF16)
        return 0

    lax.fori_loop(0, nj, up, 0)
    loads[3].wait()
    out_arrives = []
    for s in range(S):
        tokens = pl.ds(s * L, L)
        branch = dot_nn(act[tokens, :], wdown[...]) + b_down[...]
        result = branch + mid[tokens, :]
        tally(10, result * result)
        tally(12, branch * branch)
        obuf[s] = result.astype(BF16).reshape(FRAMES, plan.pos, D)
        out_arrives += to_frames(2, obuf, refs.out_h, s)

    for s in range(S):
        wait_all(g_arrives[s])
    wait_all(sends)
    sends.clear()
    def put(group, chunk, frame_block, block):
        for of_group, order, first, height in plan.parts:
            if of_group == group:
                at = plan.place(order, chunk, frame_block)
                rows = pl.multiple_of(first * plan.blocks + at * height, 16)
                piece = block[first : first + height]
                refs.groups[group][pl.ds(rows, height), :] = piece.astype(BF16)

    def grad_down(i, _):
        out = dot_tn(act[:, ds(i * D, D)], gin[...].reshape(T, D))
        share = FF // plan.F
        for n in range(D // plan.R):
            place = n * plan.R
            frames = D // share
            chunk = place % share // plan.R
            put(0, chunk, i * frames + place // share, out[place : place + plan.R])
        return 0

    pieces("GD", nj, nj, grad_down)
    start(0)

    def through_gelu(i, _):
        columns = ds(i * D, D)
        d_active = dot_nt(gin[...].reshape(T, D), wdown[columns, :])
        d_hidden = (d_active * slope[:, columns].astype(F32)).astype(BF16)
        slope[:, columns] = d_hidden
        sums[13 + i] += fold8(d_hidden.astype(F32))
        return 0

    pieces("TG", nj, nj, through_gelu)

    def grad_columns(group, chunk, lhs, rhs):
        out = dot_tn(lhs, rhs)
        for f in range(plan.F):
            put(group, chunk, f, out[f * plan.R : (f + 1) * plan.R])

    def grad_up(c, _):
        grad_columns(1, c, n2[...], slope[:, ds(c * D, D)])
        return 0

    pieces("GU", plan.C, plan.C, grad_up)
    start(1)
    acc[...] = dot_nt(slope[...], wup[...])
    tick("DT")

    for s in range(S):

        def second_norm_back(i, _):
            rows = ds(s * L + i * ROW_BLOCK, ROW_BLOCK)
            up_grad = acc[rows, :]
            unit, inverse = unit_norm(mid[rows, :])
            g = seq_rows(gin, s, i * ROW_BLOCK, ROW_BLOCK).astype(F32)
            d_middle = g + norm_pull(up_grad * ln2_gain[...], unit, inverse)
            dmid[rows, :] = d_middle
            low = d_middle.astype(BF16)
            dbranch[rows, :] = low
            tally(4, low.astype(F32))
            tally(5, up_grad * unit)
            tally(6, up_grad)
            tally(7, g)
            return 0

        lax.fori_loop(0, L // ROW_BLOCK, second_norm_back, 0)
        tick("LB" + str(s))

    grad_columns(2, plan.C - 1, mixed[...], dbranch[...])
    tick("DO")
    dmixed[...] = dot_nt(dbranch[...], wout[...]).astype(BF16)
    tick("DM")

    for s in range(S):
        tokens = pl.ds(s * L, L)

        def attend_back(pair, _):
            columns, q_at, k_at, v_at = head_columns(pair)
            q, k, v = qkv[tokens, q_at], qkv[tokens, k_at], qkv[tokens, v_at]
            d_out = dmixed[tokens, columns]
            zero = jnp.zeros((L, 128), F32)
            d_q, d_k, d_v = zero, zero, zero
            for e in range(2):
                weight = prob[s * HEADS + pair * 2 + e]
                own = d_out * head_masks[e]
                d_weight = dot_nt(own, v)
                d_v = d_v + dot_tn(weight, own)
                wide_weight = weight.astype(F32)
                centre = jnp.sum(wide_weight * d_weight, axis=-1, keepdims=True)
                d_score = (wide_weight * (d_weight - centre)).astype(BF16)
                d_q = d_q + dot_nn(d_score, k * head_masks[e])
                d_k = d_k + dot_tn(d_score, q * head_masks[e])
            qkv[tokens, q_at] = (d_q * scale).astype(BF16)
            qkv[tokens, k_at] = d_k.astype(BF16)
            qkv[tokens, v_at] = d_v.astype(BF16)
            return 0

        pieces("AB" + str(s), 2, HEADS // 2, attend_back)

    def grad_qkv(c, _):
        grad_columns(2, c, n1[...], qkv[:, ds(c * D, D)])
        return 0

    pieces("GQ", plan.C - 1, plan.C - 1, grad_qkv)
    start(2)
    acc[...] = dot_nt(qkv[...], wqkv[...])
    tick("D1")
    for recv, send in out_arrives:
        send()
    in_arrives = []
    for s in range(S):

        def first_norm_back(i, _):
            rows = ds(s * L + i * ROW_BLOCK, ROW_BLOCK)
            up_grad = acc[rows, :]
            x = seq_rows(xin, s, i * ROW_BLOCK, ROW_BLOCK).astype(F32)
            unit, inverse = unit_norm(x)
            total = dmid[rows, :] + norm_pull(up_grad * ln1_gain[...], unit, inverse)
            frames = ROW_BLOCK // plan.pos
            igbuf[s, pl.ds(i * frames, frames)] = total.astype(BF16).reshape(frames, plan.pos, D)
            tally(0, up_grad * unit)
            tally(1, up_grad)
            tally(2, qkv[rows, pl.ds(0, D)].astype(F32))
            tally(3, qkv[rows, pl.ds(2 * D, D)].astype(F32))
            return 0

        lax.fori_loop(0, L // ROW_BLOCK, first_norm_back, 0)
        in_arrives += to_frames(3, igbuf, refs.ig_h, s)
        tick("L1" + str(s))

    vbuf, vrecv = refs.vbuf, refs.vrecv
    count = sums.shape[0]
    for i in range(count):
        vbuf[0, pl.ds(i, 1), :] = jnp.sum(sums[i], axis=0, keepdims=True)
    hops = plan.steps("xyz")
    small = []
    for i, (axis, bit) in enumerate(hops):
        flipped = me[axis] + bit * (1 - 2 * ((me[axis] // bit) % 2))
        to = {**me, axis: flipped}
        copy = pltpu.make_async_remote_copy(
            src_ref=vbuf.at[i],
            dst_ref=vrecv.at[i],
            send_sem=refs.v_send.at[i],
            recv_sem=refs.v_recv.at[i],
            device_id=(to[CLIP], to[FRAME]),
            device_id_type=MESH,
        )
        copy.start()
        small.append(copy)
        tick("V" + str(i))
        copy.wait_recv()
        vbuf[i + 1] = vbuf[i] + vrecv[i]
    refs.vec[...] = vbuf[len(hops)]
    for copy in small:
        copy.wait_send()
    tick("END")
    while not all(scatter.done() for scatter in scatters):
        for scatter in scatters:
            if not scatter.done():
                scatter.advance()
    for scatter in scatters:
        scatter.finish()
    for recv, send in out_arrives:
        recv()
    for recv, send in in_arrives:
        send()
        recv()
    wait_all(sends)


def fused(plan, stream, out_grad, token_mask, weights, small):
    D, T, S, L, FF = plan.D, plan.T, plan.S, plan.L, plan.FF
    n_steps = len(plan.steps("xyz"))
    n_parts = len(plan.parts)
    n_hops = n_steps + len(plan.gather_steps())
    n_vec = 13 + plan.nj
    vec_rows = -(-n_vec // 8) * 8
    vmem = lambda shape, kind=BF16: pltpu.VMEM(shape, kind)
    token_shape = (plan.fd, plan.cd, plan.spatial, D)
    scratch = dict(
        wqkv=vmem((D, 3 * D)),
        wout=vmem((D, D)),
        wup=vmem((D, FF)),
        wdown=vmem((FF, D)),
        xin=vmem((S, FRAMES, plan.pos, D)),
        gin=vmem((S, FRAMES, plan.pos, D)),
        n1=vmem((T, D)),
        qkv=vmem((T, 3 * D)),
        prob=vmem((S * HEADS, L, L)),
        mixed=vmem((T, D)),
        mid=vmem((T, D), F32),
        n2=vmem((T, D)),
        act=vmem((T, FF)),
        slope=vmem((T, FF)),
        obuf=vmem((S, FRAMES, plan.pos, D)),
        acc=vmem((T, D), F32),
        dmid=vmem((T, D), F32),
        sums=vmem((n_vec, 8, D), F32),
        g_down=vmem((plan.whole, D)),
        g_up=vmem((plan.whole, D)),
        vbuf=vmem((n_steps + 1, vec_rows, D), F32),
        vrecv=vmem((n_steps, vec_rows, D), F32),
        small_rows=[vmem((1, item.size), F32) for item in small],
        gsrc=vmem(token_shape),
        load_sems=pltpu.SemaphoreType.DMA((4,)),
        grad_sems=pltpu.SemaphoreType.DMA((plan.rows,)),
        a2a_send=pltpu.SemaphoreType.DMA((4, S, plan.F)),
        a2a_recv=pltpu.SemaphoreType.DMA((4, S, plan.F)),
        rs_send=pltpu.SemaphoreType.DMA((n_parts, n_hops)),
        rs_recv=pltpu.SemaphoreType.DMA((n_parts, n_hops)),
        v_send=pltpu.SemaphoreType.DMA((n_steps,)),
        v_recv=pltpu.SemaphoreType.DMA((n_steps,)),
        slots=[
            vmem((3, plan.whole >> (i + 1), D)) for i in range(n_steps)
        ],
    )

    def kernel(stream, grad, wqkv, wout, wup, wdown, mask, *rest):
        count = len(small)
        refs = SimpleNamespace(
            stream=stream,
            grad=grad,
            from_hbm=(wqkv, wout, wup, wdown),
            mask=mask,
            small=rest[:count],
        )
        refs.out_h, refs.ig_h, refs.res, refs.vec = rest[count : count + 4]
        vars(refs).update(rest[count + 4])
        refs.groups = (refs.g_down, refs.g_up, refs.wdown)
        refs.group_slots = [[slot.at[group] for slot in refs.slots] for group in range(3)]
        layer_kernel(plan, refs)

    hbm = pl.BlockSpec(memory_space=pl.ANY)
    in_vmem = pl.BlockSpec(memory_space=pltpu.VMEM)
    return pl.pallas_call(
        kernel,
        out_shape=(
            jax.ShapeDtypeStruct(token_shape, BF16),
            jax.ShapeDtypeStruct(token_shape, BF16),
            jax.ShapeDtypeStruct((3, plan.C * plan.R, D), BF16),
            jax.ShapeDtypeStruct((vec_rows, D), F32),
        ),
        in_specs=[hbm] * 6 + [in_vmem] * (1 + len(small)),
        out_specs=(hbm, hbm, in_vmem, in_vmem),
        scratch_shapes=(scratch,),
        compiler_params=pltpu.CompilerParams(
            collective_id=0, has_side_effects=True, vmem_limit_bytes=VMEM_LIMIT
        ),
        name="tube_layer",
    )(
        stream.reshape(token_shape),
        out_grad.reshape(token_shape),
        *weights,
        token_mask,
        *small,
    )


VMEM_LIMIT = 64 * 1024 * 1024 - 512 * 1024


def finish_kernel(plan, out_s, ig_s, res_h, vec_h, out_d, ig_d, *refs):
    C, R, D = plan.C, plan.R, plan.D
    qkv_d, up_d, proj_d, down_d = refs[:4]
    vectors, statistics = refs[4:12], refs[12]
    qkv_v, up_v, proj_v, down_v, res, vec, out_v, ig_v, sems = refs[13:]
    moves = [(res_h.at[group], res.at[group]) for group in range(3)]
    moves += [(vec_h, vec), (out_s, out_v), (ig_s, ig_v)]
    copies = [pltpu.make_async_copy(*move, sems.at[i]) for i, move in enumerate(moves)]
    for copy in copies:
        copy.start()

    def write(value, target):
        copy = pltpu.make_async_copy(value, target, sems.at[len(copies)])
        copy.start()
        copies.append(copy)

    def each_piece(group):
        for of_group, _, first, height in plan.parts:
            if of_group == group:
                for chunk in range(C):
                    block = res[group, pl.ds(first * C + chunk * height, height), :]
                    yield chunk, first, height, block.astype(F32)

    copies[0].wait()
    for chunk, first, height, block in each_piece(0):
        down_v[pl.ds(chunk * R + first, height), :] = block
    write(down_v, down_d)
    copies[1].wait()
    for chunk, first, height, block in each_piece(1):
        up_v[pl.ds(first, height), pl.ds(chunk * D, D)] = block
    write(up_v, up_d)
    copies[2].wait()
    for chunk, first, height, block in each_piece(2):
        if chunk < C - 1:
            qkv_v[pl.ds(first, height), pl.ds(chunk * D, D)] = block
        else:
            proj_v[pl.ds(first, height), :] = block
    write(qkv_v, qkv_d)
    write(proj_v, proj_d)
    copies[4].wait()
    write(out_v, out_d)
    copies[5].wait()
    write(ig_v, ig_d)

    copies[3].wait()
    frame = lax.axis_index(FRAME)
    counts = (1, 1, 2, 1, 1, 1, plan.nj, 1)
    firsts = (0, 1, 2, 4, 5, 6, 13, 7)
    for target, count, first in zip(vectors, counts, firsts):
        share = count * D // plan.F
        per_row = plan.F // count
        row = vec[pl.ds(first + frame // per_row, 1), :]
        turned = pltpu.roll(row, lax.rem(D - (frame % per_row) * share, D), 1)
        target[...] = turned[:, :share].reshape(-1)
    squares = jnp.sum(vec[pl.ds(8, 8), :], axis=-1, keepdims=True)
    entries = plan.T * D * C * plan.F
    roots = jnp.sqrt(squares / entries)
    lanes = lax.broadcasted_iota(jnp.int32, (8, 8), 1)
    rows = lax.broadcasted_iota(jnp.int32, (8, 8), 0)
    across = jnp.sum(jnp.where(lanes == rows, roots, 0.0), axis=0, keepdims=True)
    statistics[...] = across[:, :5].reshape(-1)
    for copy in copies[6:]:
        copy.wait()


def finish(plan, output, input_grad, res, vec):
    D, F, C, R = plan.D, plan.F, plan.C, plan.R
    shapes = [(R, 3 * D), (R, C * D), (R, D), (C * R, D)]
    vectors = [(count * D // F,) for count in (1, 1, 2, 1, 1, 1, plan.nj, 1)]
    hbm = pl.BlockSpec(memory_space=pltpu.HBM)
    in_vmem = pl.BlockSpec(memory_space=pltpu.VMEM)
    like = lambda item: jax.ShapeDtypeStruct(item.shape, item.dtype)
    return pl.pallas_call(
        functools.partial(finish_kernel, plan),
        out_shape=tuple(
            [like(output), like(input_grad)]
            + [jax.ShapeDtypeStruct(shape, F32) for shape in shapes + vectors + [(5,)]]
        ),
        in_specs=[hbm] * 4,
        out_specs=tuple([hbm] * 6 + [in_vmem] * 9),
        scratch_shapes=[pltpu.VMEM(shape, F32) for shape in shapes]
        + [pltpu.VMEM(res.shape, BF16), pltpu.VMEM(vec.shape, F32)]
        + [pltpu.VMEM(output.shape, BF16)] * 2
        + [pltpu.SemaphoreType.DMA((12,))],
        compiler_params=pltpu.CompilerParams(vmem_limit_bytes=VMEM_LIMIT),
        name="tube_layer_results",
    )(output, input_grad, res, vec)


def with_kernel(
    plan,
    stream,
    out_grad,
    token_mask,
    ln1_gain,
    ln1_bias,
    w_qkv,
    b_qv,
    w_out,
    b_out,
    ln2_gain,
    ln2_bias,
    w_up,
    b_up,
    w_down,
    b_down,
):
    small = (ln1_gain, ln1_bias, b_qv, b_out, ln2_gain, ln2_bias, b_up, b_down)
    parts = fused(plan, stream, out_grad, token_mask, (w_qkv, w_out, w_up, w_down), small)
    output, input_grad, g_qkv, g_up, g_out, g_down, *vectors, statistics = finish(plan, *parts)
    return (
        output.reshape(stream.shape),
        input_grad.reshape(stream.shape),
        vectors[0],
        vectors[1],
        g_qkv,
        vectors[2],
        g_out,
        vectors[3],
        vectors[4],
        vectors[5],
        g_up,
        vectors[6],
        g_down,
        vectors[7],
        statistics,
    )


def layer_norm(inputs, norm_gain, norm_shift):
    center = jnp.mean(inputs, axis=-1, keepdims=True)
    shifted = inputs - center
    spread = jnp.mean(shifted * shifted, axis=-1, keepdims=True)
    inverse = lax.rsqrt(spread + EPS)
    unit = shifted * inverse
    return (unit * norm_gain + norm_shift, unit, inverse)


def norm_backward(upstream, unit, inverse, norm_gain):
    scaled = upstream * norm_gain
    first = jnp.mean(scaled, axis=-1, keepdims=True)
    second = jnp.mean(scaled * unit, axis=-1, keepdims=True)
    return inverse * (scaled - first - unit * second)


def gelu_slope(hidden_state):
    cumulative = 0.5 * (1.0 + lax.erf(hidden_state * (1.0 / math.sqrt(2.0))))
    density = jnp.exp(-0.5 * hidden_state * hidden_state) * (1.0 / math.sqrt(2.0 * math.pi))
    return cumulative + hidden_state * density


def with_collectives(
    stream,
    out_grad,
    token_mask,
    ln1_gain,
    ln1_bias,
    w_qkv,
    b_qv,
    w_out,
    b_out,
    ln2_gain,
    ln2_bias,
    w_up,
    b_up,
    w_down,
    b_down,
):
    frame_count = lax.axis_size(FRAME)
    clip_count = lax.axis_size(CLIP)
    device_count = clip_count * frame_count
    frame_split = min(FRAMES, frame_count)
    clip_split = frame_count // frame_split
    frames_dev = FRAMES // frame_split
    tubes_dev = TUBES // frame_split
    row_count, spatial, width = stream.shape
    clips_dev = row_count // frames_dev
    clip_sets = clips_dev // clip_split
    tube_pos = spatial // TUBES
    length = FRAMES * tube_pos
    head_dim = width // HEADS
    scale = 1.0 / math.sqrt(head_dim)

    def leaving(tensor):
        return tensor.reshape(frames_dev, clip_sets, frame_count, tubes_dev * tube_pos, width)

    def arranged(tensor):
        tensor = tensor.reshape(clip_split, FRAMES, clip_sets, tubes_dev, tube_pos, width)
        tensor = jnp.transpose(tensor, (0, 2, 3, 1, 4, 5))
        return tensor.reshape(-1, width)

    def restored(tensor):
        tensor = tensor.reshape(clip_split, clip_sets, tubes_dev, FRAMES, tube_pos, width)
        tensor = jnp.transpose(tensor, (0, 3, 1, 2, 4, 5))
        return tensor.reshape(frame_count * frames_dev, clip_sets, 1, tubes_dev * tube_pos, width)

    masked = jnp.where(token_mask[:, :, None] == 1, out_grad, jnp.zeros((), jnp.bfloat16))
    arrived = (
        lax.all_to_all(leaving(stream), FRAME, split_axis=2, concat_axis=0, tiled=True),
        lax.all_to_all(leaving(masked), FRAME, split_axis=2, concat_axis=0, tiled=True),
    )
    inputs = arranged(arrived[0]).astype(jnp.float32)
    grad_y = arranged(arrived[1])
    seq_count = inputs.shape[0] // length

    def split_heads(tensor):
        return tensor.reshape(seq_count, length, HEADS, head_dim)

    def attention_scores(queries, key_part):
        return (
            jnp.einsum("slhe,smhe->shlm", queries, key_part, preferred_element_type=jnp.float32)
            * scale
        )

    first_normed_input, unit_one, inverse_one = layer_norm(inputs, ln1_gain, ln1_bias)
    first_normed_input = first_normed_input.astype(jnp.bfloat16)
    third_bias_term = jnp.concatenate(
        [b_qv[:width], jnp.zeros((width,), jnp.float32), b_qv[width:]]
    )
    query_key_value = (
        jnp.dot(first_normed_input, w_qkv, preferred_element_type=jnp.float32) + third_bias_term
    ).astype(jnp.bfloat16)
    queries = split_heads(query_key_value[:, :width])
    key_part = split_heads(query_key_value[:, width : 2 * width])
    values = split_heads(query_key_value[:, 2 * width :])
    scores = attention_scores(queries, key_part)
    largest = jnp.max(scores, axis=-1, keepdims=True)
    logsum = largest + jnp.log(jnp.sum(jnp.exp(scores - largest), axis=-1, keepdims=True))
    attend_low = jnp.exp(scores - logsum).astype(jnp.bfloat16)
    mixed_heads = jnp.einsum(
        "shlm,smhe->slhe", attend_low, values, preferred_element_type=jnp.float32
    )
    mixed_heads = mixed_heads.reshape(-1, width).astype(jnp.bfloat16)
    attention_branch = jnp.dot(mixed_heads, w_out, preferred_element_type=jnp.float32) + b_out
    middle = inputs + attention_branch
    second_normed_input, unit_two, inverse_two = layer_norm(middle, ln2_gain, ln2_bias)
    second_normed_input = second_normed_input.astype(jnp.bfloat16)
    hidden_state = jnp.dot(second_normed_input, w_up, preferred_element_type=jnp.float32) + b_up
    activated_hidden = jax.nn.gelu(hidden_state, approximate=False).astype(jnp.bfloat16)
    feedforward_branch = (
        jnp.dot(activated_hidden, w_down, preferred_element_type=jnp.float32) + b_down
    )
    result = middle + feedforward_branch
    squares = jnp.stack(
        [
            jnp.sum(inputs * inputs),
            jnp.sum(middle * middle),
            jnp.sum(result * result),
            jnp.sum(attention_branch * attention_branch),
            jnp.sum(feedforward_branch * feedforward_branch),
        ]
    )
    totals = lax.psum(squares, (CLIP, FRAME))
    statistics = jnp.sqrt(totals / (row_count * spatial * width * device_count))
    grad_w_down = jnp.einsum(
        "tf,td->fd", activated_hidden, grad_y, preferred_element_type=jnp.float32
    )
    grad_b_down = jnp.sum(grad_y.astype(jnp.float32), axis=0)
    d_active = jnp.einsum("td,fd->tf", grad_y, w_down, preferred_element_type=jnp.float32)
    d_hidden = (d_active * gelu_slope(hidden_state)).astype(jnp.bfloat16)
    grad_w_up = jnp.einsum(
        "td,tf->df", second_normed_input, d_hidden, preferred_element_type=jnp.float32
    )
    grad_b_up = jnp.sum(d_hidden.astype(jnp.float32), axis=0)
    d_two = jnp.einsum("tf,df->td", d_hidden, w_up, preferred_element_type=jnp.float32)
    grad_ln2_gain = jnp.sum(d_two * unit_two, axis=0)
    grad_ln2_bias = jnp.sum(d_two, axis=0)
    d_middle = grad_y.astype(jnp.float32) + norm_backward(d_two, unit_two, inverse_two, ln2_gain)
    d_branch = d_middle.astype(jnp.bfloat16)
    grad_w_out = jnp.einsum("td,te->de", mixed_heads, d_branch, preferred_element_type=jnp.float32)
    grad_b_out = jnp.sum(d_branch.astype(jnp.float32), axis=0)
    d_mixed = jnp.einsum("te,de->td", d_branch, w_out, preferred_element_type=jnp.float32)
    d_mixed = split_heads(d_mixed.astype(jnp.bfloat16))
    again = attention_scores(queries, key_part)
    attend = jnp.exp(again - logsum)
    attend_again = attend.astype(jnp.bfloat16)
    d_attend = jnp.einsum("slhe,smhe->shlm", d_mixed, values, preferred_element_type=jnp.float32)
    d_values = jnp.einsum(
        "shlm,slhe->smhe", attend_again, d_mixed, preferred_element_type=jnp.float32
    )
    centre_term = jnp.sum(attend * d_attend, axis=-1, keepdims=True)
    d_scores = (attend * (d_attend - centre_term)).astype(jnp.bfloat16)
    d_queries = (
        jnp.einsum("shlm,smhe->slhe", d_scores, key_part, preferred_element_type=jnp.float32)
        * scale
    )
    d_keys = (
        jnp.einsum("shlm,slhe->smhe", d_scores, queries, preferred_element_type=jnp.float32) * scale
    )
    d_qkv = jnp.concatenate(
        [d_queries.reshape(-1, width), d_keys.reshape(-1, width), d_values.reshape(-1, width)],
        axis=1,
    ).astype(jnp.bfloat16)
    grad_w_qkv = jnp.einsum(
        "td,te->de", first_normed_input, d_qkv, preferred_element_type=jnp.float32
    )
    bias_sums = jnp.sum(d_qkv.astype(jnp.float32), axis=0)
    grad_b_qv = jnp.concatenate([bias_sums[:width], bias_sums[2 * width :]])
    d_one = jnp.einsum("te,de->td", d_qkv, w_qkv, preferred_element_type=jnp.float32)
    grad_ln1_gain = jnp.sum(d_one * unit_one, axis=0)
    grad_ln1_bias = jnp.sum(d_one, axis=0)
    d_inputs = d_middle + norm_backward(d_one, unit_one, inverse_one, ln1_gain)
    departed = (
        lax.all_to_all(
            restored(result.astype(jnp.bfloat16)), FRAME, split_axis=0, concat_axis=2, tiled=True
        ),
        lax.all_to_all(
            restored(d_inputs.astype(jnp.bfloat16)),
            FRAME,
            split_axis=0,
            concat_axis=2,
            tiled=True,
        ),
    )
    output = departed[0].reshape(row_count, spatial, width)
    input_grad = departed[1].reshape(row_count, spatial, width)
    gradients = [
        grad_ln1_gain,
        grad_ln1_bias,
        grad_w_qkv,
        grad_b_qv,
        grad_w_out,
        grad_b_out,
        grad_ln2_gain,
        grad_ln2_bias,
        grad_w_up,
        grad_b_up,
        grad_w_down,
        grad_b_down,
    ]
    grouped = jnp.concatenate([item.reshape(frame_count, -1) for item in gradients], axis=1)
    extent_all = grouped.shape[1]
    padding = -extent_all % clip_count
    grouped = jnp.concatenate([grouped, jnp.zeros((frame_count, padding), jnp.float32)], axis=1)
    own_rows = lax.psum_scatter(
        grouped.astype(jnp.bfloat16), FRAME, scatter_dimension=0, tiled=True
    ).astype(jnp.float32)
    summed = lax.psum(own_rows, CLIP).reshape(-1)
    finished = []
    offset = 0
    for item in gradients:
        extent = item.size // frame_count
        local_shape = (item.shape[0] // frame_count,) + item.shape[1:]
        finished.append(summed[offset : offset + extent].reshape(local_shape))
        offset = offset + extent
    return (
        output,
        input_grad,
        finished[0],
        finished[1],
        finished[2],
        finished[3],
        finished[4],
        finished[5],
        finished[6],
        finished[7],
        finished[8],
        finished[9],
        finished[10],
        finished[11],
        statistics,
    )


def solution(mesh):
    clips, frames = mesh.shape[CLIP], mesh.shape[FRAME]

    def on_device(stream, *rest):
        ff = rest[-4].shape[1]
        plan = Plan(clips, frames, stream.shape, ff)
        if plan.fits:
            return with_kernel(plan, stream, *rest)
        return with_collectives(stream, *rest)

    tokens = P((CLIP, FRAME), None, None)
    in_specs = (tokens, tokens, P((CLIP, FRAME), None)) + (P(),) * 12
    rows, vector = P(FRAME, None), P(FRAME)
    out_specs = (
        tokens,
        tokens,
        vector,
        vector,
        rows,
        vector,
        rows,
        vector,
        vector,
        vector,
        rows,
        vector,
        rows,
        vector,
        P(),
    )
    return jax.shard_map(
        on_device, mesh=mesh, in_specs=in_specs, out_specs=out_specs, check_vma=False
    )
```

```python
import functools
import math
from types import SimpleNamespace

import jax
import jax.numpy as jnp
from jax import lax
from jax.experimental import pallas as pl
from jax.experimental.pallas import tpu as pltpu
from jax.sharding import PartitionSpec as P

HEADS = 12
FRAMES = 16
TUBES = 16
EPS = 1e-05

F32 = jnp.float32
BF16 = jnp.bfloat16
MESH = pl.DeviceIdType.MESH
ROW_BLOCK = 64
CLIP = "clip"
FRAME = "frame"


SIXTHS = 6
SHARES = (
    (("zyx", 2), ("xzy", 1), ("yzx", 1), ("yxz", 2),),
    (("xzy", 1), ("xyz", 3), ("yxz", 2),),
    (("xzy", 2), ("xyz", 2), ("yxz", 2),),
)
DUE = dict(
    GU0=(0, 1),
    GU1=(2, 3),
    DT=(4,),
    LB1=(5, 6),
    DO=(1,),
    AB00=(2,),
    AB01=(0,),
    AB10=(4,),
    AB11=(1,),
    GQ0=(2, 3),
    V0=(7, 4, 8, 5, 9, 0, 6, 1),
    V1=(3, 2, 7, 5, 3, 8, 7, 6, 9, 4, 5, 0, 2, 3, 1),
    V2=(6, 9, 7, 8, 4, 0, 2, 3, 2, 1, 5, 4, 7, 3),
    V3=(9, 1, 0, 4, 6, 0, 8, 5, 7, 5, 6, 7),
    V4=(9, 6, 8, 9, 8, 9, 8),
)


def dot_nn(lhs, rhs):
    return lax.dot_general(lhs, rhs, (((1,), (0,)), ((), ())), preferred_element_type=F32)


def dot_nt(lhs, rhs):
    return lax.dot_general(lhs, rhs, (((1,), (1,)), ((), ())), preferred_element_type=F32)


def dot_tn(lhs, rhs):
    return lax.dot_general(lhs, rhs, (((0,), (0,)), ((), ())), preferred_element_type=F32)


def unit_norm(rows):
    shifted = rows - jnp.mean(rows, axis=-1, keepdims=True)
    inverse = lax.rsqrt(jnp.mean(shifted * shifted, axis=-1, keepdims=True) + EPS)
    return shifted * inverse, inverse


def norm_pull(scaled, unit, inverse):
    first = jnp.mean(scaled, axis=-1, keepdims=True)
    second = jnp.mean(scaled * unit, axis=-1, keepdims=True)
    return inverse * (scaled - first - unit * second)


def gelu_and_slope(hidden):
    bell = jnp.exp(hidden * hidden * -0.5)
    t = 1.0 / (1.0 + jnp.abs(hidden) * (0.3275911 / math.sqrt(2.0)))
    poly = t * (
        0.5 * 0.254829592
        + t
        * (
            0.5 * -0.284496736
            + t * (0.5 * 1.421413741 + t * (0.5 * -1.453152027 + t * (0.5 * 1.061405429)))
        )
    )
    below = poly * bell
    cumulative = jnp.where(hidden >= 0.0, 1.0 - below, below)
    return hidden * cumulative, cumulative + hidden * bell * (1.0 / math.sqrt(2.0 * math.pi))


def fold8(rows):
    return jnp.sum(rows.reshape(rows.shape[0] // 8, 8, rows.shape[1]), axis=0)


def ds(start, size, unit=None):
    return pl.ds(pl.multiple_of(start, unit or size), size)


class Plan:
    def __init__(self, clips, frames, stream_shape, ff):
        self.C, self.F, self.FF = clips, frames, ff
        self.rows, self.spatial, self.D = stream_shape
        self.frame_split = min(FRAMES, frames)
        self.clip_split = frames // self.frame_split
        self.fd = FRAMES // self.frame_split
        self.td = TUBES // self.frame_split
        self.cd = self.rows // self.fd
        self.pos = self.spatial // TUBES
        self.L = FRAMES * self.pos
        self.S = self.cd * self.td
        self.T = self.S * self.L
        self.R = self.D // frames
        self.blocks = clips * frames
        self.whole = self.blocks * self.R
        self.parts = []
        for group, shares in enumerate(SHARES):
            first = 0
            for part, (order, share) in enumerate(shares):
                rows = self.R * share // SIXTHS
                self.parts.append((group, order, first, rows))
                first += rows
        self.nj = ff // self.D
        self.X = clips // 2
        self.Y = self.X if frames % self.X == 0 else 1
        powers = all(n & (n - 1) == 0 for n in (clips, frames, self.X, self.Y))
        self.fits = (
            self.clip_split == 1
            and clips >= 4
            and powers
            and frames % 2 == 0
            and self.R % (16 * SIXTHS) == 0
            and ff == clips * self.D
            and self.pos % 16 == 0
            and self.D % (ff // frames) == 0
        )

    def steps(self, order):
        bits = lambda n: [1 << i for i in range(n.bit_length() - 1)]
        along = dict(
            x=[(CLIP, 2 * b) for b in bits(self.X)],
            y=[(FRAME, b) for b in bits(self.Y)],
            z=[(FRAME, self.Y * b) for b in bits(self.F // self.Y)],
        )
        return [(CLIP, 1)] + along[order[0]] + along[order[1]] + along[order[2]]

    def peer_order(self):
        return range(self.F - 1, -1, -1)

    def gather_steps(self):
        return [(CLIP, 2 * (1 << i)) for i in range(self.X.bit_length() - 1)] + [(CLIP, 1)]

    def place(self, order, chunk, frame):
        clip = (chunk % self.X) * 2 + chunk // self.X
        where = 0
        for axis, bit in self.steps(order):
            where = where * 2 + ((clip if axis == CLIP else frame) // bit) % 2
        return where


class Scatter:
    def __init__(self, plan, me, part, held, slots, results, send_sems, recv_sems):
        group, order, first, self.height = plan.parts[part]
        self.plan, self.me = plan, me
        self.steps = plan.steps(order)
        self.gather = plan.gather_steps()
        rows = lambda count, per: pl.ds(first * per, count * per)
        self.held = held.at[rows(self.height, plan.blocks)]
        self.slots = [
            slot.at[rows(self.height, plan.blocks >> (i + 1))] for i, slot in enumerate(slots)
        ]
        self.result = results.at[rows(self.height, plan.C)]
        self.send_sems, self.recv_sems = send_sems.at[part], recv_sems.at[part]
        self.at = 0
        self.base = 0
        self.size = plan.blocks
        self.copies = []
        self.slot_of_me = (me[CLIP] % 2) * plan.X + me[CLIP] // 2

    def bit_of(self, axis, bit):
        return (self.me[axis] // bit) % 2

    def partner(self, axis, bit):
        flipped = self.me[axis] + bit * (1 - 2 * self.bit_of(axis, bit))
        return {**self.me, axis: flipped}

    def rows(self, base, size):
        return pl.ds(pl.multiple_of(base * self.height, self.height), size * self.height)

    def send(self, src, dst, axis, bit):
        to = self.partner(axis, bit)
        copy = pltpu.make_async_remote_copy(
            src_ref=src,
            dst_ref=dst,
            send_sem=self.send_sems.at[len(self.copies)],
            recv_sem=self.recv_sems.at[len(self.copies)],
            device_id=(to[CLIP], to[FRAME]),
            device_id_type=MESH,
        )
        copy.start()
        self.copies.append(copy)

    def start(self):
        if self.at < len(self.steps):
            axis, bit = self.steps[self.at]
            mine = self.bit_of(axis, bit)
            half = self.size // 2
            self.send(
                self.held.at[self.rows(self.base + (1 - mine) * half, half)],
                self.slots[self.at],
                axis,
                bit,
            )
            self.base = self.base + mine * half
            self.size = half
        elif self.at < len(self.steps) + len(self.gather):
            done = self.at - len(self.steps)
            axis, bit = self.gather[done]
            size = 1 << done
            region = self.rows((self.slot_of_me // size) * size, size)
            self.send(self.result.at[region], self.result.at[region], axis, bit)

    def advance(self):
        self.copies[self.at].wait_recv()
        if self.at < len(self.steps):
            slot = self.slots[self.at]
            last = self.at == len(self.steps) - 1
            target = self.result if last else self.held
            target_base = self.slot_of_me if last else self.base
            base, held = self.base, self.held

            def add(i, _):
                total = held[self.rows(base + i, 1)].astype(F32) + slot[self.rows(i, 1)].astype(F32)
                target[self.rows(target_base + i, 1)] = total.astype(BF16)
                return 0

            lax.fori_loop(0, self.size, add, 0)
        self.at += 1
        self.start()

    def done(self):
        return self.at == len(self.steps) + len(self.gather)

    def finish(self):
        assert self.done()
        for copy in self.copies:
            copy.wait_send()


def flipped_bits(index, bits):
    for b in range(bits.bit_length()):
        if bits >> b & 1:
            index = index + (1 << b) * (1 - 2 * ((index // (1 << b)) % 2))
    return index


def layer_kernel(plan, refs):
    D, T, S, L, FF, nj = plan.D, plan.T, plan.S, plan.L, plan.FF, plan.nj
    me = {CLIP: lax.axis_index(CLIP), FRAME: lax.axis_index(FRAME)}
    frame = me[FRAME]
    xin, gin, n1, qkv, prob, mixed = refs.xin, refs.gin, refs.n1, refs.qkv, refs.prob, refs.mixed
    mid, n2, act, slope, obuf, acc = refs.mid, refs.n2, refs.act, refs.slope, refs.obuf, refs.acc
    sums = refs.sums
    for source, target in zip(refs.small, refs.small_rows):
        target[...] = source[...].reshape(1, -1)
    ln1_gain, ln1_bias, b_qv, b_out, ln2_gain, ln2_bias, b_up, b_down = refs.small_rows
    wqkv, wout, wup, wdown = refs.wqkv, refs.wout, refs.wup, refs.wdown
    dbranch, dmixed, igbuf, dmid = n2, mixed, obuf, mid

    barrier = pltpu.get_barrier_semaphore()
    greeted = [(me[CLIP], lax.rem(frame + i, plan.F)) for i in range(1, plan.F)]
    for axis, bit in plan.gather_steps():
        flipped = me[axis] + bit * (1 - 2 * ((me[axis] // bit) % 2))
        greeted.append((flipped, frame))
    for peer in greeted:
        pl.semaphore_signal(barrier, inc=1, device_id=peer, device_id_type=MESH)
    pl.semaphore_wait(barrier, len(greeted))

    def tubes(n, device):
        clip_set, tube = n // plan.td, n % plan.td
        return clip_set, ds((device * plan.td + tube) * plan.pos, plan.pos)

    sends = []

    def to_tubes(which, source, target, n):
        arriving = []
        for i in plan.peer_order():
            peer = flipped_bits(frame, i)
            clip_set, positions = tubes(n, peer)
            src = source.at[:, clip_set, positions]
            dst = target.at[n, pl.ds(frame * plan.fd, plan.fd)]
            recv = refs.a2a_recv.at[which, n, i]
            if i == 0:
                copy = pltpu.make_async_copy(src, dst, recv)
                copy.start()
                arriving.append(copy.wait)
            else:
                copy = pltpu.make_async_remote_copy(
                    src_ref=src,
                    dst_ref=dst,
                    send_sem=refs.a2a_send.at[which, n, i],
                    recv_sem=recv,
                    device_id=(me[CLIP], peer),
                    device_id_type=MESH,
                )
                copy.start()
                sends.append(copy.wait_send)
                arriving.append(copy.wait_recv)
        return arriving

    def to_frames(which, source, target, n):
        arriving = []
        for i in plan.peer_order():
            peer = flipped_bits(frame, i)
            clip_set, positions = tubes(n, frame)
            src = source.at[n, pl.ds(peer * plan.fd, plan.fd)]
            dst = target.at[:, clip_set, positions]
            recv = refs.a2a_recv.at[which, n, i]
            if i == 0:
                copy = pltpu.make_async_copy(src, dst, recv)
                copy.start()
                arriving.append((lambda: None, copy.wait))
            else:
                copy = pltpu.make_async_remote_copy(
                    src_ref=src,
                    dst_ref=dst,
                    send_sem=refs.a2a_send.at[which, n, i],
                    recv_sem=recv,
                    device_id=(me[CLIP], peer),
                    device_id_type=MESH,
                )
                copy.start()
                arriving.append((copy.wait_recv, copy.wait_send))
        return arriving

    def wait_all(waits):
        for wait in waits:
            wait()

    x_arrives = [to_tubes(0, refs.stream, xin, 0)]
    g_arrives = []

    loads = []
    for i, (src, dst) in enumerate(zip(refs.from_hbm, (wqkv, wout, wup, wdown))):
        load = pltpu.make_async_copy(src, dst, refs.load_sems.at[i])
        load.start()
        loads.append(load)

    raw = n2
    grad_loads = []
    for r in range(plan.rows):
        grad_load = pltpu.make_async_copy(
            refs.grad.at[r // plan.cd, r % plan.cd],
            raw.at[pl.ds(r * plan.spatial, plan.spatial)],
            refs.grad_sems.at[r],
        )
        grad_load.start()
        grad_loads.append(grad_load.wait)
    wait_all(grad_loads)
    places = (plan.spatial, plan.spatial)
    diagonal = lax.broadcasted_iota(jnp.int32, places, 0) == lax.broadcasted_iota(
        jnp.int32, places, 1
    )
    for r in range(plan.rows):
        kept = refs.mask[pl.ds(r, 1), :] == 1
        keep = jnp.where(diagonal & kept, 1.0, 0.0).astype(BF16)
        rows = dot_nn(keep, raw[pl.ds(r * plan.spatial, plan.spatial), :])
        refs.gsrc[r // plan.cd, r % plan.cd] = rows.astype(BF16)
    for n in range(1, S):
        wait_all(sends)
        sends.clear()
        x_arrives.append(to_tubes(0, refs.stream, xin, n))

    scatters = [
        Scatter(
            plan,
            me,
            part,
            refs.groups[group],
            refs.group_slots[group],
            refs.res.at[group],
            refs.rs_send,
            refs.rs_recv,
        )
        for part, (group, *_) in enumerate(plan.parts)
    ]

    def start(group):
        for part, scatter in enumerate(scatters):
            if plan.parts[part][0] == group:
                scatter.start()

    def tick(name):
        for part in DUE.get(name, ()):
            if part < len(scatters) and scatters[part].copies and not scatters[part].done():
                scatters[part].advance()

    def pieces(name, count, total, body, unroll=1):
        for i in range(count):
            lax.fori_loop(total * i // count, total * (i + 1) // count, body, 0, unroll=unroll)
            tick(name + str(i))

    def seq_rows(ref, s, start, size):
        frames = size // plan.pos
        block = ref[s, pl.ds(start // plan.pos, frames)]
        return block.reshape(size, D)

    sums[...] = jnp.zeros_like(sums)

    def tally(i, value):
        sums[i] += fold8(value)

    lanes = lax.broadcasted_iota(jnp.int32, (1, 128), 1)
    head_masks = [(lanes < 64).astype(BF16), (lanes >= 64).astype(BF16)]

    scale = 1.0 / math.sqrt(D // HEADS)

    def head_columns(pair):
        at = pair * 128
        return tuple(ds(first + at, 128) for first in (0, 0, D, 2 * D))

    for s in range(S):
        wait_all(x_arrives[s])
        if s == S - 1:
            g_arrives += [to_tubes(1, refs.gsrc, gin, n) for n in range(S)]

        def first_norm(i, _):
            x = seq_rows(xin, s, i * ROW_BLOCK, ROW_BLOCK).astype(F32)
            unit, _ = unit_norm(x)
            tally(8, x * x)
            n1[ds(s * L + i * ROW_BLOCK, ROW_BLOCK), :] = (unit * ln1_gain[...] + ln1_bias[...]).astype(BF16)
            return 0

        lax.fori_loop(0, L // ROW_BLOCK, first_norm, 0)
        if s == 0:
            loads[0].wait()
        tokens = pl.ds(s * L, L)
        for third in range(3):
            columns = pl.ds(third * D, D)
            out = dot_nn(n1[tokens, :], wqkv[:, columns])
            if third != 1:
                out = out + b_qv[:, pl.ds(third // 2 * D, D)]
            if third == 0:
                out = out * scale
            qkv[tokens, columns] = out.astype(BF16)

        def attend(pair, _):
            columns, q_at, k_at, v_at = head_columns(pair)
            q, k, v = qkv[tokens, q_at], qkv[tokens, k_at], qkv[tokens, v_at]
            out = jnp.zeros((L, 128), F32)
            for e in range(2):
                scores = dot_nt(q * head_masks[e], k)
                power = jnp.exp(scores - jnp.max(scores, axis=-1, keepdims=True))
                share = 1.0 / jnp.sum(power, axis=-1, keepdims=True)
                weight = (power * share).astype(BF16)
                prob[s * HEADS + pair * 2 + e] = weight
                out = out + dot_nn(weight, v * head_masks[e])
            mixed[tokens, columns] = out.astype(BF16)
            return 0

        lax.fori_loop(0, HEADS // 2, attend, 0, unroll=3)

    loads[1].wait()

    mid[...] = dot_nn(mixed[...], wout[...]) + b_out[...]
    for s in range(S):

        def second_norm(i, _):
            rows = ds(s * L + i * ROW_BLOCK, ROW_BLOCK)
            branch = mid[rows, :]
            middle = seq_rows(xin, s, i * ROW_BLOCK, ROW_BLOCK).astype(F32) + branch
            mid[rows, :] = middle
            tally(9, middle * middle)
            tally(11, branch * branch)
            unit, _ = unit_norm(middle)
            n2[rows, :] = (unit * ln2_gain[...] + ln2_bias[...]).astype(BF16)
            return 0

        lax.fori_loop(0, L // ROW_BLOCK, second_norm, 0)

    loads[2].wait()

    def up(i, _):
        columns = ds(i * D, D)
        hidden = dot_nn(n2[...], wup[:, columns]) + b_up[:, columns]
        active, steep = gelu_and_slope(hidden)
        act[:, columns] = active.astype(BF16)
        slope[:, columns] = steep.astype(BF16)
        return 0

    lax.fori_loop(0, nj, up, 0)
    loads[3].wait()
    out_arrives = []
    for s in range(S):
        tokens = pl.ds(s * L, L)
        branch = dot_nn(act[tokens, :], wdown[...]) + b_down[...]
        result = branch + mid[tokens, :]
        tally(10, result * result)
        tally(12, branch * branch)
        obuf[s] = result.astype(BF16).reshape(FRAMES, plan.pos, D)
        out_arrives += to_frames(2, obuf, refs.out_h, s)

    for s in range(S):
        wait_all(g_arrives[s])
    wait_all(sends)
    sends.clear()
    def put(group, chunk, frame_block, block):
        for of_group, order, first, height in plan.parts:
            if of_group == group:
                at = plan.place(order, chunk, frame_block)
                rows = pl.multiple_of(first * plan.blocks + at * height, 16)
                piece = block[first : first + height]
                refs.groups[group][pl.ds(rows, height), :] = piece.astype(BF16)

    def grad_down(i, _):
        out = dot_tn(act[:, ds(i * D, D)], gin[...].reshape(T, D))
        share = FF // plan.F
        for n in range(D // plan.R):
            place = n * plan.R
            frames = D // share
            chunk = place % share // plan.R
            put(0, chunk, i * frames + place // share, out[place : place + plan.R])
        return 0

    pieces("GD", nj, nj, grad_down)
    start(0)

    def through_gelu(i, _):
        columns = ds(i * D, D)
        d_active = dot_nt(gin[...].reshape(T, D), wdown[columns, :])
        d_hidden = (d_active * slope[:, columns].astype(F32)).astype(BF16)
        slope[:, columns] = d_hidden
        sums[13 + i] += fold8(d_hidden.astype(F32))
        return 0

    pieces("TG", nj, nj, through_gelu)

    def grad_columns(group, chunk, lhs, rhs):
        out = dot_tn(lhs, rhs)
        for f in range(plan.F):
            put(group, chunk, f, out[f * plan.R : (f + 1) * plan.R])

    core = lax.rem(me[CLIP], 2)

    def grad_up(i, _):
        c = lax.rem((1 - core) * plan.X + i, plan.C)
        grad_columns(1, c, n2[...], slope[:, ds(c * D, D)])
        return 0

    lax.fori_loop(0, plan.X, grad_up, 0)
    tick("GU0")
    start(1)
    lax.fori_loop(plan.X, plan.C, grad_up, 0)
    tick("GU1")
    acc[...] = dot_nt(slope[...], wup[...])
    tick("DT")

    for s in range(S):

        def second_norm_back(i, _):
            rows = ds(s * L + i * ROW_BLOCK, ROW_BLOCK)
            up_grad = acc[rows, :]
            unit, inverse = unit_norm(mid[rows, :])
            g = seq_rows(gin, s, i * ROW_BLOCK, ROW_BLOCK).astype(F32)
            d_middle = g + norm_pull(up_grad * ln2_gain[...], unit, inverse)
            dmid[rows, :] = d_middle
            low = d_middle.astype(BF16)
            dbranch[rows, :] = low
            tally(4, low.astype(F32))
            tally(5, up_grad * unit)
            tally(6, up_grad)
            tally(7, g)
            return 0

        lax.fori_loop(0, L // ROW_BLOCK, second_norm_back, 0)
        tick("LB" + str(s))

    grad_columns(2, plan.C - 1, mixed[...], dbranch[...])
    tick("DO")
    dmixed[...] = dot_nt(dbranch[...], wout[...]).astype(BF16)
    tick("DM")

    for s in range(S):
        tokens = pl.ds(s * L, L)

        def attend_back(pair, _):
            columns, q_at, k_at, v_at = head_columns(pair)
            q, k, v = qkv[tokens, q_at], qkv[tokens, k_at], qkv[tokens, v_at]
            d_out = dmixed[tokens, columns]
            zero = jnp.zeros((L, 128), F32)
            d_q, d_k, d_v = zero, zero, zero
            for e in range(2):
                weight = prob[s * HEADS + pair * 2 + e]
                own = d_out * head_masks[e]
                d_weight = dot_nt(own, v)
                d_v = d_v + dot_tn(weight, own)
                wide_weight = weight.astype(F32)
                centre = jnp.sum(wide_weight * d_weight, axis=-1, keepdims=True)
                d_score = (wide_weight * (d_weight - centre)).astype(BF16)
                d_q = d_q + dot_nn(d_score, k * head_masks[e])
                d_k = d_k + dot_tn(d_score, q * head_masks[e])
            qkv[tokens, q_at] = (d_q * scale).astype(BF16)
            qkv[tokens, k_at] = d_k.astype(BF16)
            qkv[tokens, v_at] = d_v.astype(BF16)
            return 0

        pieces("AB" + str(s), 2, HEADS // 2, attend_back, unroll=3)

    def grad_qkv(i, _):
        c = core * i + (1 - core) * lax.rem(plan.X + i + (i + 1) // plan.X, plan.C)
        grad_columns(2, c, n1[...], qkv[:, ds(c * D, D)])
        return 0

    lax.fori_loop(0, plan.X, grad_qkv, 0)
    tick("GQ0")
    start(2)
    lax.fori_loop(plan.X, plan.C - 1, grad_qkv, 0)
    tick("GQ1")
    acc[...] = dot_nt(qkv[...], wqkv[...])
    tick("D1")
    for recv, send in out_arrives:
        send()
    in_arrives = []
    for s in range(S):

        def first_norm_back(i, _):
            rows = ds(s * L + i * ROW_BLOCK, ROW_BLOCK)
            up_grad = acc[rows, :]
            x = seq_rows(xin, s, i * ROW_BLOCK, ROW_BLOCK).astype(F32)
            unit, inverse = unit_norm(x)
            total = dmid[rows, :] + norm_pull(up_grad * ln1_gain[...], unit, inverse)
            frames = ROW_BLOCK // plan.pos
            igbuf[s, pl.ds(i * frames, frames)] = total.astype(BF16).reshape(frames, plan.pos, D)
            tally(0, up_grad * unit)
            tally(1, up_grad)
            tally(2, qkv[rows, pl.ds(0, D)].astype(F32))
            tally(3, qkv[rows, pl.ds(2 * D, D)].astype(F32))
            return 0

        lax.fori_loop(0, L // ROW_BLOCK, first_norm_back, 0)
        in_arrives += to_frames(3, igbuf, refs.ig_h, s)
        tick("L1" + str(s))

    vbuf, vrecv = refs.vbuf, refs.vrecv
    count = sums.shape[0]
    for i in range(count):
        vbuf[0, pl.ds(i, 1), :] = jnp.sum(sums[i], axis=0, keepdims=True)
    hops = plan.steps("xyz")
    small = []
    for i, (axis, bit) in enumerate(hops):
        flipped = me[axis] + bit * (1 - 2 * ((me[axis] // bit) % 2))
        to = {**me, axis: flipped}
        copy = pltpu.make_async_remote_copy(
            src_ref=vbuf.at[i],
            dst_ref=vrecv.at[i],
            send_sem=refs.v_send.at[i],
            recv_sem=refs.v_recv.at[i],
            device_id=(to[CLIP], to[FRAME]),
            device_id_type=MESH,
        )
        copy.start()
        small.append(copy)
        tick("V" + str(i))
        copy.wait_recv()
        vbuf[i + 1] = vbuf[i] + vrecv[i]
    refs.vec[...] = vbuf[len(hops)]
    for copy in small:
        copy.wait_send()
    tick("END")
    while not all(scatter.done() for scatter in scatters):
        for scatter in scatters:
            if not scatter.done():
                scatter.advance()
    for scatter in scatters:
        scatter.finish()
    for recv, send in out_arrives:
        recv()
    for recv, send in in_arrives:
        send()
        recv()
    wait_all(sends)


def fused(plan, stream, out_grad, token_mask, weights, small):
    D, T, S, L, FF = plan.D, plan.T, plan.S, plan.L, plan.FF
    n_steps = len(plan.steps("xyz"))
    n_parts = len(plan.parts)
    n_hops = n_steps + len(plan.gather_steps())
    n_vec = 13 + plan.nj
    vec_rows = -(-n_vec // 8) * 8
    vmem = lambda shape, kind=BF16: pltpu.VMEM(shape, kind)
    token_shape = (plan.fd, plan.cd, plan.spatial, D)
    scratch = dict(
        wqkv=vmem((D, 3 * D)),
        wout=vmem((D, D)),
        wup=vmem((D, FF)),
        wdown=vmem((FF, D)),
        xin=vmem((S, FRAMES, plan.pos, D)),
        gin=vmem((S, FRAMES, plan.pos, D)),
        n1=vmem((T, D)),
        qkv=vmem((T, 3 * D)),
        prob=vmem((S * HEADS, L, L)),
        mixed=vmem((T, D)),
        mid=vmem((T, D), F32),
        n2=vmem((T, D)),
        act=vmem((T, FF)),
        slope=vmem((T, FF)),
        obuf=vmem((S, FRAMES, plan.pos, D)),
        acc=vmem((T, D), F32),
        sums=vmem((n_vec, 8, D), F32),
        g_down=vmem((plan.whole, D)),
        g_up=vmem((plan.whole, D)),
        vbuf=vmem((n_steps + 1, vec_rows, D), F32),
        vrecv=vmem((n_steps, vec_rows, D), F32),
        small_rows=[vmem((1, item.size), F32) for item in small],
        gsrc=vmem(token_shape),
        load_sems=pltpu.SemaphoreType.DMA((4,)),
        grad_sems=pltpu.SemaphoreType.DMA((plan.rows,)),
        a2a_send=pltpu.SemaphoreType.DMA((4, S, plan.F)),
        a2a_recv=pltpu.SemaphoreType.DMA((4, S, plan.F)),
        rs_send=pltpu.SemaphoreType.DMA((n_parts, n_hops)),
        rs_recv=pltpu.SemaphoreType.DMA((n_parts, n_hops)),
        v_send=pltpu.SemaphoreType.DMA((n_steps,)),
        v_recv=pltpu.SemaphoreType.DMA((n_steps,)),
        slots=[
            vmem((3, plan.whole >> (i + 1), D)) for i in range(n_steps)
        ],
    )

    def kernel(stream, grad, wqkv, wout, wup, wdown, mask, *rest):
        count = len(small)
        refs = SimpleNamespace(
            stream=stream,
            grad=grad,
            from_hbm=(wqkv, wout, wup, wdown),
            mask=mask,
            small=rest[:count],
        )
        refs.out_h, refs.ig_h, refs.res, refs.vec = rest[count : count + 4]
        vars(refs).update(rest[count + 4])
        refs.groups = (refs.g_down, refs.g_up, refs.wdown)
        refs.group_slots = [[slot.at[group] for slot in refs.slots] for group in range(3)]
        layer_kernel(plan, refs)

    hbm = pl.BlockSpec(memory_space=pl.ANY)
    in_vmem = pl.BlockSpec(memory_space=pltpu.VMEM)
    return pl.pallas_call(
        kernel,
        out_shape=(
            jax.ShapeDtypeStruct(token_shape, BF16),
            jax.ShapeDtypeStruct(token_shape, BF16),
            jax.ShapeDtypeStruct((3, plan.C * plan.R, D), BF16),
            jax.ShapeDtypeStruct((vec_rows, D), F32),
        ),
        in_specs=[hbm] * 6 + [in_vmem] * (1 + len(small)),
        out_specs=(hbm, hbm, in_vmem, in_vmem),
        scratch_shapes=(scratch,),
        compiler_params=pltpu.CompilerParams(
            collective_id=0, has_side_effects=True, vmem_limit_bytes=VMEM_LIMIT
        ),
        name="tube_layer",
    )(
        stream.reshape(token_shape),
        out_grad.reshape(token_shape),
        *weights,
        token_mask,
        *small,
    )


VMEM_LIMIT = 64 * 1024 * 1024 - 512 * 1024


def finish_kernel(plan, out_s, ig_s, res_h, vec_h, out_d, ig_d, *refs):
    C, R, D = plan.C, plan.R, plan.D
    qkv_d, up_d, proj_d, down_d = refs[:4]
    vectors, statistics = refs[4:12], refs[12]
    qkv_v, up_v, proj_v, down_v, res, vec, out_v, ig_v, sems = refs[13:]
    moves = [(res_h.at[group], res.at[group]) for group in range(3)]
    moves += [(vec_h, vec), (out_s, out_v), (ig_s, ig_v)]
    copies = [pltpu.make_async_copy(*move, sems.at[i]) for i, move in enumerate(moves)]
    for copy in copies:
        copy.start()

    def write(value, target):
        copy = pltpu.make_async_copy(value, target, sems.at[len(copies)])
        copy.start()
        copies.append(copy)

    def each_piece(group):
        for of_group, _, first, height in plan.parts:
            if of_group == group:
                for chunk in range(C):
                    block = res[group, pl.ds(first * C + chunk * height, height), :]
                    yield chunk, first, height, block.astype(F32)

    copies[0].wait()
    for chunk, first, height, block in each_piece(0):
        down_v[pl.ds(chunk * R + first, height), :] = block
    write(down_v, down_d)
    copies[1].wait()
    for chunk, first, height, block in each_piece(1):
        up_v[pl.ds(first, height), pl.ds(chunk * D, D)] = block
    write(up_v, up_d)
    copies[2].wait()
    for chunk, first, height, block in each_piece(2):
        if chunk < C - 1:
            qkv_v[pl.ds(first, height), pl.ds(chunk * D, D)] = block
        else:
            proj_v[pl.ds(first, height), :] = block
    write(qkv_v, qkv_d)
    write(proj_v, proj_d)
    copies[4].wait()
    write(out_v, out_d)
    copies[5].wait()
    write(ig_v, ig_d)

    copies[3].wait()
    frame = lax.axis_index(FRAME)
    counts = (1, 1, 2, 1, 1, 1, plan.nj, 1)
    firsts = (0, 1, 2, 4, 5, 6, 13, 7)
    for target, count, first in zip(vectors, counts, firsts):
        share = count * D // plan.F
        per_row = plan.F // count
        row = vec[pl.ds(first + frame // per_row, 1), :]
        turned = pltpu.roll(row, lax.rem(D - (frame % per_row) * share, D), 1)
        target[...] = turned[:, :share].reshape(-1)
    squares = jnp.sum(vec[pl.ds(8, 8), :], axis=-1, keepdims=True)
    entries = plan.T * D * C * plan.F
    roots = jnp.sqrt(squares / entries)
    lanes = lax.broadcasted_iota(jnp.int32, (8, 8), 1)
    rows = lax.broadcasted_iota(jnp.int32, (8, 8), 0)
    across = jnp.sum(jnp.where(lanes == rows, roots, 0.0), axis=0, keepdims=True)
    statistics[...] = across[:, :5].reshape(-1)
    for copy in copies[6:]:
        copy.wait()


def finish(plan, output, input_grad, res, vec):
    D, F, C, R = plan.D, plan.F, plan.C, plan.R
    shapes = [(R, 3 * D), (R, C * D), (R, D), (C * R, D)]
    vectors = [(count * D // F,) for count in (1, 1, 2, 1, 1, 1, plan.nj, 1)]
    hbm = pl.BlockSpec(memory_space=pltpu.HBM)
    in_vmem = pl.BlockSpec(memory_space=pltpu.VMEM)
    like = lambda item: jax.ShapeDtypeStruct(item.shape, item.dtype)
    return pl.pallas_call(
        functools.partial(finish_kernel, plan),
        out_shape=tuple(
            [like(output), like(input_grad)]
            + [jax.ShapeDtypeStruct(shape, F32) for shape in shapes + vectors + [(5,)]]
        ),
        in_specs=[hbm] * 4,
        out_specs=tuple([hbm] * 6 + [in_vmem] * 9),
        scratch_shapes=[pltpu.VMEM(shape, F32) for shape in shapes]
        + [pltpu.VMEM(res.shape, BF16), pltpu.VMEM(vec.shape, F32)]
        + [pltpu.VMEM(output.shape, BF16)] * 2
        + [pltpu.SemaphoreType.DMA((12,))],
        compiler_params=pltpu.CompilerParams(vmem_limit_bytes=VMEM_LIMIT),
        name="tube_layer_results",
    )(output, input_grad, res, vec)


def with_kernel(
    plan,
    stream,
    out_grad,
    token_mask,
    ln1_gain,
    ln1_bias,
    w_qkv,
    b_qv,
    w_out,
    b_out,
    ln2_gain,
    ln2_bias,
    w_up,
    b_up,
    w_down,
    b_down,
):
    small = (ln1_gain, ln1_bias, b_qv, b_out, ln2_gain, ln2_bias, b_up, b_down)
    parts = fused(plan, stream, out_grad, token_mask, (w_qkv, w_out, w_up, w_down), small)
    output, input_grad, g_qkv, g_up, g_out, g_down, *vectors, statistics = finish(plan, *parts)
    return (
        output.reshape(stream.shape),
        input_grad.reshape(stream.shape),
        vectors[0],
        vectors[1],
        g_qkv,
        vectors[2],
        g_out,
        vectors[3],
        vectors[4],
        vectors[5],
        g_up,
        vectors[6],
        g_down,
        vectors[7],
        statistics,
    )


def layer_norm(inputs, norm_gain, norm_shift):
    center = jnp.mean(inputs, axis=-1, keepdims=True)
    shifted = inputs - center
    spread = jnp.mean(shifted * shifted, axis=-1, keepdims=True)
    inverse = lax.rsqrt(spread + EPS)
    unit = shifted * inverse
    return (unit * norm_gain + norm_shift, unit, inverse)


def norm_backward(upstream, unit, inverse, norm_gain):
    scaled = upstream * norm_gain
    first = jnp.mean(scaled, axis=-1, keepdims=True)
    second = jnp.mean(scaled * unit, axis=-1, keepdims=True)
    return inverse * (scaled - first - unit * second)


def gelu_slope(hidden_state):
    cumulative = 0.5 * (1.0 + lax.erf(hidden_state * (1.0 / math.sqrt(2.0))))
    density = jnp.exp(-0.5 * hidden_state * hidden_state) * (1.0 / math.sqrt(2.0 * math.pi))
    return cumulative + hidden_state * density


def with_collectives(
    stream,
    out_grad,
    token_mask,
    ln1_gain,
    ln1_bias,
    w_qkv,
    b_qv,
    w_out,
    b_out,
    ln2_gain,
    ln2_bias,
    w_up,
    b_up,
    w_down,
    b_down,
):
    frame_count = lax.axis_size(FRAME)
    clip_count = lax.axis_size(CLIP)
    device_count = clip_count * frame_count
    frame_split = min(FRAMES, frame_count)
    clip_split = frame_count // frame_split
    frames_dev = FRAMES // frame_split
    tubes_dev = TUBES // frame_split
    row_count, spatial, width = stream.shape
    clips_dev = row_count // frames_dev
    clip_sets = clips_dev // clip_split
    tube_pos = spatial // TUBES
    length = FRAMES * tube_pos
    head_dim = width // HEADS
    scale = 1.0 / math.sqrt(head_dim)

    def leaving(tensor):
        return tensor.reshape(frames_dev, clip_sets, frame_count, tubes_dev * tube_pos, width)

    def arranged(tensor):
        tensor = tensor.reshape(clip_split, FRAMES, clip_sets, tubes_dev, tube_pos, width)
        tensor = jnp.transpose(tensor, (0, 2, 3, 1, 4, 5))
        return tensor.reshape(-1, width)

    def restored(tensor):
        tensor = tensor.reshape(clip_split, clip_sets, tubes_dev, FRAMES, tube_pos, width)
        tensor = jnp.transpose(tensor, (0, 3, 1, 2, 4, 5))
        return tensor.reshape(frame_count * frames_dev, clip_sets, 1, tubes_dev * tube_pos, width)

    masked = jnp.where(token_mask[:, :, None] == 1, out_grad, jnp.zeros((), jnp.bfloat16))
    arrived = (
        lax.all_to_all(leaving(stream), FRAME, split_axis=2, concat_axis=0, tiled=True),
        lax.all_to_all(leaving(masked), FRAME, split_axis=2, concat_axis=0, tiled=True),
    )
    inputs = arranged(arrived[0]).astype(jnp.float32)
    grad_y = arranged(arrived[1])
    seq_count = inputs.shape[0] // length

    def split_heads(tensor):
        return tensor.reshape(seq_count, length, HEADS, head_dim)

    def attention_scores(queries, key_part):
        return (
            jnp.einsum("slhe,smhe->shlm", queries, key_part, preferred_element_type=jnp.float32)
            * scale
        )

    first_normed_input, unit_one, inverse_one = layer_norm(inputs, ln1_gain, ln1_bias)
    first_normed_input = first_normed_input.astype(jnp.bfloat16)
    third_bias_term = jnp.concatenate(
        [b_qv[:width], jnp.zeros((width,), jnp.float32), b_qv[width:]]
    )
    query_key_value = (
        jnp.dot(first_normed_input, w_qkv, preferred_element_type=jnp.float32) + third_bias_term
    ).astype(jnp.bfloat16)
    queries = split_heads(query_key_value[:, :width])
    key_part = split_heads(query_key_value[:, width : 2 * width])
    values = split_heads(query_key_value[:, 2 * width :])
    scores = attention_scores(queries, key_part)
    largest = jnp.max(scores, axis=-1, keepdims=True)
    logsum = largest + jnp.log(jnp.sum(jnp.exp(scores - largest), axis=-1, keepdims=True))
    attend_low = jnp.exp(scores - logsum).astype(jnp.bfloat16)
    mixed_heads = jnp.einsum(
        "shlm,smhe->slhe", attend_low, values, preferred_element_type=jnp.float32
    )
    mixed_heads = mixed_heads.reshape(-1, width).astype(jnp.bfloat16)
    attention_branch = jnp.dot(mixed_heads, w_out, preferred_element_type=jnp.float32) + b_out
    middle = inputs + attention_branch
    second_normed_input, unit_two, inverse_two = layer_norm(middle, ln2_gain, ln2_bias)
    second_normed_input = second_normed_input.astype(jnp.bfloat16)
    hidden_state = jnp.dot(second_normed_input, w_up, preferred_element_type=jnp.float32) + b_up
    activated_hidden = jax.nn.gelu(hidden_state, approximate=False).astype(jnp.bfloat16)
    feedforward_branch = (
        jnp.dot(activated_hidden, w_down, preferred_element_type=jnp.float32) + b_down
    )
    result = middle + feedforward_branch
    squares = jnp.stack(
        [
            jnp.sum(inputs * inputs),
            jnp.sum(middle * middle),
            jnp.sum(result * result),
            jnp.sum(attention_branch * attention_branch),
            jnp.sum(feedforward_branch * feedforward_branch),
        ]
    )
    totals = lax.psum(squares, (CLIP, FRAME))
    statistics = jnp.sqrt(totals / (row_count * spatial * width * device_count))
    grad_w_down = jnp.einsum(
        "tf,td->fd", activated_hidden, grad_y, preferred_element_type=jnp.float32
    )
    grad_b_down = jnp.sum(grad_y.astype(jnp.float32), axis=0)
    d_active = jnp.einsum("td,fd->tf", grad_y, w_down, preferred_element_type=jnp.float32)
    d_hidden = (d_active * gelu_slope(hidden_state)).astype(jnp.bfloat16)
    grad_w_up = jnp.einsum(
        "td,tf->df", second_normed_input, d_hidden, preferred_element_type=jnp.float32
    )
    grad_b_up = jnp.sum(d_hidden.astype(jnp.float32), axis=0)
    d_two = jnp.einsum("tf,df->td", d_hidden, w_up, preferred_element_type=jnp.float32)
    grad_ln2_gain = jnp.sum(d_two * unit_two, axis=0)
    grad_ln2_bias = jnp.sum(d_two, axis=0)
    d_middle = grad_y.astype(jnp.float32) + norm_backward(d_two, unit_two, inverse_two, ln2_gain)
    d_branch = d_middle.astype(jnp.bfloat16)
    grad_w_out = jnp.einsum("td,te->de", mixed_heads, d_branch, preferred_element_type=jnp.float32)
    grad_b_out = jnp.sum(d_branch.astype(jnp.float32), axis=0)
    d_mixed = jnp.einsum("te,de->td", d_branch, w_out, preferred_element_type=jnp.float32)
    d_mixed = split_heads(d_mixed.astype(jnp.bfloat16))
    again = attention_scores(queries, key_part)
    attend = jnp.exp(again - logsum)
    attend_again = attend.astype(jnp.bfloat16)
    d_attend = jnp.einsum("slhe,smhe->shlm", d_mixed, values, preferred_element_type=jnp.float32)
    d_values = jnp.einsum(
        "shlm,slhe->smhe", attend_again, d_mixed, preferred_element_type=jnp.float32
    )
    centre_term = jnp.sum(attend * d_attend, axis=-1, keepdims=True)
    d_scores = (attend * (d_attend - centre_term)).astype(jnp.bfloat16)
    d_queries = (
        jnp.einsum("shlm,smhe->slhe", d_scores, key_part, preferred_element_type=jnp.float32)
        * scale
    )
    d_keys = (
        jnp.einsum("shlm,slhe->smhe", d_scores, queries, preferred_element_type=jnp.float32) * scale
    )
    d_qkv = jnp.concatenate(
        [d_queries.reshape(-1, width), d_keys.reshape(-1, width), d_values.reshape(-1, width)],
        axis=1,
    ).astype(jnp.bfloat16)
    grad_w_qkv = jnp.einsum(
        "td,te->de", first_normed_input, d_qkv, preferred_element_type=jnp.float32
    )
    bias_sums = jnp.sum(d_qkv.astype(jnp.float32), axis=0)
    grad_b_qv = jnp.concatenate([bias_sums[:width], bias_sums[2 * width :]])
    d_one = jnp.einsum("te,de->td", d_qkv, w_qkv, preferred_element_type=jnp.float32)
    grad_ln1_gain = jnp.sum(d_one * unit_one, axis=0)
    grad_ln1_bias = jnp.sum(d_one, axis=0)
    d_inputs = d_middle + norm_backward(d_one, unit_one, inverse_one, ln1_gain)
    departed = (
        lax.all_to_all(
            restored(result.astype(jnp.bfloat16)), FRAME, split_axis=0, concat_axis=2, tiled=True
        ),
        lax.all_to_all(
            restored(d_inputs.astype(jnp.bfloat16)),
            FRAME,
            split_axis=0,
            concat_axis=2,
            tiled=True,
        ),
    )
    output = departed[0].reshape(row_count, spatial, width)
    input_grad = departed[1].reshape(row_count, spatial, width)
    gradients = [
        grad_ln1_gain,
        grad_ln1_bias,
        grad_w_qkv,
        grad_b_qv,
        grad_w_out,
        grad_b_out,
        grad_ln2_gain,
        grad_ln2_bias,
        grad_w_up,
        grad_b_up,
        grad_w_down,
        grad_b_down,
    ]
    grouped = jnp.concatenate([item.reshape(frame_count, -1) for item in gradients], axis=1)
    extent_all = grouped.shape[1]
    padding = -extent_all % clip_count
    grouped = jnp.concatenate([grouped, jnp.zeros((frame_count, padding), jnp.float32)], axis=1)
    own_rows = lax.psum_scatter(
        grouped.astype(jnp.bfloat16), FRAME, scatter_dimension=0, tiled=True
    ).astype(jnp.float32)
    summed = lax.psum(own_rows, CLIP).reshape(-1)
    finished = []
    offset = 0
    for item in gradients:
        extent = item.size // frame_count
        local_shape = (item.shape[0] // frame_count,) + item.shape[1:]
        finished.append(summed[offset : offset + extent].reshape(local_shape))
        offset = offset + extent
    return (
        output,
        input_grad,
        finished[0],
        finished[1],
        finished[2],
        finished[3],
        finished[4],
        finished[5],
        finished[6],
        finished[7],
        finished[8],
        finished[9],
        finished[10],
        finished[11],
        statistics,
    )


def solution(mesh):
    clips, frames = mesh.shape[CLIP], mesh.shape[FRAME]

    def on_device(stream, *rest):
        ff = rest[-4].shape[1]
        plan = Plan(clips, frames, stream.shape, ff)
        if plan.fits:
            return with_kernel(plan, stream, *rest)
        return with_collectives(stream, *rest)

    tokens = P((CLIP, FRAME), None, None)
    in_specs = (tokens, tokens, P((CLIP, FRAME), None)) + (P(),) * 12
    rows, vector = P(FRAME, None), P(FRAME)
    out_specs = (
        tokens,
        tokens,
        vector,
        vector,
        rows,
        vector,
        rows,
        vector,
        vector,
        vector,
        rows,
        vector,
        rows,
        vector,
        P(),
    )
    return jax.shard_map(
        on_device, mesh=mesh, in_specs=in_specs, out_specs=out_specs, check_vma=False
    )
```

```python
import functools
import math
from types import SimpleNamespace

import jax
import jax.numpy as jnp
from jax import lax
from jax.experimental import pallas as pl
from jax.experimental.pallas import tpu as pltpu
from jax.sharding import PartitionSpec as P

HEADS = 12
FRAMES = 16
TUBES = 16
EPS = 1e-05

F32 = jnp.float32
BF16 = jnp.bfloat16
MESH = pl.DeviceIdType.MESH
ROW_BLOCK = 64
CLIP = "clip"
FRAME = "frame"


SIXTHS = 6
SHARES = (
    (("zyx", 2), ("xzy", 1), ("yzx", 1), ("yxz", 2),),
    (("xzy", 1), ("xyz", 3), ("yxz", 2),),
    (("xzy", 2), ("xyz", 2), ("yxz", 2),),
)
DUE = dict(
    GU0=(0, 1),
    GU1=(2, 3),
    DT=(4,),
    LB1=(5, 6),
    DO=(1,),
    AB00=(2,),
    AB01=(0,),
    AB10=(4,),
    AB11=(1,),
    GQ0=(2, 3),
    V0=(7, 4, 8, 5, 9, 0, 6, 1),
    V1=(3, 2, 7, 5, 3, 8, 7, 6, 9, 4, 5, 0, 2, 3, 1),
    V2=(6, 9, 7, 8, 4, 0, 2, 3, 2, 1, 5, 4, 7, 3),
    V3=(9, 1, 0, 4, 6, 0, 8, 5, 7, 5, 6, 7),
    V4=(9, 6, 8, 9, 8, 9, 8),
)


def dot_nn(lhs, rhs):
    return lax.dot_general(lhs, rhs, (((1,), (0,)), ((), ())), preferred_element_type=F32)


def dot_nt(lhs, rhs):
    return lax.dot_general(lhs, rhs, (((1,), (1,)), ((), ())), preferred_element_type=F32)


def dot_tn(lhs, rhs):
    return lax.dot_general(lhs, rhs, (((0,), (0,)), ((), ())), preferred_element_type=F32)


def unit_norm(rows):
    shifted = rows - jnp.mean(rows, axis=-1, keepdims=True)
    inverse = lax.rsqrt(jnp.mean(shifted * shifted, axis=-1, keepdims=True) + EPS)
    return shifted * inverse, inverse


def norm_pull(scaled, unit, inverse):
    first = jnp.mean(scaled, axis=-1, keepdims=True)
    second = jnp.mean(scaled * unit, axis=-1, keepdims=True)
    return inverse * (scaled - first - unit * second)


def gelu_and_slope(hidden):
    bell = jnp.exp(hidden * hidden * -0.5)
    t = 1.0 / (1.0 + jnp.abs(hidden) * (0.3275911 / math.sqrt(2.0)))
    poly = t * (
        0.5 * 0.254829592
        + t
        * (
            0.5 * -0.284496736
            + t * (0.5 * 1.421413741 + t * (0.5 * -1.453152027 + t * (0.5 * 1.061405429)))
        )
    )
    below = poly * bell
    cumulative = jnp.where(hidden >= 0.0, 1.0 - below, below)
    return hidden * cumulative, cumulative + hidden * bell * (1.0 / math.sqrt(2.0 * math.pi))


def fold8(rows):
    return jnp.sum(rows.reshape(rows.shape[0] // 8, 8, rows.shape[1]), axis=0)


def ds(start, size, unit=None):
    return pl.ds(pl.multiple_of(start, unit or size), size)


class Plan:
    def __init__(self, clips, frames, stream_shape, ff):
        self.C, self.F, self.FF = clips, frames, ff
        self.rows, self.spatial, self.D = stream_shape
        self.frame_split = min(FRAMES, frames)
        self.clip_split = frames // self.frame_split
        self.fd = FRAMES // self.frame_split
        self.td = TUBES // self.frame_split
        self.cd = self.rows // self.fd
        self.pos = self.spatial // TUBES
        self.L = FRAMES * self.pos
        self.S = self.cd * self.td
        self.T = self.S * self.L
        self.R = self.D // frames
        self.blocks = clips * frames
        self.whole = self.blocks * self.R
        self.parts = []
        for group, shares in enumerate(SHARES):
            first = 0
            for part, (order, share) in enumerate(shares):
                rows = self.R * share // SIXTHS
                self.parts.append((group, order, first, rows))
                first += rows
        self.nj = ff // self.D
        self.X = clips // 2
        self.Y = self.X if frames % self.X == 0 else 1
        powers = all(n & (n - 1) == 0 for n in (clips, frames, self.X, self.Y))
        self.fits = (
            self.clip_split == 1
            and clips >= 4
            and powers
            and frames % 2 == 0
            and self.R % (16 * SIXTHS) == 0
            and ff == clips * self.D
            and self.pos % 16 == 0
            and self.D % (ff // frames) == 0
        )

    def steps(self, order):
        bits = lambda n: [1 << i for i in range(n.bit_length() - 1)]
        along = dict(
            x=[(CLIP, 2 * b) for b in bits(self.X)],
            y=[(FRAME, b) for b in bits(self.Y)],
            z=[(FRAME, self.Y * b) for b in bits(self.F // self.Y)],
        )
        return [(CLIP, 1)] + along[order[0]] + along[order[1]] + along[order[2]]

    def peer_order(self):
        return range(self.F - 1, -1, -1)

    def gather_steps(self):
        return [(CLIP, 2 * (1 << i)) for i in range(self.X.bit_length() - 1)] + [(CLIP, 1)]

    def place(self, order, chunk, frame):
        clip = (chunk % self.X) * 2 + chunk // self.X
        where = 0
        for axis, bit in self.steps(order):
            where = where * 2 + ((clip if axis == CLIP else frame) // bit) % 2
        return where


class Scatter:
    def __init__(self, plan, me, part, held, slots, results, send_sems, recv_sems):
        group, order, first, self.height = plan.parts[part]
        self.plan, self.me = plan, me
        self.steps = plan.steps(order)
        self.gather = plan.gather_steps()
        rows = lambda count, per: pl.ds(first * per, count * per)
        self.held = held.at[rows(self.height, plan.blocks)]
        self.slots = [
            slot.at[rows(self.height, plan.blocks >> (i + 1))] for i, slot in enumerate(slots)
        ]
        self.result = results.at[rows(self.height, plan.C)]
        self.send_sems, self.recv_sems = send_sems.at[part], recv_sems.at[part]
        self.at = 0
        self.base = 0
        self.size = plan.blocks
        self.copies = []
        self.slot_of_me = (me[CLIP] % 2) * plan.X + me[CLIP] // 2

    def bit_of(self, axis, bit):
        return (self.me[axis] // bit) % 2

    def partner(self, axis, bit):
        flipped = self.me[axis] + bit * (1 - 2 * self.bit_of(axis, bit))
        return {**self.me, axis: flipped}

    def rows(self, base, size):
        return pl.ds(pl.multiple_of(base * self.height, self.height), size * self.height)

    def send(self, src, dst, axis, bit):
        to = self.partner(axis, bit)
        copy = pltpu.make_async_remote_copy(
            src_ref=src,
            dst_ref=dst,
            send_sem=self.send_sems.at[len(self.copies)],
            recv_sem=self.recv_sems.at[len(self.copies)],
            device_id=(to[CLIP], to[FRAME]),
            device_id_type=MESH,
        )
        copy.start()
        self.copies.append(copy)

    def start(self):
        if self.at < len(self.steps):
            axis, bit = self.steps[self.at]
            mine = self.bit_of(axis, bit)
            half = self.size // 2
            self.send(
                self.held.at[self.rows(self.base + (1 - mine) * half, half)],
                self.slots[self.at],
                axis,
                bit,
            )
            self.base = self.base + mine * half
            self.size = half
        elif self.at < len(self.steps) + len(self.gather):
            done = self.at - len(self.steps)
            axis, bit = self.gather[done]
            size = 1 << done
            region = self.rows((self.slot_of_me // size) * size, size)
            self.send(self.result.at[region], self.result.at[region], axis, bit)

    def advance(self):
        self.copies[self.at].wait_recv()
        if self.at < len(self.steps):
            slot = self.slots[self.at]
            last = self.at == len(self.steps) - 1
            target = self.result if last else self.held
            target_base = self.slot_of_me if last else self.base
            base, held = self.base, self.held

            def add(i, _):
                total = held[self.rows(base + i, 1)].astype(F32) + slot[self.rows(i, 1)].astype(F32)
                target[self.rows(target_base + i, 1)] = total.astype(BF16)
                return 0

            lax.fori_loop(0, self.size, add, 0)
        self.at += 1
        self.start()

    def done(self):
        return self.at == len(self.steps) + len(self.gather)

    def finish(self):
        assert self.done()
        for copy in self.copies:
            copy.wait_send()


def flipped_bits(index, bits):
    for b in range(bits.bit_length()):
        if bits >> b & 1:
            index = index + (1 << b) * (1 - 2 * ((index // (1 << b)) % 2))
    return index


def layer_kernel(plan, refs):
    D, T, S, L, FF, nj = plan.D, plan.T, plan.S, plan.L, plan.FF, plan.nj
    me = {CLIP: lax.axis_index(CLIP), FRAME: lax.axis_index(FRAME)}
    frame = me[FRAME]
    xin, gin, n1, qkv, prob, mixed = refs.xin, refs.gin, refs.n1, refs.qkv, refs.prob, refs.mixed
    mid, n2, act, slope, obuf, acc = refs.mid, refs.n2, refs.act, refs.slope, refs.obuf, refs.acc
    sums = refs.sums
    for source, target in zip(refs.small, refs.small_rows):
        target[...] = source[...].reshape(1, -1)
    ln1_gain, ln1_bias, b_qv, b_out, ln2_gain, ln2_bias, b_up, b_down = refs.small_rows
    wqkv, wout, wup, wdown = refs.wqkv, refs.wout, refs.wup, refs.wdown
    dbranch, dmixed, igbuf, dmid = n2, mixed, obuf, mid

    barrier = pltpu.get_barrier_semaphore()
    greeted = [(me[CLIP], lax.rem(frame + i, plan.F)) for i in range(1, plan.F)]
    for axis, bit in plan.gather_steps():
        flipped = me[axis] + bit * (1 - 2 * ((me[axis] // bit) % 2))
        greeted.append((flipped, frame))
    for peer in greeted:
        pl.semaphore_signal(barrier, inc=1, device_id=peer, device_id_type=MESH)
    pl.semaphore_wait(barrier, len(greeted))

    def tubes(n, device):
        clip_set, tube = n // plan.td, n % plan.td
        return clip_set, ds((device * plan.td + tube) * plan.pos, plan.pos)

    sends = []

    def to_tubes(which, source, target, n):
        arriving = []
        for i in plan.peer_order():
            peer = flipped_bits(frame, i)
            clip_set, positions = tubes(n, peer)
            src = source.at[:, clip_set, positions]
            dst = target.at[n, pl.ds(frame * plan.fd, plan.fd)]
            recv = refs.a2a_recv.at[which, n, i]
            if i == 0:
                copy = pltpu.make_async_copy(src, dst, recv)
                copy.start()
                arriving.append(copy.wait)
            else:
                copy = pltpu.make_async_remote_copy(
                    src_ref=src,
                    dst_ref=dst,
                    send_sem=refs.a2a_send.at[which, n, i],
                    recv_sem=recv,
                    device_id=(me[CLIP], peer),
                    device_id_type=MESH,
                )
                copy.start()
                sends.append(copy.wait_send)
                arriving.append(copy.wait_recv)
        return arriving

    def to_frames(which, source, target, n):
        arriving = []
        for i in plan.peer_order():
            peer = flipped_bits(frame, i)
            clip_set, positions = tubes(n, frame)
            src = source.at[n, pl.ds(peer * plan.fd, plan.fd)]
            dst = target.at[:, clip_set, positions]
            recv = refs.a2a_recv.at[which, n, i]
            if i == 0:
                copy = pltpu.make_async_copy(src, dst, recv)
                copy.start()
                arriving.append((lambda: None, copy.wait))
            else:
                copy = pltpu.make_async_remote_copy(
                    src_ref=src,
                    dst_ref=dst,
                    send_sem=refs.a2a_send.at[which, n, i],
                    recv_sem=recv,
                    device_id=(me[CLIP], peer),
                    device_id_type=MESH,
                )
                copy.start()
                arriving.append((copy.wait_recv, copy.wait_send))
        return arriving

    def wait_all(waits):
        for wait in waits:
            wait()

    x_arrives = [to_tubes(0, refs.stream, xin, 0)]
    g_arrives = []

    loads = []
    for i, (src, dst) in enumerate(zip(refs.from_hbm, (wqkv, wout, wup, wdown))):
        load = pltpu.make_async_copy(src, dst, refs.load_sems.at[i])
        load.start()
        loads.append(load)

    raw = n2
    grad_loads = []
    for r in range(plan.rows):
        grad_load = pltpu.make_async_copy(
            refs.grad.at[r // plan.cd, r % plan.cd],
            raw.at[pl.ds(r * plan.spatial, plan.spatial)],
            refs.grad_sems.at[r],
        )
        grad_load.start()
        grad_loads.append(grad_load.wait)
    wait_all(grad_loads)
    places = (plan.spatial, plan.spatial)
    diagonal = lax.broadcasted_iota(jnp.int32, places, 0) == lax.broadcasted_iota(
        jnp.int32, places, 1
    )
    for r in range(plan.rows):
        kept = refs.mask[pl.ds(r, 1), :] == 1
        keep = jnp.where(diagonal & kept, 1.0, 0.0).astype(BF16)
        rows = dot_nn(keep, raw[pl.ds(r * plan.spatial, plan.spatial), :])
        refs.gsrc[r // plan.cd, r % plan.cd] = rows.astype(BF16)
    for n in range(1, S):
        wait_all(sends)
        sends.clear()
        x_arrives.append(to_tubes(0, refs.stream, xin, n))

    scatters = [
        Scatter(
            plan,
            me,
            part,
            refs.groups[group],
            refs.group_slots[group],
            refs.res.at[group],
            refs.rs_send,
            refs.rs_recv,
        )
        for part, (group, *_) in enumerate(plan.parts)
    ]

    def start(group):
        for part, scatter in enumerate(scatters):
            if plan.parts[part][0] == group:
                scatter.start()

    def tick(name):
        for part in DUE.get(name, ()):
            if part < len(scatters) and scatters[part].copies and not scatters[part].done():
                scatters[part].advance()

    def pieces(name, count, total, body, unroll=1):
        for i in range(count):
            lax.fori_loop(total * i // count, total * (i + 1) // count, body, 0, unroll=unroll)
            tick(name + str(i))

    def seq_rows(ref, s, start, size):
        frames = size // plan.pos
        block = ref[s, pl.ds(start // plan.pos, frames)]
        return block.reshape(size, D)

    sums[...] = jnp.zeros_like(sums)

    def tally(i, value):
        sums[i] += fold8(value)

    lanes = lax.broadcasted_iota(jnp.int32, (1, 128), 1)
    head_masks = [(lanes < 64).astype(BF16), (lanes >= 64).astype(BF16)]

    scale = 1.0 / math.sqrt(D // HEADS)

    def head_columns(pair):
        at = pair * 128
        return tuple(ds(first + at, 128) for first in (0, 0, D, 2 * D))

    for s in range(S):
        wait_all(x_arrives[s])
        if s == S - 1:
            g_arrives += [to_tubes(1, refs.gsrc, gin, n) for n in range(S)]

        def first_norm(i, _):
            x = seq_rows(xin, s, i * ROW_BLOCK, ROW_BLOCK).astype(F32)
            unit, _ = unit_norm(x)
            tally(8, x * x)
            n1[ds(s * L + i * ROW_BLOCK, ROW_BLOCK), :] = (unit * ln1_gain[...] + ln1_bias[...]).astype(BF16)
            return 0

        lax.fori_loop(0, L // ROW_BLOCK, first_norm, 0)
        if s == 0:
            loads[0].wait()
        tokens = pl.ds(s * L, L)
        for third in range(3):
            columns = pl.ds(third * D, D)
            out = dot_nn(n1[tokens, :], wqkv[:, columns])
            if third != 1:
                out = out + b_qv[:, pl.ds(third // 2 * D, D)]
            if third == 0:
                out = out * scale
            qkv[tokens, columns] = out.astype(BF16)

        def attend(pair, _):
            columns, q_at, k_at, v_at = head_columns(pair)
            q, k, v = qkv[tokens, q_at], qkv[tokens, k_at], qkv[tokens, v_at]
            out = jnp.zeros((L, 128), F32)
            for e in range(2):
                scores = dot_nt(q * head_masks[e], k)
                power = jnp.exp(scores - jnp.max(scores, axis=-1, keepdims=True))
                share = 1.0 / jnp.sum(power, axis=-1, keepdims=True)
                weight = (power * share).astype(BF16)
                prob[s * HEADS + pair * 2 + e] = weight
                out = out + dot_nn(weight, v * head_masks[e])
            mixed[tokens, columns] = out.astype(BF16)
            return 0

        lax.fori_loop(0, HEADS // 2, attend, 0, unroll=3)

    loads[1].wait()

    mid[...] = dot_nn(mixed[...], wout[...]) + b_out[...]
    for s in range(S):

        def second_norm(i, _):
            rows = ds(s * L + i * ROW_BLOCK, ROW_BLOCK)
            branch = mid[rows, :]
            middle = seq_rows(xin, s, i * ROW_BLOCK, ROW_BLOCK).astype(F32) + branch
            mid[rows, :] = middle
            tally(9, middle * middle)
            tally(11, branch * branch)
            unit, _ = unit_norm(middle)
            n2[rows, :] = (unit * ln2_gain[...] + ln2_bias[...]).astype(BF16)
            return 0

        lax.fori_loop(0, L // ROW_BLOCK, second_norm, 0)

    loads[2].wait()

    def up(i, _):
        columns = ds(i * D, D)
        hidden = dot_nn(n2[...], wup[:, columns]) + b_up[:, columns]
        active, steep = gelu_and_slope(hidden)
        act[:, columns] = active.astype(BF16)
        slope[:, columns] = steep.astype(BF16)
        return 0

    lax.fori_loop(0, nj, up, 0)
    loads[3].wait()
    out_arrives = []
    for s in range(S):
        tokens = pl.ds(s * L, L)
        branch = dot_nn(act[tokens, :], wdown[...]) + b_down[...]
        result = branch + mid[tokens, :]
        tally(10, result * result)
        tally(12, branch * branch)
        obuf[s] = result.astype(BF16).reshape(FRAMES, plan.pos, D)
        out_arrives += to_frames(2, obuf, refs.out_h, s)

    for s in range(S):
        wait_all(g_arrives[s])
    wait_all(sends)
    sends.clear()
    def put(group, chunk, frame_block, block):
        for of_group, order, first, height in plan.parts:
            if of_group == group:
                at = plan.place(order, chunk, frame_block)
                rows = pl.multiple_of(first * plan.blocks + at * height, 16)
                piece = block[first : first + height]
                refs.groups[group][pl.ds(rows, height), :] = piece.astype(BF16)

    def grad_down(i, _):
        out = dot_tn(act[:, ds(i * D, D)], gin[...].reshape(T, D))
        share = FF // plan.F
        for n in range(D // plan.R):
            place = n * plan.R
            frames = D // share
            chunk = place % share // plan.R
            put(0, chunk, i * frames + place // share, out[place : place + plan.R])
        return 0

    pieces("GD", nj, nj, grad_down)
    start(0)

    def through_gelu(i, _):
        columns = ds(i * D, D)
        d_active = dot_nt(gin[...].reshape(T, D), wdown[columns, :])
        d_hidden = (d_active * slope[:, columns].astype(F32)).astype(BF16)
        slope[:, columns] = d_hidden
        sums[13 + i] += fold8(d_hidden.astype(F32))
        return 0

    pieces("TG", nj, nj, through_gelu)

    def grad_columns(group, chunk, lhs, rhs):
        out = dot_tn(lhs, rhs)
        for f in range(plan.F):
            put(group, chunk, f, out[f * plan.R : (f + 1) * plan.R])

    core = lax.rem(me[CLIP], 2)

    def grad_up(i, _):
        c = lax.rem((1 - core) * plan.X + i, plan.C)
        grad_columns(1, c, n2[...], slope[:, ds(c * D, D)])
        return 0

    lax.fori_loop(0, plan.X, grad_up, 0)
    tick("GU0")
    start(1)
    lax.fori_loop(plan.X, plan.C, grad_up, 0)
    tick("GU1")
    acc[...] = dot_nt(slope[...], wup[...])
    tick("DT")

    for s in range(S):

        def second_norm_back(i, _):
            rows = ds(s * L + i * ROW_BLOCK, ROW_BLOCK)
            up_grad = acc[rows, :]
            unit, inverse = unit_norm(mid[rows, :])
            g = seq_rows(gin, s, i * ROW_BLOCK, ROW_BLOCK).astype(F32)
            d_middle = g + norm_pull(up_grad * ln2_gain[...], unit, inverse)
            dmid[rows, :] = d_middle
            low = d_middle.astype(BF16)
            dbranch[rows, :] = low
            tally(4, low.astype(F32))
            tally(5, up_grad * unit)
            tally(6, up_grad)
            tally(7, g)
            return 0

        lax.fori_loop(0, L // ROW_BLOCK, second_norm_back, 0)
        tick("LB" + str(s))

    grad_columns(2, plan.C - 1, mixed[...], dbranch[...])
    tick("DO")
    dmixed[...] = dot_nt(dbranch[...], wout[...]).astype(BF16)
    tick("DM")

    for s in range(S):
        tokens = pl.ds(s * L, L)

        def attend_back(pair, _):
            columns, q_at, k_at, v_at = head_columns(pair)
            q, k, v = qkv[tokens, q_at], qkv[tokens, k_at], qkv[tokens, v_at]
            d_out = dmixed[tokens, columns]
            zero = jnp.zeros((L, 128), F32)
            d_q, d_k, d_v = zero, zero, zero
            for e in range(2):
                weight = prob[s * HEADS + pair * 2 + e]
                own = d_out * head_masks[e]
                d_weight = dot_nt(own, v)
                d_v = d_v + dot_tn(weight, own)
                wide_weight = weight.astype(F32)
                centre = jnp.sum(wide_weight * d_weight, axis=-1, keepdims=True)
                d_score = (wide_weight * (d_weight - centre)).astype(BF16)
                d_q = d_q + dot_nn(d_score, k * head_masks[e])
                d_k = d_k + dot_tn(d_score, q * head_masks[e])
            qkv[tokens, q_at] = (d_q * scale).astype(BF16)
            qkv[tokens, k_at] = d_k.astype(BF16)
            qkv[tokens, v_at] = d_v.astype(BF16)
            return 0

        pieces("AB" + str(s), 2, HEADS // 2, attend_back, unroll=3)

    def grad_qkv(i, _):
        c = core * i + (1 - core) * lax.rem(plan.X + i + (i + 1) // plan.X, plan.C)
        grad_columns(2, c, n1[...], qkv[:, ds(c * D, D)])
        return 0

    lax.fori_loop(0, plan.X, grad_qkv, 0)
    tick("GQ0")
    start(2)
    lax.fori_loop(plan.X, plan.C - 1, grad_qkv, 0)
    tick("GQ1")
    acc[...] = dot_nt(qkv[...], wqkv[...])
    tick("D1")
    for recv, send in out_arrives:
        send()
    in_arrives = []
    for s in range(S):

        def first_norm_back(i, _):
            rows = ds(s * L + i * ROW_BLOCK, ROW_BLOCK)
            up_grad = acc[rows, :]
            x = seq_rows(xin, s, i * ROW_BLOCK, ROW_BLOCK).astype(F32)
            unit, inverse = unit_norm(x)
            total = dmid[rows, :] + norm_pull(up_grad * ln1_gain[...], unit, inverse)
            frames = ROW_BLOCK // plan.pos
            igbuf[s, pl.ds(i * frames, frames)] = total.astype(BF16).reshape(frames, plan.pos, D)
            tally(0, up_grad * unit)
            tally(1, up_grad)
            tally(2, qkv[rows, pl.ds(0, D)].astype(F32))
            tally(3, qkv[rows, pl.ds(2 * D, D)].astype(F32))
            return 0

        lax.fori_loop(0, L // ROW_BLOCK, first_norm_back, 0)
        in_arrives += to_frames(3, igbuf, refs.ig_h, s)
        tick("L1" + str(s))

    vbuf, vrecv = refs.vbuf, refs.vrecv
    count = sums.shape[0]
    for i in range(count):
        vbuf[0, pl.ds(i, 1), :] = jnp.sum(sums[i], axis=0, keepdims=True)
    hops = plan.steps("xyz")
    small = []
    for i, (axis, bit) in enumerate(hops):
        flipped = me[axis] + bit * (1 - 2 * ((me[axis] // bit) % 2))
        to = {**me, axis: flipped}
        copy = pltpu.make_async_remote_copy(
            src_ref=vbuf.at[i],
            dst_ref=vrecv.at[i],
            send_sem=refs.v_send.at[i],
            recv_sem=refs.v_recv.at[i],
            device_id=(to[CLIP], to[FRAME]),
            device_id_type=MESH,
        )
        copy.start()
        small.append(copy)
        tick("V" + str(i))
        copy.wait_recv()
        vbuf[i + 1] = vbuf[i] + vrecv[i]
    refs.vec[...] = vbuf[len(hops)]
    for copy in small:
        copy.wait_send()
    tick("END")
    while not all(scatter.done() for scatter in scatters):
        for scatter in scatters:
            if not scatter.done():
                scatter.advance()
    for scatter in scatters:
        scatter.finish()
    for recv, send in out_arrives:
        recv()
    for recv, send in in_arrives:
        send()
        recv()
    wait_all(sends)


def fused(plan, stream, out_grad, token_mask, weights, small):
    D, T, S, L, FF = plan.D, plan.T, plan.S, plan.L, plan.FF
    n_steps = len(plan.steps("xyz"))
    n_parts = len(plan.parts)
    n_hops = n_steps + len(plan.gather_steps())
    n_vec = 13 + plan.nj
    vec_rows = -(-n_vec // 8) * 8
    vmem = lambda shape, kind=BF16: pltpu.VMEM(shape, kind)
    token_shape = (plan.fd, plan.cd, plan.spatial, D)
    scratch = dict(
        wqkv=vmem((D, 3 * D)),
        wout=vmem((D, D)),
        wup=vmem((D, FF)),
        wdown=vmem((FF, D)),
        xin=vmem((S, FRAMES, plan.pos, D)),
        gin=vmem((S, FRAMES, plan.pos, D)),
        n1=vmem((T, D)),
        qkv=vmem((T, 3 * D)),
        prob=vmem((S * HEADS, L, L)),
        mixed=vmem((T, D)),
        mid=vmem((T, D), F32),
        n2=vmem((T, D)),
        act=vmem((T, FF)),
        slope=vmem((T, FF)),
        obuf=vmem((S, FRAMES, plan.pos, D)),
        acc=vmem((T, D), F32),
        sums=vmem((n_vec, 8, D), F32),
        g_down=vmem((plan.whole, D)),
        g_up=vmem((plan.whole, D)),
        vbuf=vmem((n_steps + 1, vec_rows, D), F32),
        vrecv=vmem((n_steps, vec_rows, D), F32),
        small_rows=[vmem((1, item.size), F32) for item in small],
        gsrc=vmem(token_shape),
        load_sems=pltpu.SemaphoreType.DMA((4,)),
        grad_sems=pltpu.SemaphoreType.DMA((plan.rows,)),
        a2a_send=pltpu.SemaphoreType.DMA((4, S, plan.F)),
        a2a_recv=pltpu.SemaphoreType.DMA((4, S, plan.F)),
        rs_send=pltpu.SemaphoreType.DMA((n_parts, n_hops)),
        rs_recv=pltpu.SemaphoreType.DMA((n_parts, n_hops)),
        v_send=pltpu.SemaphoreType.DMA((n_steps,)),
        v_recv=pltpu.SemaphoreType.DMA((n_steps,)),
        slots=[
            vmem((3, plan.whole >> (i + 1), D)) for i in range(n_steps)
        ],
    )

    def kernel(stream, grad, wqkv, wout, wup, wdown, mask, *rest):
        count = len(small)
        refs = SimpleNamespace(
            stream=stream,
            grad=grad,
            from_hbm=(wqkv, wout, wup, wdown),
            mask=mask,
            small=rest[:count],
        )
        refs.out_h, refs.ig_h, refs.res, refs.vec = rest[count : count + 4]
        vars(refs).update(rest[count + 4])
        refs.groups = (refs.g_down, refs.g_up, refs.wdown)
        refs.group_slots = [[slot.at[group] for slot in refs.slots] for group in range(3)]
        layer_kernel(plan, refs)

    hbm = pl.BlockSpec(memory_space=pl.ANY)
    in_vmem = pl.BlockSpec(memory_space=pltpu.VMEM)
    return pl.pallas_call(
        kernel,
        out_shape=(
            jax.ShapeDtypeStruct(token_shape, BF16),
            jax.ShapeDtypeStruct(token_shape, BF16),
            jax.ShapeDtypeStruct((3, plan.C * plan.R, D), BF16),
            jax.ShapeDtypeStruct((vec_rows, D), F32),
        ),
        in_specs=[hbm] * 6 + [in_vmem] * (1 + len(small)),
        out_specs=(hbm, hbm, in_vmem, in_vmem),
        scratch_shapes=(scratch,),
        compiler_params=pltpu.CompilerParams(
            collective_id=0, has_side_effects=True, vmem_limit_bytes=VMEM_LIMIT
        ),
        name="tube_layer",
    )(
        stream.reshape(token_shape),
        out_grad.reshape(token_shape),
        *weights,
        token_mask,
        *small,
    )


VMEM_LIMIT = 64 * 1024 * 1024 - 512 * 1024


def finish_kernel(plan, out_s, ig_s, res_h, vec_h, out_d, ig_d, *refs):
    C, R, D = plan.C, plan.R, plan.D
    qkv_d, up_d, proj_d, down_d = refs[:4]
    vectors_d, statistics_d = refs[4:12], refs[12]
    qkv_v, up_v, proj_v, down_v, res, vec, out_v, ig_v = refs[13:21]
    vectors, statistics, sems = refs[21:29], refs[29], refs[30]
    moves = [(res_h.at[group], res.at[group]) for group in range(3)]
    moves += [(vec_h, vec), (out_s, out_v), (ig_s, ig_v)]
    copies = [pltpu.make_async_copy(*move, sems.at[i]) for i, move in enumerate(moves)]
    for i in (3, 0, 1, 2, 4, 5):
        copies[i].start()

    def write(value, target):
        copy = pltpu.make_async_copy(value, target, sems.at[len(copies)])
        copy.start()
        copies.append(copy)

    def each_piece(group):
        for of_group, _, first, height in plan.parts:
            if of_group == group:
                for chunk in range(C):
                    block = res[group, pl.ds(first * C + chunk * height, height), :]
                    yield chunk, first, height, block.astype(F32)

    copies[3].wait()
    frame = lax.axis_index(FRAME)
    counts = (1, 1, 2, 1, 1, 1, plan.nj, 1)
    firsts = (0, 1, 2, 4, 5, 6, 13, 7)
    for target, count, first in zip(vectors, counts, firsts):
        share = count * D // plan.F
        per_row = plan.F // count
        row = vec[pl.ds(first + frame // per_row, 1), :]
        turned = pltpu.roll(row, lax.rem(D - (frame % per_row) * share, D), 1)
        target[...] = turned[:, :share].reshape(-1)
    squares = jnp.sum(vec[pl.ds(8, 8), :], axis=-1, keepdims=True)
    entries = plan.T * D * C * plan.F
    roots = jnp.sqrt(squares / entries)
    lanes = lax.broadcasted_iota(jnp.int32, (8, 8), 1)
    rows = lax.broadcasted_iota(jnp.int32, (8, 8), 0)
    across = jnp.sum(jnp.where(lanes == rows, roots, 0.0), axis=0, keepdims=True)
    statistics[...] = across[:, :5].reshape(-1)
    for value, target in zip((*vectors, statistics), (*vectors_d, statistics_d)):
        write(value, target)

    copies[0].wait()
    for chunk, first, height, block in each_piece(0):
        down_v[pl.ds(chunk * R + first, height), :] = block
    write(down_v, down_d)
    copies[1].wait()
    for chunk, first, height, block in each_piece(1):
        up_v[pl.ds(first, height), pl.ds(chunk * D, D)] = block
    write(up_v, up_d)
    copies[2].wait()
    for chunk, first, height, block in each_piece(2):
        if chunk < C - 1:
            qkv_v[pl.ds(first, height), pl.ds(chunk * D, D)] = block
        else:
            proj_v[pl.ds(first, height), :] = block
    write(qkv_v, qkv_d)
    write(proj_v, proj_d)
    copies[4].wait()
    write(out_v, out_d)
    copies[5].wait()
    write(ig_v, ig_d)

    for copy in copies[6:]:
        copy.wait()


def finish(plan, output, input_grad, res, vec):
    D, F, C, R = plan.D, plan.F, plan.C, plan.R
    shapes = [(R, 3 * D), (R, C * D), (R, D), (C * R, D)]
    vectors = [(count * D // F,) for count in (1, 1, 2, 1, 1, 1, plan.nj, 1)]
    hbm = pl.BlockSpec(memory_space=pltpu.HBM)
    like = lambda item: jax.ShapeDtypeStruct(item.shape, item.dtype)
    return pl.pallas_call(
        functools.partial(finish_kernel, plan),
        out_shape=tuple(
            [like(output), like(input_grad)]
            + [jax.ShapeDtypeStruct(shape, F32) for shape in shapes + vectors + [(5,)]]
        ),
        in_specs=[hbm] * 4,
        out_specs=(hbm,) * 15,
        scratch_shapes=[pltpu.VMEM(shape, F32) for shape in shapes]
        + [pltpu.VMEM(res.shape, BF16), pltpu.VMEM(vec.shape, F32)]
        + [pltpu.VMEM(output.shape, BF16)] * 2
        + [pltpu.VMEM(shape, F32) for shape in vectors + [(5,)]]
        + [pltpu.SemaphoreType.DMA((21,))],
        compiler_params=pltpu.CompilerParams(vmem_limit_bytes=VMEM_LIMIT),
        name="tube_layer_results",
    )(output, input_grad, res, vec)


def with_kernel(
    plan,
    stream,
    out_grad,
    token_mask,
    ln1_gain,
    ln1_bias,
    w_qkv,
    b_qv,
    w_out,
    b_out,
    ln2_gain,
    ln2_bias,
    w_up,
    b_up,
    w_down,
    b_down,
):
    small = (ln1_gain, ln1_bias, b_qv, b_out, ln2_gain, ln2_bias, b_up, b_down)
    parts = fused(plan, stream, out_grad, token_mask, (w_qkv, w_out, w_up, w_down), small)
    output, input_grad, g_qkv, g_up, g_out, g_down, *vectors, statistics = finish(plan, *parts)
    return (
        output.reshape(stream.shape),
        input_grad.reshape(stream.shape),
        vectors[0],
        vectors[1],
        g_qkv,
        vectors[2],
        g_out,
        vectors[3],
        vectors[4],
        vectors[5],
        g_up,
        vectors[6],
        g_down,
        vectors[7],
        statistics,
    )


def layer_norm(inputs, norm_gain, norm_shift):
    center = jnp.mean(inputs, axis=-1, keepdims=True)
    shifted = inputs - center
    spread = jnp.mean(shifted * shifted, axis=-1, keepdims=True)
    inverse = lax.rsqrt(spread + EPS)
    unit = shifted * inverse
    return (unit * norm_gain + norm_shift, unit, inverse)


def norm_backward(upstream, unit, inverse, norm_gain):
    scaled = upstream * norm_gain
    first = jnp.mean(scaled, axis=-1, keepdims=True)
    second = jnp.mean(scaled * unit, axis=-1, keepdims=True)
    return inverse * (scaled - first - unit * second)


def gelu_slope(hidden_state):
    cumulative = 0.5 * (1.0 + lax.erf(hidden_state * (1.0 / math.sqrt(2.0))))
    density = jnp.exp(-0.5 * hidden_state * hidden_state) * (1.0 / math.sqrt(2.0 * math.pi))
    return cumulative + hidden_state * density


def with_collectives(
    stream,
    out_grad,
    token_mask,
    ln1_gain,
    ln1_bias,
    w_qkv,
    b_qv,
    w_out,
    b_out,
    ln2_gain,
    ln2_bias,
    w_up,
    b_up,
    w_down,
    b_down,
):
    frame_count = lax.axis_size(FRAME)
    clip_count = lax.axis_size(CLIP)
    device_count = clip_count * frame_count
    frame_split = min(FRAMES, frame_count)
    clip_split = frame_count // frame_split
    frames_dev = FRAMES // frame_split
    tubes_dev = TUBES // frame_split
    row_count, spatial, width = stream.shape
    clips_dev = row_count // frames_dev
    clip_sets = clips_dev // clip_split
    tube_pos = spatial // TUBES
    length = FRAMES * tube_pos
    head_dim = width // HEADS
    scale = 1.0 / math.sqrt(head_dim)

    def leaving(tensor):
        return tensor.reshape(frames_dev, clip_sets, frame_count, tubes_dev * tube_pos, width)

    def arranged(tensor):
        tensor = tensor.reshape(clip_split, FRAMES, clip_sets, tubes_dev, tube_pos, width)
        tensor = jnp.transpose(tensor, (0, 2, 3, 1, 4, 5))
        return tensor.reshape(-1, width)

    def restored(tensor):
        tensor = tensor.reshape(clip_split, clip_sets, tubes_dev, FRAMES, tube_pos, width)
        tensor = jnp.transpose(tensor, (0, 3, 1, 2, 4, 5))
        return tensor.reshape(frame_count * frames_dev, clip_sets, 1, tubes_dev * tube_pos, width)

    masked = jnp.where(token_mask[:, :, None] == 1, out_grad, jnp.zeros((), jnp.bfloat16))
    arrived = (
        lax.all_to_all(leaving(stream), FRAME, split_axis=2, concat_axis=0, tiled=True),
        lax.all_to_all(leaving(masked), FRAME, split_axis=2, concat_axis=0, tiled=True),
    )
    inputs = arranged(arrived[0]).astype(jnp.float32)
    grad_y = arranged(arrived[1])
    seq_count = inputs.shape[0] // length

    def split_heads(tensor):
        return tensor.reshape(seq_count, length, HEADS, head_dim)

    def attention_scores(queries, key_part):
        return (
            jnp.einsum("slhe,smhe->shlm", queries, key_part, preferred_element_type=jnp.float32)
            * scale
        )

    first_normed_input, unit_one, inverse_one = layer_norm(inputs, ln1_gain, ln1_bias)
    first_normed_input = first_normed_input.astype(jnp.bfloat16)
    third_bias_term = jnp.concatenate(
        [b_qv[:width], jnp.zeros((width,), jnp.float32), b_qv[width:]]
    )
    query_key_value = (
        jnp.dot(first_normed_input, w_qkv, preferred_element_type=jnp.float32) + third_bias_term
    ).astype(jnp.bfloat16)
    queries = split_heads(query_key_value[:, :width])
    key_part = split_heads(query_key_value[:, width : 2 * width])
    values = split_heads(query_key_value[:, 2 * width :])
    scores = attention_scores(queries, key_part)
    largest = jnp.max(scores, axis=-1, keepdims=True)
    logsum = largest + jnp.log(jnp.sum(jnp.exp(scores - largest), axis=-1, keepdims=True))
    attend_low = jnp.exp(scores - logsum).astype(jnp.bfloat16)
    mixed_heads = jnp.einsum(
        "shlm,smhe->slhe", attend_low, values, preferred_element_type=jnp.float32
    )
    mixed_heads = mixed_heads.reshape(-1, width).astype(jnp.bfloat16)
    attention_branch = jnp.dot(mixed_heads, w_out, preferred_element_type=jnp.float32) + b_out
    middle = inputs + attention_branch
    second_normed_input, unit_two, inverse_two = layer_norm(middle, ln2_gain, ln2_bias)
    second_normed_input = second_normed_input.astype(jnp.bfloat16)
    hidden_state = jnp.dot(second_normed_input, w_up, preferred_element_type=jnp.float32) + b_up
    activated_hidden = jax.nn.gelu(hidden_state, approximate=False).astype(jnp.bfloat16)
    feedforward_branch = (
        jnp.dot(activated_hidden, w_down, preferred_element_type=jnp.float32) + b_down
    )
    result = middle + feedforward_branch
    squares = jnp.stack(
        [
            jnp.sum(inputs * inputs),
            jnp.sum(middle * middle),
            jnp.sum(result * result),
            jnp.sum(attention_branch * attention_branch),
            jnp.sum(feedforward_branch * feedforward_branch),
        ]
    )
    totals = lax.psum(squares, (CLIP, FRAME))
    statistics = jnp.sqrt(totals / (row_count * spatial * width * device_count))
    grad_w_down = jnp.einsum(
        "tf,td->fd", activated_hidden, grad_y, preferred_element_type=jnp.float32
    )
    grad_b_down = jnp.sum(grad_y.astype(jnp.float32), axis=0)
    d_active = jnp.einsum("td,fd->tf", grad_y, w_down, preferred_element_type=jnp.float32)
    d_hidden = (d_active * gelu_slope(hidden_state)).astype(jnp.bfloat16)
    grad_w_up = jnp.einsum(
        "td,tf->df", second_normed_input, d_hidden, preferred_element_type=jnp.float32
    )
    grad_b_up = jnp.sum(d_hidden.astype(jnp.float32), axis=0)
    d_two = jnp.einsum("tf,df->td", d_hidden, w_up, preferred_element_type=jnp.float32)
    grad_ln2_gain = jnp.sum(d_two * unit_two, axis=0)
    grad_ln2_bias = jnp.sum(d_two, axis=0)
    d_middle = grad_y.astype(jnp.float32) + norm_backward(d_two, unit_two, inverse_two, ln2_gain)
    d_branch = d_middle.astype(jnp.bfloat16)
    grad_w_out = jnp.einsum("td,te->de", mixed_heads, d_branch, preferred_element_type=jnp.float32)
    grad_b_out = jnp.sum(d_branch.astype(jnp.float32), axis=0)
    d_mixed = jnp.einsum("te,de->td", d_branch, w_out, preferred_element_type=jnp.float32)
    d_mixed = split_heads(d_mixed.astype(jnp.bfloat16))
    again = attention_scores(queries, key_part)
    attend = jnp.exp(again - logsum)
    attend_again = attend.astype(jnp.bfloat16)
    d_attend = jnp.einsum("slhe,smhe->shlm", d_mixed, values, preferred_element_type=jnp.float32)
    d_values = jnp.einsum(
        "shlm,slhe->smhe", attend_again, d_mixed, preferred_element_type=jnp.float32
    )
    centre_term = jnp.sum(attend * d_attend, axis=-1, keepdims=True)
    d_scores = (attend * (d_attend - centre_term)).astype(jnp.bfloat16)
    d_queries = (
        jnp.einsum("shlm,smhe->slhe", d_scores, key_part, preferred_element_type=jnp.float32)
        * scale
    )
    d_keys = (
        jnp.einsum("shlm,slhe->smhe", d_scores, queries, preferred_element_type=jnp.float32) * scale
    )
    d_qkv = jnp.concatenate(
        [d_queries.reshape(-1, width), d_keys.reshape(-1, width), d_values.reshape(-1, width)],
        axis=1,
    ).astype(jnp.bfloat16)
    grad_w_qkv = jnp.einsum(
        "td,te->de", first_normed_input, d_qkv, preferred_element_type=jnp.float32
    )
    bias_sums = jnp.sum(d_qkv.astype(jnp.float32), axis=0)
    grad_b_qv = jnp.concatenate([bias_sums[:width], bias_sums[2 * width :]])
    d_one = jnp.einsum("te,de->td", d_qkv, w_qkv, preferred_element_type=jnp.float32)
    grad_ln1_gain = jnp.sum(d_one * unit_one, axis=0)
    grad_ln1_bias = jnp.sum(d_one, axis=0)
    d_inputs = d_middle + norm_backward(d_one, unit_one, inverse_one, ln1_gain)
    departed = (
        lax.all_to_all(
            restored(result.astype(jnp.bfloat16)), FRAME, split_axis=0, concat_axis=2, tiled=True
        ),
        lax.all_to_all(
            restored(d_inputs.astype(jnp.bfloat16)),
            FRAME,
            split_axis=0,
            concat_axis=2,
            tiled=True,
        ),
    )
    output = departed[0].reshape(row_count, spatial, width)
    input_grad = departed[1].reshape(row_count, spatial, width)
    gradients = [
        grad_ln1_gain,
        grad_ln1_bias,
        grad_w_qkv,
        grad_b_qv,
        grad_w_out,
        grad_b_out,
        grad_ln2_gain,
        grad_ln2_bias,
        grad_w_up,
        grad_b_up,
        grad_w_down,
        grad_b_down,
    ]
    grouped = jnp.concatenate([item.reshape(frame_count, -1) for item in gradients], axis=1)
    extent_all = grouped.shape[1]
    padding = -extent_all % clip_count
    grouped = jnp.concatenate([grouped, jnp.zeros((frame_count, padding), jnp.float32)], axis=1)
    own_rows = lax.psum_scatter(
        grouped.astype(jnp.bfloat16), FRAME, scatter_dimension=0, tiled=True
    ).astype(jnp.float32)
    summed = lax.psum(own_rows, CLIP).reshape(-1)
    finished = []
    offset = 0
    for item in gradients:
        extent = item.size // frame_count
        local_shape = (item.shape[0] // frame_count,) + item.shape[1:]
        finished.append(summed[offset : offset + extent].reshape(local_shape))
        offset = offset + extent
    return (
        output,
        input_grad,
        finished[0],
        finished[1],
        finished[2],
        finished[3],
        finished[4],
        finished[5],
        finished[6],
        finished[7],
        finished[8],
        finished[9],
        finished[10],
        finished[11],
        statistics,
    )


def solution(mesh):
    clips, frames = mesh.shape[CLIP], mesh.shape[FRAME]

    def on_device(stream, *rest):
        ff = rest[-4].shape[1]
        plan = Plan(clips, frames, stream.shape, ff)
        if plan.fits:
            return with_kernel(plan, stream, *rest)
        return with_collectives(stream, *rest)

    tokens = P((CLIP, FRAME), None, None)
    in_specs = (tokens, tokens, P((CLIP, FRAME), None)) + (P(),) * 12
    rows, vector = P(FRAME, None), P(FRAME)
    out_specs = (
        tokens,
        tokens,
        vector,
        vector,
        rows,
        vector,
        rows,
        vector,
        vector,
        vector,
        rows,
        vector,
        rows,
        vector,
        P(),
    )
    return jax.shard_map(
        on_device, mesh=mesh, in_specs=in_specs, out_specs=out_specs, check_vma=False
    )
```

```python
import functools
import math
from types import SimpleNamespace

import jax
import jax.numpy as jnp
from jax import lax
from jax.experimental import pallas as pl
from jax.experimental.pallas import tpu as pltpu
from jax.sharding import PartitionSpec as P

HEADS = 12
FRAMES = 16
TUBES = 16
EPS = 1e-05

F32 = jnp.float32
BF16 = jnp.bfloat16
MESH = pl.DeviceIdType.MESH
ROW_BLOCK = 32
CLIP = "clip"
FRAME = "frame"


SIXTHS = 6
SHARES = (
    (("zyx", 2), ("xzy", 1), ("yzx", 1), ("yxz", 2),),
    (("xzy", 1), ("xyz", 3), ("yxz", 2),),
    (("xzy", 2), ("xyz", 2), ("yxz", 2),),
)
DUE = dict(
    GU0=(0, 1),
    GU1=(2, 3),
    DT=(4,),
    LB1=(5, 6),
    DO=(1,),
    AB00=(2,),
    AB01=(0,),
    AB10=(4,),
    AB11=(1,),
    GQ0=(2, 3),
    V0=(7, 4, 8, 5, 9, 0, 6, 1),
    V1=(3, 2, 7, 5, 3, 8, 7, 6, 9, 4, 5, 0, 2, 3, 1),
    V2=(6, 9, 7, 8, 4, 0, 2, 3, 2, 1, 5, 4, 7, 3),
    V3=(9, 1, 0, 4, 6, 0, 8, 5, 7, 5, 6, 7),
    V4=(9, 6, 8, 9, 8, 9, 8),
)


def dot_nn(lhs, rhs):
    return lax.dot_general(lhs, rhs, (((1,), (0,)), ((), ())), preferred_element_type=F32)


def dot_nt(lhs, rhs):
    return lax.dot_general(lhs, rhs, (((1,), (1,)), ((), ())), preferred_element_type=F32)


def dot_tn(lhs, rhs):
    return lax.dot_general(lhs, rhs, (((0,), (0,)), ((), ())), preferred_element_type=F32)


def unit_norm(rows):
    shifted = rows - jnp.mean(rows, axis=-1, keepdims=True)
    inverse = lax.rsqrt(jnp.mean(shifted * shifted, axis=-1, keepdims=True) + EPS)
    return shifted * inverse, inverse


def norm_pull(scaled, unit, inverse):
    first = jnp.mean(scaled, axis=-1, keepdims=True)
    second = jnp.mean(scaled * unit, axis=-1, keepdims=True)
    return inverse * (scaled - first - unit * second)


def gelu_and_slope(hidden):
    bell = jnp.exp(hidden * hidden * -0.5)
    t = 1.0 / (1.0 + jnp.abs(hidden) * (0.3275911 / math.sqrt(2.0)))
    poly = t * (
        0.5 * 0.254829592
        + t
        * (
            0.5 * -0.284496736
            + t * (0.5 * 1.421413741 + t * (0.5 * -1.453152027 + t * (0.5 * 1.061405429)))
        )
    )
    below = poly * bell
    cumulative = jnp.where(hidden >= 0.0, 1.0 - below, below)
    return hidden * cumulative, cumulative + hidden * bell * (1.0 / math.sqrt(2.0 * math.pi))


def fold8(rows):
    return jnp.sum(rows.reshape(rows.shape[0] // 8, 8, rows.shape[1]), axis=0)


def ds(start, size, unit=None):
    return pl.ds(pl.multiple_of(start, unit or size), size)


class Plan:
    def __init__(self, clips, frames, stream_shape, ff):
        self.C, self.F, self.FF = clips, frames, ff
        self.rows, self.spatial, self.D = stream_shape
        self.frame_split = min(FRAMES, frames)
        self.clip_split = frames // self.frame_split
        self.fd = FRAMES // self.frame_split
        self.td = TUBES // self.frame_split
        self.cd = self.rows // self.fd
        self.pos = self.spatial // TUBES
        self.L = FRAMES * self.pos
        self.S = self.cd * self.td
        self.T = self.S * self.L
        self.R = self.D // frames
        self.blocks = clips * frames
        self.whole = self.blocks * self.R
        self.parts = []
        for group, shares in enumerate(SHARES):
            first = 0
            for part, (order, share) in enumerate(shares):
                rows = self.R * share // SIXTHS
                self.parts.append((group, order, first, rows))
                first += rows
        self.nj = ff // self.D
        self.X = clips // 2
        self.Y = self.X if frames % self.X == 0 else 1
        powers = all(n & (n - 1) == 0 for n in (clips, frames, self.X, self.Y))
        self.fits = (
            self.clip_split == 1
            and clips >= 4
            and powers
            and frames % 2 == 0
            and self.R % (16 * SIXTHS) == 0
            and ff == clips * self.D
            and self.pos % 16 == 0
            and self.D % (ff // frames) == 0
        )

    def steps(self, order):
        bits = lambda n: [1 << i for i in range(n.bit_length() - 1)]
        along = dict(
            x=[(CLIP, 2 * b) for b in bits(self.X)],
            y=[(FRAME, b) for b in bits(self.Y)],
            z=[(FRAME, self.Y * b) for b in bits(self.F // self.Y)],
        )
        return [(CLIP, 1)] + along[order[0]] + along[order[1]] + along[order[2]]

    def peer_order(self):
        return range(self.F - 1, -1, -1)

    def gather_steps(self):
        return [(CLIP, 2 * (1 << i)) for i in range(self.X.bit_length() - 1)] + [(CLIP, 1)]

    def place(self, order, chunk, frame):
        clip = (chunk % self.X) * 2 + chunk // self.X
        where = 0
        for axis, bit in self.steps(order):
            where = where * 2 + ((clip if axis == CLIP else frame) // bit) % 2
        return where


class Scatter:
    def __init__(self, plan, me, part, held, slots, results, send_sems, recv_sems):
        group, order, first, self.height = plan.parts[part]
        self.plan, self.me = plan, me
        self.steps = plan.steps(order)
        self.gather = plan.gather_steps()
        rows = lambda count, per: pl.ds(first * per, count * per)
        self.held = held.at[rows(self.height, plan.blocks)]
        self.slots = [
            slot.at[rows(self.height, plan.blocks >> (i + 1))] for i, slot in enumerate(slots)
        ]
        self.result = results.at[rows(self.height, plan.C)]
        self.send_sems, self.recv_sems = send_sems.at[part], recv_sems.at[part]
        self.at = 0
        self.base = 0
        self.size = plan.blocks
        self.copies = []
        self.slot_of_me = (me[CLIP] % 2) * plan.X + me[CLIP] // 2

    def bit_of(self, axis, bit):
        return (self.me[axis] // bit) % 2

    def partner(self, axis, bit):
        flipped = self.me[axis] + bit * (1 - 2 * self.bit_of(axis, bit))
        return {**self.me, axis: flipped}

    def rows(self, base, size):
        return pl.ds(pl.multiple_of(base * self.height, self.height), size * self.height)

    def send(self, src, dst, axis, bit):
        to = self.partner(axis, bit)
        copy = pltpu.make_async_remote_copy(
            src_ref=src,
            dst_ref=dst,
            send_sem=self.send_sems.at[len(self.copies)],
            recv_sem=self.recv_sems.at[len(self.copies)],
            device_id=(to[CLIP], to[FRAME]),
            device_id_type=MESH,
        )
        copy.start()
        self.copies.append(copy)

    def start(self):
        if self.at < len(self.steps):
            axis, bit = self.steps[self.at]
            mine = self.bit_of(axis, bit)
            half = self.size // 2
            self.send(
                self.held.at[self.rows(self.base + (1 - mine) * half, half)],
                self.slots[self.at],
                axis,
                bit,
            )
            self.base = self.base + mine * half
            self.size = half
        elif self.at < len(self.steps) + len(self.gather):
            done = self.at - len(self.steps)
            axis, bit = self.gather[done]
            size = 1 << done
            region = self.rows((self.slot_of_me // size) * size, size)
            self.send(self.result.at[region], self.result.at[region], axis, bit)

    def advance(self):
        self.copies[self.at].wait_recv()
        if self.at < len(self.steps):
            slot = self.slots[self.at]
            last = self.at == len(self.steps) - 1
            target = self.result if last else self.held
            target_base = self.slot_of_me if last else self.base
            base, held = self.base, self.held

            def add(i, _):
                total = held[self.rows(base + i, 1)].astype(F32) + slot[self.rows(i, 1)].astype(F32)
                target[self.rows(target_base + i, 1)] = total.astype(BF16)
                return 0

            lax.fori_loop(0, self.size, add, 0)
        self.at += 1
        self.start()

    def done(self):
        return self.at == len(self.steps) + len(self.gather)

    def finish(self):
        assert self.done()
        for copy in self.copies:
            copy.wait_send()


def flipped_bits(index, bits):
    for b in range(bits.bit_length()):
        if bits >> b & 1:
            index = index + (1 << b) * (1 - 2 * ((index // (1 << b)) % 2))
    return index


def layer_kernel(plan, refs):
    D, T, S, L, FF, nj = plan.D, plan.T, plan.S, plan.L, plan.FF, plan.nj
    me = {CLIP: lax.axis_index(CLIP), FRAME: lax.axis_index(FRAME)}
    frame = me[FRAME]
    xin, gin, n1, qkv, prob, mixed = refs.xin, refs.gin, refs.n1, refs.qkv, refs.prob, refs.mixed
    mid, n2, act, slope, obuf, acc = refs.mid, refs.n2, refs.act, refs.slope, refs.obuf, refs.acc
    sums = refs.sums
    for source, target in zip(refs.small, refs.small_rows):
        target[...] = source[...].reshape(1, -1)
    ln1_gain, ln1_bias, b_qv, b_out, ln2_gain, ln2_bias, b_up, b_down = refs.small_rows
    wqkv, wout, wup, wdown = refs.wqkv, refs.wout, refs.wup, refs.wdown
    dbranch, dmixed, igbuf, dmid = n2, mixed, obuf, mid

    barrier = pltpu.get_barrier_semaphore()
    greeted = [(me[CLIP], lax.rem(frame + i, plan.F)) for i in range(1, plan.F)]
    for axis, bit in plan.gather_steps():
        flipped = me[axis] + bit * (1 - 2 * ((me[axis] // bit) % 2))
        greeted.append((flipped, frame))
    for peer in greeted:
        pl.semaphore_signal(barrier, inc=1, device_id=peer, device_id_type=MESH)
    pl.semaphore_wait(barrier, len(greeted))

    def tubes(n, device):
        clip_set, tube = n // plan.td, n % plan.td
        return clip_set, ds((device * plan.td + tube) * plan.pos, plan.pos)

    sends = []

    def to_tubes(which, source, target, n):
        arriving = []
        for i in plan.peer_order():
            peer = flipped_bits(frame, i)
            clip_set, positions = tubes(n, peer)
            src = source.at[:, clip_set, positions]
            dst = target.at[n, pl.ds(frame * plan.fd, plan.fd)]
            recv = refs.a2a_recv.at[which, n, i]
            if i == 0:
                copy = pltpu.make_async_copy(src, dst, recv)
                copy.start()
                arriving.append(copy.wait)
            else:
                copy = pltpu.make_async_remote_copy(
                    src_ref=src,
                    dst_ref=dst,
                    send_sem=refs.a2a_send.at[which, n, i],
                    recv_sem=recv,
                    device_id=(me[CLIP], peer),
                    device_id_type=MESH,
                )
                copy.start()
                sends.append(copy.wait_send)
                arriving.append(copy.wait_recv)
        return arriving

    def to_frames(which, source, target, n):
        arriving = []
        for i in plan.peer_order():
            peer = flipped_bits(frame, i)
            clip_set, positions = tubes(n, frame)
            src = source.at[n, pl.ds(peer * plan.fd, plan.fd)]
            dst = target.at[:, clip_set, positions]
            recv = refs.a2a_recv.at[which, n, i]
            if i == 0:
                copy = pltpu.make_async_copy(src, dst, recv)
                copy.start()
                arriving.append((lambda: None, copy.wait))
            else:
                copy = pltpu.make_async_remote_copy(
                    src_ref=src,
                    dst_ref=dst,
                    send_sem=refs.a2a_send.at[which, n, i],
                    recv_sem=recv,
                    device_id=(me[CLIP], peer),
                    device_id_type=MESH,
                )
                copy.start()
                arriving.append((copy.wait_recv, copy.wait_send))
        return arriving

    def wait_all(waits):
        for wait in waits:
            wait()

    x_arrives = [to_tubes(0, refs.stream, xin, 0)]
    g_arrives = []

    loads = []
    for i, (src, dst) in enumerate(zip(refs.from_hbm, (wqkv, wout, wup, wdown))):
        load = pltpu.make_async_copy(src, dst, refs.load_sems.at[i])
        load.start()
        loads.append(load)

    raw = n2
    grad_loads = []
    for r in range(plan.rows):
        grad_load = pltpu.make_async_copy(
            refs.grad.at[r // plan.cd, r % plan.cd],
            raw.at[pl.ds(r * plan.spatial, plan.spatial)],
            refs.grad_sems.at[r],
        )
        grad_load.start()
        grad_loads.append(grad_load.wait)
    wait_all(grad_loads)
    places = (plan.spatial, plan.spatial)
    diagonal = lax.broadcasted_iota(jnp.int32, places, 0) == lax.broadcasted_iota(
        jnp.int32, places, 1
    )
    for r in range(plan.rows):
        kept = refs.mask[pl.ds(r, 1), :] == 1
        keep = jnp.where(diagonal & kept, 1.0, 0.0).astype(BF16)
        rows = dot_nn(keep, raw[pl.ds(r * plan.spatial, plan.spatial), :])
        refs.gsrc[r // plan.cd, r % plan.cd] = rows.astype(BF16)
    for n in range(1, S):
        wait_all(sends)
        sends.clear()
        x_arrives.append(to_tubes(0, refs.stream, xin, n))

    scatters = [
        Scatter(
            plan,
            me,
            part,
            refs.groups[group],
            refs.group_slots[group],
            refs.res.at[group],
            refs.rs_send,
            refs.rs_recv,
        )
        for part, (group, *_) in enumerate(plan.parts)
    ]

    def start(group):
        for part, scatter in enumerate(scatters):
            if plan.parts[part][0] == group:
                scatter.start()

    def tick(name):
        for part in DUE.get(name, ()):
            if part < len(scatters) and scatters[part].copies and not scatters[part].done():
                scatters[part].advance()

    def pieces(name, count, total, body, unroll=1):
        for i in range(count):
            lax.fori_loop(total * i // count, total * (i + 1) // count, body, 0, unroll=unroll)
            tick(name + str(i))

    def seq_rows(ref, s, start, size):
        frames = size // plan.pos
        block = ref[s, pl.ds(start // plan.pos, frames)]
        return block.reshape(size, D)

    sums[...] = jnp.zeros_like(sums)

    def tally(i, value):
        sums[i] += fold8(value)

    lanes = lax.broadcasted_iota(jnp.int32, (1, 128), 1)
    head_masks = [(lanes < 64).astype(BF16), (lanes >= 64).astype(BF16)]

    scale = 1.0 / math.sqrt(D // HEADS)

    def head_columns(pair):
        at = pair * 128
        return tuple(ds(first + at, 128) for first in (0, 0, D, 2 * D))

    for s in range(S):
        wait_all(x_arrives[s])
        if s == S - 1:
            g_arrives += [to_tubes(1, refs.gsrc, gin, n) for n in range(S)]

        def first_norm(i, _):
            x = seq_rows(xin, s, i * ROW_BLOCK, ROW_BLOCK).astype(F32)
            unit, _ = unit_norm(x)
            tally(8, x * x)
            n1[ds(s * L + i * ROW_BLOCK, ROW_BLOCK), :] = (unit * ln1_gain[...] + ln1_bias[...]).astype(BF16)
            return 0

        lax.fori_loop(0, L // ROW_BLOCK, first_norm, 0)
        if s == 0:
            loads[0].wait()
        tokens = pl.ds(s * L, L)
        for third in range(3):
            columns = pl.ds(third * D, D)
            out = dot_nn(n1[tokens, :], wqkv[:, columns])
            if third != 1:
                out = out + b_qv[:, pl.ds(third // 2 * D, D)]
            if third == 0:
                out = out * scale
            qkv[tokens, columns] = out.astype(BF16)

        def attend(pair, _):
            columns, q_at, k_at, v_at = head_columns(pair)
            q, k, v = qkv[tokens, q_at], qkv[tokens, k_at], qkv[tokens, v_at]
            out = jnp.zeros((L, 128), F32)
            for e in range(2):
                scores = dot_nt(q * head_masks[e], k)
                power = jnp.exp(scores - jnp.max(scores, axis=-1, keepdims=True))
                share = 1.0 / jnp.sum(power, axis=-1, keepdims=True)
                weight = (power * share).astype(BF16)
                prob[s * HEADS + pair * 2 + e] = weight
                out = out + dot_nn(weight, v * head_masks[e])
            mixed[tokens, columns] = out.astype(BF16)
            return 0

        lax.fori_loop(0, HEADS // 2, attend, 0, unroll=3)

    loads[1].wait()

    mid[...] = dot_nn(mixed[...], wout[...]) + b_out[...]
    for s in range(S):

        def second_norm(i, _):
            rows = ds(s * L + i * ROW_BLOCK, ROW_BLOCK)
            branch = mid[rows, :]
            middle = seq_rows(xin, s, i * ROW_BLOCK, ROW_BLOCK).astype(F32) + branch
            mid[rows, :] = middle
            tally(9, middle * middle)
            tally(11, branch * branch)
            unit, _ = unit_norm(middle)
            n2[rows, :] = (unit * ln2_gain[...] + ln2_bias[...]).astype(BF16)
            return 0

        lax.fori_loop(0, L // ROW_BLOCK, second_norm, 0)

    loads[2].wait()

    def up(i, _):
        columns = ds(i * D, D)
        hidden = dot_nn(n2[...], wup[:, columns]) + b_up[:, columns]
        active, steep = gelu_and_slope(hidden)
        act[:, columns] = active.astype(BF16)
        slope[:, columns] = steep.astype(BF16)
        return 0

    lax.fori_loop(0, nj, up, 0)
    loads[3].wait()
    out_arrives = []
    for s in range(S):
        tokens = pl.ds(s * L, L)
        branch = dot_nn(act[tokens, :], wdown[...]) + b_down[...]
        result = branch + mid[tokens, :]
        tally(10, result * result)
        tally(12, branch * branch)
        obuf[s] = result.astype(BF16).reshape(FRAMES, plan.pos, D)
        out_arrives += to_frames(2, obuf, refs.out_h, s)

    for s in range(S):
        wait_all(g_arrives[s])
    wait_all(sends)
    sends.clear()
    def put(group, chunk, frame_block, block):
        for of_group, order, first, height in plan.parts:
            if of_group == group:
                at = plan.place(order, chunk, frame_block)
                rows = pl.multiple_of(first * plan.blocks + at * height, 16)
                piece = block[first : first + height]
                refs.groups[group][pl.ds(rows, height), :] = piece.astype(BF16)

    def grad_down(i, _):
        out = dot_tn(act[:, ds(i * D, D)], gin[...].reshape(T, D))
        share = FF // plan.F
        for n in range(D // plan.R):
            place = n * plan.R
            frames = D // share
            chunk = place % share // plan.R
            put(0, chunk, i * frames + place // share, out[place : place + plan.R])
        return 0

    pieces("GD", nj, nj, grad_down)
    start(0)

    def through_gelu(i, _):
        columns = ds(i * D, D)
        d_active = dot_nt(gin[...].reshape(T, D), wdown[columns, :])
        d_hidden = (d_active * slope[:, columns].astype(F32)).astype(BF16)
        slope[:, columns] = d_hidden
        sums[13 + i] += fold8(d_hidden.astype(F32))
        return 0

    pieces("TG", nj, nj, through_gelu)

    def grad_columns(group, chunk, lhs, rhs):
        out = dot_tn(lhs, rhs)
        for f in range(plan.F):
            put(group, chunk, f, out[f * plan.R : (f + 1) * plan.R])

    core = lax.rem(me[CLIP], 2)

    def grad_up(i, _):
        c = lax.rem((1 - core) * plan.X + i, plan.C)
        grad_columns(1, c, n2[...], slope[:, ds(c * D, D)])
        return 0

    lax.fori_loop(0, plan.X, grad_up, 0)
    tick("GU0")
    start(1)
    lax.fori_loop(plan.X, plan.C, grad_up, 0)
    tick("GU1")
    acc[...] = dot_nt(slope[...], wup[...])
    tick("DT")

    for s in range(S):

        def second_norm_back(i, _):
            rows = ds(s * L + i * ROW_BLOCK, ROW_BLOCK)
            up_grad = acc[rows, :]
            unit, inverse = unit_norm(mid[rows, :])
            g = seq_rows(gin, s, i * ROW_BLOCK, ROW_BLOCK).astype(F32)
            d_middle = g + norm_pull(up_grad * ln2_gain[...], unit, inverse)
            dmid[rows, :] = d_middle
            low = d_middle.astype(BF16)
            dbranch[rows, :] = low
            tally(4, low.astype(F32))
            tally(5, up_grad * unit)
            tally(6, up_grad)
            tally(7, g)
            return 0

        lax.fori_loop(0, L // ROW_BLOCK, second_norm_back, 0)
        tick("LB" + str(s))

    grad_columns(2, plan.C - 1, mixed[...], dbranch[...])
    tick("DO")
    dmixed[...] = dot_nt(dbranch[...], wout[...]).astype(BF16)
    tick("DM")

    for s in range(S):
        tokens = pl.ds(s * L, L)

        def attend_back(pair, _):
            columns, q_at, k_at, v_at = head_columns(pair)
            q, k, v = qkv[tokens, q_at], qkv[tokens, k_at], qkv[tokens, v_at]
            d_out = dmixed[tokens, columns]
            zero = jnp.zeros((L, 128), F32)
            d_q, d_k, d_v = zero, zero, zero
            for e in range(2):
                weight = prob[s * HEADS + pair * 2 + e]
                own = d_out * head_masks[e]
                d_weight = dot_nt(own, v)
                d_v = d_v + dot_tn(weight, own)
                wide_weight = weight.astype(F32)
                centre = jnp.sum(wide_weight * d_weight, axis=-1, keepdims=True)
                d_score = (wide_weight * (d_weight - centre)).astype(BF16)
                d_q = d_q + dot_nn(d_score, k * head_masks[e])
                d_k = d_k + dot_tn(d_score, q * head_masks[e])
            qkv[tokens, q_at] = (d_q * scale).astype(BF16)
            qkv[tokens, k_at] = d_k.astype(BF16)
            qkv[tokens, v_at] = d_v.astype(BF16)
            return 0

        pieces("AB" + str(s), 2, HEADS // 2, attend_back, unroll=3)

    def grad_qkv(i, _):
        c = core * i + (1 - core) * lax.rem(plan.X + i + (i + 1) // plan.X, plan.C)
        grad_columns(2, c, n1[...], qkv[:, ds(c * D, D)])
        return 0

    lax.fori_loop(0, plan.X, grad_qkv, 0)
    tick("GQ0")
    start(2)
    lax.fori_loop(plan.X, plan.C - 1, grad_qkv, 0)
    tick("GQ1")
    acc[...] = dot_nt(qkv[...], wqkv[...])
    tick("D1")
    for recv, send in out_arrives:
        send()
    in_arrives = []
    for s in range(S):

        def first_norm_back(i, _):
            rows = ds(s * L + i * ROW_BLOCK, ROW_BLOCK)
            up_grad = acc[rows, :]
            x = seq_rows(xin, s, i * ROW_BLOCK, ROW_BLOCK).astype(F32)
            unit, inverse = unit_norm(x)
            total = dmid[rows, :] + norm_pull(up_grad * ln1_gain[...], unit, inverse)
            frames = ROW_BLOCK // plan.pos
            igbuf[s, pl.ds(i * frames, frames)] = total.astype(BF16).reshape(frames, plan.pos, D)
            tally(0, up_grad * unit)
            tally(1, up_grad)
            tally(2, qkv[rows, pl.ds(0, D)].astype(F32))
            tally(3, qkv[rows, pl.ds(2 * D, D)].astype(F32))
            return 0

        lax.fori_loop(0, L // ROW_BLOCK, first_norm_back, 0)
        in_arrives += to_frames(3, igbuf, refs.ig_h, s)
        tick("L1" + str(s))

    vbuf, vrecv = refs.vbuf, refs.vrecv
    count = sums.shape[0]
    for i in range(count):
        vbuf[0, pl.ds(i, 1), :] = jnp.sum(sums[i], axis=0, keepdims=True)
    hops = plan.steps("xyz")
    small = []
    for i, (axis, bit) in enumerate(hops):
        flipped = me[axis] + bit * (1 - 2 * ((me[axis] // bit) % 2))
        to = {**me, axis: flipped}
        copy = pltpu.make_async_remote_copy(
            src_ref=vbuf.at[i],
            dst_ref=vrecv.at[i],
            send_sem=refs.v_send.at[i],
            recv_sem=refs.v_recv.at[i],
            device_id=(to[CLIP], to[FRAME]),
            device_id_type=MESH,
        )
        copy.start()
        small.append(copy)
        tick("V" + str(i))
        copy.wait_recv()
        vbuf[i + 1] = vbuf[i] + vrecv[i]
    refs.vec[...] = vbuf[len(hops)]
    for copy in small:
        copy.wait_send()
    tick("END")
    while not all(scatter.done() for scatter in scatters):
        for scatter in scatters:
            if not scatter.done():
                scatter.advance()
    for scatter in scatters:
        scatter.finish()
    for recv, send in out_arrives:
        recv()
    for recv, send in in_arrives:
        send()
        recv()
    wait_all(sends)


def fused(plan, stream, out_grad, token_mask, weights, small):
    D, T, S, L, FF = plan.D, plan.T, plan.S, plan.L, plan.FF
    n_steps = len(plan.steps("xyz"))
    n_parts = len(plan.parts)
    n_hops = n_steps + len(plan.gather_steps())
    n_vec = 13 + plan.nj
    vec_rows = -(-n_vec // 8) * 8
    vmem = lambda shape, kind=BF16: pltpu.VMEM(shape, kind)
    token_shape = (plan.fd, plan.cd, plan.spatial, D)
    scratch = dict(
        wqkv=vmem((D, 3 * D)),
        wout=vmem((D, D)),
        wup=vmem((D, FF)),
        wdown=vmem((FF, D)),
        xin=vmem((S, FRAMES, plan.pos, D)),
        gin=vmem((S, FRAMES, plan.pos, D)),
        n1=vmem((T, D)),
        qkv=vmem((T, 3 * D)),
        prob=vmem((S * HEADS, L, L)),
        mixed=vmem((T, D)),
        mid=vmem((T, D), F32),
        n2=vmem((T, D)),
        act=vmem((T, FF)),
        slope=vmem((T, FF)),
        obuf=vmem((S, FRAMES, plan.pos, D)),
        acc=vmem((T, D), F32),
        sums=vmem((n_vec, 8, D), F32),
        g_down=vmem((plan.whole, D)),
        g_up=vmem((plan.whole, D)),
        vbuf=vmem((n_steps + 1, vec_rows, D), F32),
        vrecv=vmem((n_steps, vec_rows, D), F32),
        small_rows=[vmem((1, item.size), F32) for item in small],
        gsrc=vmem(token_shape),
        load_sems=pltpu.SemaphoreType.DMA((4,)),
        grad_sems=pltpu.SemaphoreType.DMA((plan.rows,)),
        a2a_send=pltpu.SemaphoreType.DMA((4, S, plan.F)),
        a2a_recv=pltpu.SemaphoreType.DMA((4, S, plan.F)),
        rs_send=pltpu.SemaphoreType.DMA((n_parts, n_hops)),
        rs_recv=pltpu.SemaphoreType.DMA((n_parts, n_hops)),
        v_send=pltpu.SemaphoreType.DMA((n_steps,)),
        v_recv=pltpu.SemaphoreType.DMA((n_steps,)),
        slots=[
            vmem((3, plan.whole >> (i + 1), D)) for i in range(n_steps)
        ],
    )

    def kernel(stream, grad, wqkv, wout, wup, wdown, mask, *rest):
        count = len(small)
        refs = SimpleNamespace(
            stream=stream,
            grad=grad,
            from_hbm=(wqkv, wout, wup, wdown),
            mask=mask,
            small=rest[:count],
        )
        refs.out_h, refs.ig_h, refs.res, refs.vec = rest[count : count + 4]
        vars(refs).update(rest[count + 4])
        refs.groups = (refs.g_down, refs.g_up, refs.wdown)
        refs.group_slots = [[slot.at[group] for slot in refs.slots] for group in range(3)]
        layer_kernel(plan, refs)

    hbm = pl.BlockSpec(memory_space=pl.ANY)
    in_vmem = pl.BlockSpec(memory_space=pltpu.VMEM)
    return pl.pallas_call(
        kernel,
        out_shape=(
            jax.ShapeDtypeStruct(token_shape, BF16),
            jax.ShapeDtypeStruct(token_shape, BF16),
            jax.ShapeDtypeStruct((3, plan.C * plan.R, D), BF16),
            jax.ShapeDtypeStruct((vec_rows, D), F32),
        ),
        in_specs=[hbm] * 6 + [in_vmem] * (1 + len(small)),
        out_specs=(hbm, hbm, in_vmem, in_vmem),
        scratch_shapes=(scratch,),
        compiler_params=pltpu.CompilerParams(
            collective_id=0, has_side_effects=True, vmem_limit_bytes=VMEM_LIMIT
        ),
        name="tube_layer",
    )(
        stream.reshape(token_shape),
        out_grad.reshape(token_shape),
        *weights,
        token_mask,
        *small,
    )


VMEM_LIMIT = 64 * 1024 * 1024 - 512 * 1024


def finish_kernel(plan, out_s, ig_s, res_h, vec_h, out_d, ig_d, *refs):
    C, R, D = plan.C, plan.R, plan.D
    qkv_d, up_d, proj_d, down_d = refs[:4]
    vectors_d, statistics_d = refs[4:12], refs[12]
    qkv_v, up_v, proj_v, down_v, res, vec, out_v, ig_v = refs[13:21]
    vectors, statistics, sems = refs[21:29], refs[29], refs[30]
    moves = [(res_h.at[group], res.at[group]) for group in range(3)]
    moves += [(vec_h, vec), (out_s, out_v), (ig_s, ig_v)]
    copies = [pltpu.make_async_copy(*move, sems.at[i]) for i, move in enumerate(moves)]
    for i in (3, 0, 1, 2, 4, 5):
        copies[i].start()

    def write(value, target):
        copy = pltpu.make_async_copy(value, target, sems.at[len(copies)])
        copy.start()
        copies.append(copy)

    def each_piece(group):
        for of_group, _, first, height in plan.parts:
            if of_group == group:
                for chunk in range(C):
                    block = res[group, pl.ds(first * C + chunk * height, height), :]
                    yield chunk, first, height, block.astype(F32)

    copies[3].wait()
    frame = lax.axis_index(FRAME)
    counts = (1, 1, 2, 1, 1, 1, plan.nj, 1)
    firsts = (0, 1, 2, 4, 5, 6, 13, 7)
    for target, count, first in zip(vectors, counts, firsts):
        share = count * D // plan.F
        per_row = plan.F // count
        row = vec[pl.ds(first + frame // per_row, 1), :]
        turned = pltpu.roll(row, lax.rem(D - (frame % per_row) * share, D), 1)
        target[...] = turned[:, :share].reshape(-1)
    squares = jnp.sum(vec[pl.ds(8, 8), :], axis=-1, keepdims=True)
    entries = plan.T * D * C * plan.F
    roots = jnp.sqrt(squares / entries)
    lanes = lax.broadcasted_iota(jnp.int32, (8, 8), 1)
    rows = lax.broadcasted_iota(jnp.int32, (8, 8), 0)
    across = jnp.sum(jnp.where(lanes == rows, roots, 0.0), axis=0, keepdims=True)
    statistics[...] = across[:, :5].reshape(-1)
    for value, target in zip((*vectors, statistics), (*vectors_d, statistics_d)):
        write(value, target)

    copies[0].wait()
    for chunk, first, height, block in each_piece(0):
        down_v[pl.ds(chunk * R + first, height), :] = block
    write(down_v, down_d)
    copies[1].wait()
    for chunk, first, height, block in each_piece(1):
        up_v[pl.ds(first, height), pl.ds(chunk * D, D)] = block
    write(up_v, up_d)
    copies[2].wait()
    for chunk, first, height, block in each_piece(2):
        if chunk < C - 1:
            qkv_v[pl.ds(first, height), pl.ds(chunk * D, D)] = block
        else:
            proj_v[pl.ds(first, height), :] = block
    write(qkv_v, qkv_d)
    write(proj_v, proj_d)
    copies[4].wait()
    write(out_v, out_d)
    copies[5].wait()
    write(ig_v, ig_d)

    for copy in copies[6:]:
        copy.wait()


def finish(plan, output, input_grad, res, vec):
    D, F, C, R = plan.D, plan.F, plan.C, plan.R
    shapes = [(R, 3 * D), (R, C * D), (R, D), (C * R, D)]
    vectors = [(count * D // F,) for count in (1, 1, 2, 1, 1, 1, plan.nj, 1)]
    hbm = pl.BlockSpec(memory_space=pltpu.HBM)
    like = lambda item: jax.ShapeDtypeStruct(item.shape, item.dtype)
    return pl.pallas_call(
        functools.partial(finish_kernel, plan),
        out_shape=tuple(
            [like(output), like(input_grad)]
            + [jax.ShapeDtypeStruct(shape, F32) for shape in shapes + vectors + [(5,)]]
        ),
        in_specs=[hbm] * 4,
        out_specs=(hbm,) * 15,
        scratch_shapes=[pltpu.VMEM(shape, F32) for shape in shapes]
        + [pltpu.VMEM(res.shape, BF16), pltpu.VMEM(vec.shape, F32)]
        + [pltpu.VMEM(output.shape, BF16)] * 2
        + [pltpu.VMEM(shape, F32) for shape in vectors + [(5,)]]
        + [pltpu.SemaphoreType.DMA((21,))],
        compiler_params=pltpu.CompilerParams(vmem_limit_bytes=VMEM_LIMIT),
        name="tube_layer_results",
    )(output, input_grad, res, vec)


def with_kernel(
    plan,
    stream,
    out_grad,
    token_mask,
    ln1_gain,
    ln1_bias,
    w_qkv,
    b_qv,
    w_out,
    b_out,
    ln2_gain,
    ln2_bias,
    w_up,
    b_up,
    w_down,
    b_down,
):
    small = (ln1_gain, ln1_bias, b_qv, b_out, ln2_gain, ln2_bias, b_up, b_down)
    parts = fused(plan, stream, out_grad, token_mask, (w_qkv, w_out, w_up, w_down), small)
    output, input_grad, g_qkv, g_up, g_out, g_down, *vectors, statistics = finish(plan, *parts)
    return (
        output.reshape(stream.shape),
        input_grad.reshape(stream.shape),
        vectors[0],
        vectors[1],
        g_qkv,
        vectors[2],
        g_out,
        vectors[3],
        vectors[4],
        vectors[5],
        g_up,
        vectors[6],
        g_down,
        vectors[7],
        statistics,
    )


def layer_norm(inputs, norm_gain, norm_shift):
    center = jnp.mean(inputs, axis=-1, keepdims=True)
    shifted = inputs - center
    spread = jnp.mean(shifted * shifted, axis=-1, keepdims=True)
    inverse = lax.rsqrt(spread + EPS)
    unit = shifted * inverse
    return (unit * norm_gain + norm_shift, unit, inverse)


def norm_backward(upstream, unit, inverse, norm_gain):
    scaled = upstream * norm_gain
    first = jnp.mean(scaled, axis=-1, keepdims=True)
    second = jnp.mean(scaled * unit, axis=-1, keepdims=True)
    return inverse * (scaled - first - unit * second)


def gelu_slope(hidden_state):
    cumulative = 0.5 * (1.0 + lax.erf(hidden_state * (1.0 / math.sqrt(2.0))))
    density = jnp.exp(-0.5 * hidden_state * hidden_state) * (1.0 / math.sqrt(2.0 * math.pi))
    return cumulative + hidden_state * density


def with_collectives(
    stream,
    out_grad,
    token_mask,
    ln1_gain,
    ln1_bias,
    w_qkv,
    b_qv,
    w_out,
    b_out,
    ln2_gain,
    ln2_bias,
    w_up,
    b_up,
    w_down,
    b_down,
):
    frame_count = lax.axis_size(FRAME)
    clip_count = lax.axis_size(CLIP)
    device_count = clip_count * frame_count
    frame_split = min(FRAMES, frame_count)
    clip_split = frame_count // frame_split
    frames_dev = FRAMES // frame_split
    tubes_dev = TUBES // frame_split
    row_count, spatial, width = stream.shape
    clips_dev = row_count // frames_dev
    clip_sets = clips_dev // clip_split
    tube_pos = spatial // TUBES
    length = FRAMES * tube_pos
    head_dim = width // HEADS
    scale = 1.0 / math.sqrt(head_dim)

    def leaving(tensor):
        return tensor.reshape(frames_dev, clip_sets, frame_count, tubes_dev * tube_pos, width)

    def arranged(tensor):
        tensor = tensor.reshape(clip_split, FRAMES, clip_sets, tubes_dev, tube_pos, width)
        tensor = jnp.transpose(tensor, (0, 2, 3, 1, 4, 5))
        return tensor.reshape(-1, width)

    def restored(tensor):
        tensor = tensor.reshape(clip_split, clip_sets, tubes_dev, FRAMES, tube_pos, width)
        tensor = jnp.transpose(tensor, (0, 3, 1, 2, 4, 5))
        return tensor.reshape(frame_count * frames_dev, clip_sets, 1, tubes_dev * tube_pos, width)

    masked = jnp.where(token_mask[:, :, None] == 1, out_grad, jnp.zeros((), jnp.bfloat16))
    arrived = (
        lax.all_to_all(leaving(stream), FRAME, split_axis=2, concat_axis=0, tiled=True),
        lax.all_to_all(leaving(masked), FRAME, split_axis=2, concat_axis=0, tiled=True),
    )
    inputs = arranged(arrived[0]).astype(jnp.float32)
    grad_y = arranged(arrived[1])
    seq_count = inputs.shape[0] // length

    def split_heads(tensor):
        return tensor.reshape(seq_count, length, HEADS, head_dim)

    def attention_scores(queries, key_part):
        return (
            jnp.einsum("slhe,smhe->shlm", queries, key_part, preferred_element_type=jnp.float32)
            * scale
        )

    first_normed_input, unit_one, inverse_one = layer_norm(inputs, ln1_gain, ln1_bias)
    first_normed_input = first_normed_input.astype(jnp.bfloat16)
    third_bias_term = jnp.concatenate(
        [b_qv[:width], jnp.zeros((width,), jnp.float32), b_qv[width:]]
    )
    query_key_value = (
        jnp.dot(first_normed_input, w_qkv, preferred_element_type=jnp.float32) + third_bias_term
    ).astype(jnp.bfloat16)
    queries = split_heads(query_key_value[:, :width])
    key_part = split_heads(query_key_value[:, width : 2 * width])
    values = split_heads(query_key_value[:, 2 * width :])
    scores = attention_scores(queries, key_part)
    largest = jnp.max(scores, axis=-1, keepdims=True)
    logsum = largest + jnp.log(jnp.sum(jnp.exp(scores - largest), axis=-1, keepdims=True))
    attend_low = jnp.exp(scores - logsum).astype(jnp.bfloat16)
    mixed_heads = jnp.einsum(
        "shlm,smhe->slhe", attend_low, values, preferred_element_type=jnp.float32
    )
    mixed_heads = mixed_heads.reshape(-1, width).astype(jnp.bfloat16)
    attention_branch = jnp.dot(mixed_heads, w_out, preferred_element_type=jnp.float32) + b_out
    middle = inputs + attention_branch
    second_normed_input, unit_two, inverse_two = layer_norm(middle, ln2_gain, ln2_bias)
    second_normed_input = second_normed_input.astype(jnp.bfloat16)
    hidden_state = jnp.dot(second_normed_input, w_up, preferred_element_type=jnp.float32) + b_up
    activated_hidden = jax.nn.gelu(hidden_state, approximate=False).astype(jnp.bfloat16)
    feedforward_branch = (
        jnp.dot(activated_hidden, w_down, preferred_element_type=jnp.float32) + b_down
    )
    result = middle + feedforward_branch
    squares = jnp.stack(
        [
            jnp.sum(inputs * inputs),
            jnp.sum(middle * middle),
            jnp.sum(result * result),
            jnp.sum(attention_branch * attention_branch),
            jnp.sum(feedforward_branch * feedforward_branch),
        ]
    )
    totals = lax.psum(squares, (CLIP, FRAME))
    statistics = jnp.sqrt(totals / (row_count * spatial * width * device_count))
    grad_w_down = jnp.einsum(
        "tf,td->fd", activated_hidden, grad_y, preferred_element_type=jnp.float32
    )
    grad_b_down = jnp.sum(grad_y.astype(jnp.float32), axis=0)
    d_active = jnp.einsum("td,fd->tf", grad_y, w_down, preferred_element_type=jnp.float32)
    d_hidden = (d_active * gelu_slope(hidden_state)).astype(jnp.bfloat16)
    grad_w_up = jnp.einsum(
        "td,tf->df", second_normed_input, d_hidden, preferred_element_type=jnp.float32
    )
    grad_b_up = jnp.sum(d_hidden.astype(jnp.float32), axis=0)
    d_two = jnp.einsum("tf,df->td", d_hidden, w_up, preferred_element_type=jnp.float32)
    grad_ln2_gain = jnp.sum(d_two * unit_two, axis=0)
    grad_ln2_bias = jnp.sum(d_two, axis=0)
    d_middle = grad_y.astype(jnp.float32) + norm_backward(d_two, unit_two, inverse_two, ln2_gain)
    d_branch = d_middle.astype(jnp.bfloat16)
    grad_w_out = jnp.einsum("td,te->de", mixed_heads, d_branch, preferred_element_type=jnp.float32)
    grad_b_out = jnp.sum(d_branch.astype(jnp.float32), axis=0)
    d_mixed = jnp.einsum("te,de->td", d_branch, w_out, preferred_element_type=jnp.float32)
    d_mixed = split_heads(d_mixed.astype(jnp.bfloat16))
    again = attention_scores(queries, key_part)
    attend = jnp.exp(again - logsum)
    attend_again = attend.astype(jnp.bfloat16)
    d_attend = jnp.einsum("slhe,smhe->shlm", d_mixed, values, preferred_element_type=jnp.float32)
    d_values = jnp.einsum(
        "shlm,slhe->smhe", attend_again, d_mixed, preferred_element_type=jnp.float32
    )
    centre_term = jnp.sum(attend * d_attend, axis=-1, keepdims=True)
    d_scores = (attend * (d_attend - centre_term)).astype(jnp.bfloat16)
    d_queries = (
        jnp.einsum("shlm,smhe->slhe", d_scores, key_part, preferred_element_type=jnp.float32)
        * scale
    )
    d_keys = (
        jnp.einsum("shlm,slhe->smhe", d_scores, queries, preferred_element_type=jnp.float32) * scale
    )
    d_qkv = jnp.concatenate(
        [d_queries.reshape(-1, width), d_keys.reshape(-1, width), d_values.reshape(-1, width)],
        axis=1,
    ).astype(jnp.bfloat16)
    grad_w_qkv = jnp.einsum(
        "td,te->de", first_normed_input, d_qkv, preferred_element_type=jnp.float32
    )
    bias_sums = jnp.sum(d_qkv.astype(jnp.float32), axis=0)
    grad_b_qv = jnp.concatenate([bias_sums[:width], bias_sums[2 * width :]])
    d_one = jnp.einsum("te,de->td", d_qkv, w_qkv, preferred_element_type=jnp.float32)
    grad_ln1_gain = jnp.sum(d_one * unit_one, axis=0)
    grad_ln1_bias = jnp.sum(d_one, axis=0)
    d_inputs = d_middle + norm_backward(d_one, unit_one, inverse_one, ln1_gain)
    departed = (
        lax.all_to_all(
            restored(result.astype(jnp.bfloat16)), FRAME, split_axis=0, concat_axis=2, tiled=True
        ),
        lax.all_to_all(
            restored(d_inputs.astype(jnp.bfloat16)),
            FRAME,
            split_axis=0,
            concat_axis=2,
            tiled=True,
        ),
    )
    output = departed[0].reshape(row_count, spatial, width)
    input_grad = departed[1].reshape(row_count, spatial, width)
    gradients = [
        grad_ln1_gain,
        grad_ln1_bias,
        grad_w_qkv,
        grad_b_qv,
        grad_w_out,
        grad_b_out,
        grad_ln2_gain,
        grad_ln2_bias,
        grad_w_up,
        grad_b_up,
        grad_w_down,
        grad_b_down,
    ]
    grouped = jnp.concatenate([item.reshape(frame_count, -1) for item in gradients], axis=1)
    extent_all = grouped.shape[1]
    padding = -extent_all % clip_count
    grouped = jnp.concatenate([grouped, jnp.zeros((frame_count, padding), jnp.float32)], axis=1)
    own_rows = lax.psum_scatter(
        grouped.astype(jnp.bfloat16), FRAME, scatter_dimension=0, tiled=True
    ).astype(jnp.float32)
    summed = lax.psum(own_rows, CLIP).reshape(-1)
    finished = []
    offset = 0
    for item in gradients:
        extent = item.size // frame_count
        local_shape = (item.shape[0] // frame_count,) + item.shape[1:]
        finished.append(summed[offset : offset + extent].reshape(local_shape))
        offset = offset + extent
    return (
        output,
        input_grad,
        finished[0],
        finished[1],
        finished[2],
        finished[3],
        finished[4],
        finished[5],
        finished[6],
        finished[7],
        finished[8],
        finished[9],
        finished[10],
        finished[11],
        statistics,
    )


def solution(mesh):
    clips, frames = mesh.shape[CLIP], mesh.shape[FRAME]

    def on_device(stream, *rest):
        ff = rest[-4].shape[1]
        plan = Plan(clips, frames, stream.shape, ff)
        if plan.fits:
            return with_kernel(plan, stream, *rest)
        return with_collectives(stream, *rest)

    tokens = P((CLIP, FRAME), None, None)
    in_specs = (tokens, tokens, P((CLIP, FRAME), None)) + (P(),) * 12
    rows, vector = P(FRAME, None), P(FRAME)
    out_specs = (
        tokens,
        tokens,
        vector,
        vector,
        rows,
        vector,
        rows,
        vector,
        vector,
        vector,
        rows,
        vector,
        rows,
        vector,
        P(),
    )
    return jax.shard_map(
        on_device, mesh=mesh, in_specs=in_specs, out_specs=out_specs, check_vma=False
    )
```
